32 devices in a mesh: section: 2 (over core), dp: 2 (over y), tensor: 8 (over z, x).
Axes of the slice: x: 2, y: 2, z: 4, core: 2. Of those that a mesh axis runs over, the one named last changes fastest.
Arguments:
- boundary: bfloat16 [2, 4, 1024, 4, 1024], P('section', None, 'tensor', 'dp'), may hold values from -6 to 6
- segment_ids: int32 [4, 4, 1024], P(None, 'dp'), may hold values from -1 to 31, as said below
- project_weight: bfloat16 [2, 1024, 3, 1024], P('section', None, None, 'tensor'), may hold values from -0.1875 to 0.1875
- project_bias: bfloat16 [2, 3, 1024], P('section', None, 'tensor'), may hold values from -3 to 3
- output_weight: bfloat16 [2, 1024, 1024], P('section', 'tensor'), may hold values from -2 to 2
- output_biases: bfloat16 [2, 2, 1024], P('section'), may hold values from -3 to 3
- norm_gains: bfloat16 [2, 2, 1024], P('section'), may hold values from 0.5 to 1.5
- norm_shifts: bfloat16 [2, 2, 1024], P('section'), may hold values from -2 to 2
- up_weight: bfloat16 [2, 1024, 4096], P('section', None, 'tensor'), may hold values from -0.1875 to 0.1875
- up_bias: bfloat16 [2, 4096], P('section', 'tensor'), may hold values from -3 to 3
- down_weight: bfloat16 [2, 4096, 1024], P('section', 'tensor'), may hold values from -0.09375 to 0.09375
- prefix_keys: bfloat16 [2, 20, 1024], P('section', None, 'tensor'), may hold values from -6 to 6
- prefix_values: bfloat16 [2, 20, 1024], P('section', None, 'tensor'), may hold values from -6 to 6
Outputs:
- result: bfloat16 [2, 4, 1024, 4, 1024], P('section', None, 'tensor', 'dp')
- key_grad: float32 [2, 20, 1024], P('section', None, 'tensor')
- value_grad: float32 [2, 20, 1024], P('section', None, 'tensor')
The draws below stay inside these ranges and needn't reach their ends.
Inputs may be any that keep to these rules, and one draw needn't show every extreme that they name: `segment_ids`: ids count a row's segments from 0 in order of position; each segment spans 1 to 96 slots, except in rows that are a single segment over all 1024 slots; -1 marks fewer than 128 padding slots at a row's end; in each micro-batch, one row of every aligned group of 2 rows is a single segment over all 1024 slots.
All inputs are finite; a program needn't handle non-finite values.
Results may differ from the reference program's by a relative error of at most 0.023.
Values may be sent and summed in bfloat16 or wider, within the bound.
No kernel may reach another device: no remote copies, remote signals or barrier semaphores. Data moves between devices by JAX's collectives and lax.ppermute only.
A program may use at most 192 MiB of HBM per device.

```python
import math
import jax
import jax.numpy as jnp
from jax import lax

D = 1024
HEADS = 16
HEAD = 64
FF = 4096
NPRE = 20
LEN = 1024
MICRO = 4
PAIR = 64
ROWS_DEV = 2
ROWS = 4
LAYERS = 2


def draw_segment_ids(key, part):
    key = jax.random.fold_in(key, 7)
    key_length, key_padding, key_choose = jax.random.split(key, 3)
    segment_count = LEN // (PAIR // 2) + 1
    lengths = jax.random.randint(key_length, (MICRO, ROWS, segment_count), PAIR // 2, 3 * PAIR // 2 + 1)
    ends = jnp.cumsum(lengths, axis=-1)
    position = jnp.arange(LEN, dtype=jnp.int32)
    labels = jnp.sum((ends[:, :, None, :] <= position[None, None, :, None]).astype(jnp.int32), axis=-1)
    padding = jax.random.randint(key_padding, (MICRO, ROWS, 1), 0, LEN // 8)
    labels = jnp.where(position[None, None, :] >= LEN - padding, -1, labels)
    chosen = jax.random.randint(key_choose, (MICRO, ROWS // ROWS_DEV), 0, ROWS_DEV)
    row_number = jnp.arange(ROWS, dtype=jnp.int32)
    regular_index = (chosen[:, 0] + 1) % ROWS_DEV
    regular_row = row_number[None, :] == regular_index[:, None]
    labels = jnp.where(regular_row[:, :, None], (position // (PAIR // 2))[None, None, :], labels)
    long_row = jnp.repeat(chosen, ROWS_DEV, axis=1) == (row_number % ROWS_DEV)[None, :]
    labels = jnp.where(long_row[:, :, None], 0, labels)
    return labels.astype(jnp.int32)


def shard_levels(key, dims, cuts, least, high):
    level, own = 1.0, jax.random.fold_in(key, 6)
    for dim, shards_of in cuts:
        heights = jnp.exp(jax.random.uniform(jax.random.fold_in(own, dim), (shards_of,), jnp.float32, least / len(cuts), high / len(cuts)))
        level = level * jnp.repeat(heights, dims[dim] // shards_of).reshape([-1 if axis == dim else 1 for axis in range(len(dims))])
    return level


def centred(stream_key, shape, scale, bound, shards=(), kind=jnp.bfloat16):
    drawn = jax.random.normal(stream_key, shape, jnp.float32) * scale
    if len(shards) > 0:
        drawn = shard_levels(stream_key, shape, shards, -0.22, 0.18) * drawn
    return jnp.clip(drawn, min=-bound, max=bound).astype(kind)


def setup_inputs(seed: int = 0) -> dict:
    key_of = jax.random.split(jax.random.key(seed), 14)
    boundary = centred(key_of[0], (2, MICRO, LEN, ROWS, D), 1.0, 6.0, ((0, 2), (2, 8), (3, 2)))
    segment_ids = draw_segment_ids(jax.random.fold_in(key_of[13], 71), 0)
    project_weight = centred(key_of[2], (LAYERS, D, 3, D), D ** -0.5, 0.1875, ((0, 2), (3, 8)))
    project_bias = centred(key_of[3], (LAYERS, 3, D), 0.5, 3.0, ((0, 2), (2, 8)))
    output_weight = centred(key_of[4], (LAYERS, D, D), (max(D // 128, 8)) ** -0.5, 2.0, ((0, 2), (1, 8)))
    output_biases = centred(key_of[5], (LAYERS, 2, D), 0.5, 3.0, ((0, 2),))
    norm_gains = jnp.clip(1.0 + 0.1 * jax.random.normal(key_of[6], (LAYERS, 2, D), jnp.float32), 0.5, 1.5).astype(jnp.bfloat16)
    norm_shifts = centred(key_of[7], (LAYERS, 2, D), 0.3, 2.0, ((0, 2),))
    up_weight = centred(key_of[8], (LAYERS, D, FF), D ** -0.5, 0.1875, ((0, 2), (2, 8)))
    up_bias = centred(key_of[9], (LAYERS, FF), 0.5, 3.0, ((0, 2), (1, 8)))
    down_weight = centred(key_of[10], (LAYERS, FF, D), FF ** -0.5, 0.09375, ((0, 2), (1, 8)))
    prefix_keys = centred(key_of[11], (LAYERS, NPRE, D), 1.0, 6.0, ((0, 2), (2, 8)))
    prefix_values = centred(key_of[12], (LAYERS, NPRE, D), 1.0, 6.0, ((0, 2), (2, 8)))
    return dict(boundary=boundary, segment_ids=segment_ids, project_weight=project_weight, project_bias=project_bias, output_weight=output_weight, output_biases=output_biases, norm_gains=norm_gains, norm_shifts=norm_shifts, up_weight=up_weight, up_bias=up_bias, down_weight=down_weight, prefix_keys=prefix_keys, prefix_values=prefix_values)


@jax.custom_vjp
def low(v):
    return lax.optimization_barrier(v.astype(jnp.bfloat16)).astype(jnp.float32)

@jax.custom_vjp
def low_back(v):
    return v

def low_keep(v):
    return (low(v), None)

def low_pass(kept, grad):
    return (grad,)

def back_keep(v):
    return (v, None)

def back_low(kept, grad):
    return (low(grad),)
low.defvjp(low_keep, low_pass)
low_back.defvjp(back_keep, back_low)
highest = lax.Precision.HIGHEST
norm_epsilon = 1e-05
masked_fill = -1000000000.0

def normalize(hidden, gain, shift):
    average = lax.optimization_barrier(jnp.mean(hidden, axis=-1, keepdims=True))
    centered = hidden - average
    variance = lax.optimization_barrier(jnp.mean(centered * centered, axis=-1, keepdims=True))
    return centered * lax.rsqrt(variance + norm_epsilon) * gain + shift

def row_attention(queries, key_rows, value_rows, segment_row):
    scores = jnp.einsum('qhe,khe->hqk', queries, key_rows, precision=highest) * (1.0 / math.sqrt(HEAD))
    scores = low_back(scores)
    same = (segment_row[:, None] == segment_row[None, :]) & (segment_row[None, :] >= 0)
    allowed = jnp.concatenate([jnp.ones((LEN, NPRE), dtype=jnp.bool_), same], axis=1)
    scores = jnp.where(allowed[None], scores, masked_fill)
    largest = lax.optimization_barrier(jnp.max(scores, axis=-1, keepdims=True))
    raised = jnp.exp(scores - largest)
    attention = raised / lax.optimization_barrier(jnp.sum(raised, axis=-1, keepdims=True))
    return jnp.einsum('hqk,khe->qhe', low(attention), value_rows, precision=highest)

def layer(tokens, segments, weights):
    project_weight, project_bias, output_weight, output_biases, norm_gains, norm_shifts, up_weight, up_bias, down_weight, prefix_keys, prefix_values = weights
    flat = tokens.reshape(LEN * ROWS, D)
    projected = jnp.dot(flat, project_weight.reshape(D, 3 * D), precision=highest) + project_bias.reshape(3 * D)
    projected = low(low_back(projected)).reshape(LEN, ROWS, 3, HEADS, HEAD)
    parts = jnp.transpose(projected, (1, 2, 0, 3, 4))
    prefix_key_rows = prefix_keys.reshape(NPRE, HEADS, HEAD)
    prefix_value_rows = prefix_values.reshape(NPRE, HEADS, HEAD)

    def one_row(items):
        part, segment_row = items
        key_rows = jnp.concatenate([prefix_key_rows, part[1]], axis=0)
        value_rows = jnp.concatenate([prefix_value_rows, part[2]], axis=0)
        return row_attention(part[0], key_rows, value_rows, segment_row)
    mixed = lax.map(jax.checkpoint(one_row), (parts, segments))
    mixed = low(low_back(jnp.transpose(mixed, (1, 0, 2, 3)).reshape(LEN * ROWS, D)))
    attended = low_back(jnp.dot(mixed, output_weight, precision=highest))
    normed = normalize(flat + attended + output_biases[0], norm_gains[0], norm_shifts[0])
    pre_act = low_back(jnp.dot(low(normed), up_weight, precision=highest) + up_bias)
    activated = low(jax.nn.gelu(pre_act, approximate=False))
    hidden_out = low_back(jnp.dot(activated, down_weight, precision=highest))
    layer_out = normalize(normed + hidden_out + output_biases[1], norm_gains[1], norm_shifts[1])
    return layer_out.reshape(LEN, ROWS, D)

def reference(boundary, segment_ids, project_weight, project_bias, output_weight, output_biases, norm_gains, norm_shifts, up_weight, up_bias, down_weight, prefix_keys, prefix_values):
    frozen = tuple((entry.astype(jnp.float32) for entry in (project_weight, project_bias, output_weight, output_biases, norm_gains, norm_shifts, up_weight, up_bias, down_weight)))
    key_start = prefix_keys.astype(jnp.float32)
    value_start = prefix_values.astype(jnp.float32)

    def forward(tokens, segments, key_table, value_table):
        first_weights = tuple((entry[0] for entry in frozen)) + (key_table[0], value_table[0])
        second_weights = tuple((entry[1] for entry in frozen)) + (key_table[1], value_table[1])
        middle = low(low_back(layer(tokens, segments, first_weights)))
        return layer(middle, segments, second_weights)

    def micro_step(totals, items):
        tokens, cotangent, segments = items

        def run(inputs, key_table, value_table):
            return forward(inputs, segments, key_table, value_table)
        layer_out, pullback = jax.vjp(run, tokens, key_start, value_start)
        input_grad, key_part, value_part = pullback(cotangent)
        return ((totals[0] + key_part, totals[1] + value_part), (layer_out.astype(jnp.bfloat16), input_grad.astype(jnp.bfloat16)))
    zeros = jnp.zeros(prefix_keys.shape, jnp.float32)
    (key_total, value_total), (outputs, input_grads) = lax.scan(micro_step, (zeros, zeros), (boundary[0].astype(jnp.float32), boundary[1].astype(jnp.float32), segment_ids))
    return (jnp.stack([input_grads, outputs]), key_total, value_total)
```

```python
import functools
import math

import jax
import jax.numpy as jnp
from jax import lax
from jax.experimental import pallas as pl
from jax.experimental.pallas import tpu as pltpu
from jax.sharding import PartitionSpec as P

HEAD = 64
PAIR = 2 * HEAD
EPSILON = 1e-05
MASKED = -1000000000.0
VMEM = 56 * 1024 * 1024
SECTIONS = 2

bf16 = jnp.bfloat16
f32 = jnp.float32


def dot_nn(left, right):
    return lax.dot_general(left, right, (((1,), (0,)), ((), ())), preferred_element_type=f32)


def dot_nt(left, right):
    return lax.dot_general(left, right, (((1,), (1,)), ((), ())), preferred_element_type=f32)


def dot_tn(left, right):
    return lax.dot_general(left, right, (((0,), (0,)), ((), ())), preferred_element_type=f32)


def unit(hidden):
    average = jnp.mean(hidden, axis=-1, keepdims=True)
    centered = hidden - average
    variance = jnp.mean(centered * centered, axis=-1, keepdims=True)
    inverse = lax.rsqrt(variance + EPSILON)
    return centered * inverse, inverse


def unit_back(grad, normed, inverse, gain):
    scaled = grad * gain
    return inverse * (
        scaled
        - jnp.mean(scaled, axis=-1, keepdims=True)
        - normed * jnp.mean(scaled * normed, axis=-1, keepdims=True)
    )


def call(kernel, grid, in_specs, out_specs, out_shape, scratch=(), flops=0, moved=0, exps=0):
    return pl.pallas_call(
        kernel,
        grid=grid,
        in_specs=in_specs,
        out_specs=out_specs,
        out_shape=out_shape,
        scratch_shapes=list(scratch),
        compiler_params=pltpu.CompilerParams(
            vmem_limit_bytes=VMEM, dimension_semantics=("arbitrary",) * len(grid)
        ),
        cost_estimate=pl.CostEstimate(flops=flops, bytes_accessed=moved, transcendentals=exps),
    )


def whole(shape):
    return pl.BlockSpec(shape, lambda i: (0,) * len(shape))


def struct(shape, dtype):
    return jax.ShapeDtypeStruct(shape, dtype)


def table_pair(table, width):
    array, first, rows = table
    return pl.BlockSpec((2, 1, rows, width), lambda i: (0, i, first // rows, 0))


def table_all(table, width):
    array, first, rows = table
    return pl.BlockSpec(
        (2, array.shape[1], rows, width), lambda i: (0, 0, first // rows, 0)
    )


def table_piece(table, width):
    array, first, rows = table
    pairs = array.shape[1]
    return pl.BlockSpec((1, 1, rows, width), lambda i: (i // pairs, i % pairs, first // rows, 0))


def pair_rows(ref):
    parts = []
    for part in range(3):
        for half in range(2):
            parts.append(ref[half, 0, part * HEAD : (part + 1) * HEAD, :])
    return jnp.concatenate(parts, axis=0)


def project_kernel(x_ref, w_ref, b_ref, q_ref, kv_ref):
    out = (dot_nt(x_ref[...], pair_rows(w_ref)) + b_ref[0]).astype(bf16)
    q_ref[0] = out[:, :PAIR] * bf16(1.0 / math.sqrt(HEAD))
    kv_ref[0, 0] = out[:, PAIR : 2 * PAIR]
    kv_ref[1, 0] = out[:, 2 * PAIR :]


def project(x, table, bias):
    count, width = x.shape
    pairs = table[0].shape[1]
    return call(
        project_kernel,
        (pairs,),
        [
            whole((count, width)),
            table_pair(table, width),
            pl.BlockSpec((1, 1, 3 * PAIR), lambda i: (i, 0, 0)),
        ],
        [
            pl.BlockSpec((1, count, PAIR), lambda i: (i, 0, 0)),
            pl.BlockSpec((2, 1, count, PAIR), lambda i: (0, i, 0, 0)),
        ],
        [struct((pairs, count, PAIR), bf16), struct((2, pairs, count, PAIR), bf16)],
        flops=2 * count * width * 3 * PAIR * pairs,
        moved=2 * (count * width * 4 + 3 * width * PAIR * pairs),
    )(x, table[0], bias)


def attend_kernel(
    prefix_count, q_ref, own_ref, other_ref, pk_ref, pv_ref, sq_ref, sk_ref,
    mixed_ref, raised_ref, inverse_ref, bias_ref,
):
    pad = pk_ref.shape[1]
    others = other_ref.shape[0]

    @pl.when(pl.program_id(0) == 0)
    def _():
        row = lax.broadcasted_iota(jnp.int32, (pad, bias_ref.shape[1]), 0)
        bias_ref[:pad] = jnp.where(row < prefix_count, 0.0, MASKED)
        keys = sk_ref[...]
        same = (keys == sq_ref[...]) & (keys >= 0)
        bias_ref[pad:] = jnp.where(same, 0.0, MASKED)

    keys = jnp.concatenate(
        [pk_ref[0], own_ref[0, 0]] + [other_ref[i, 0, 0] for i in range(others)], axis=0
    )
    values = jnp.concatenate(
        [pv_ref[0], own_ref[1, 0]] + [other_ref[i, 1, 0] for i in range(others)], axis=0
    )
    queries = q_ref[0]
    lane = lax.broadcasted_iota(jnp.int32, queries.shape, 1)
    parts = []
    inverses = []
    for head in range(2):
        chosen = (lane // HEAD) == head
        scores = dot_nt(keys, jnp.where(chosen, queries, bf16(0))) + bias_ref[...]
        raised = jnp.exp(scores - jnp.max(scores, axis=0, keepdims=True))
        inverse = 1.0 / jnp.sum(raised, axis=0, keepdims=True)
        low = raised.astype(bf16)
        raised_ref[0, head] = low
        out = dot_tn(values, low)[head * HEAD : (head + 1) * HEAD]
        parts.append(out * inverse)
        inverses.append(jnp.broadcast_to(inverse, out.shape))
    mixed_ref[0] = jnp.concatenate(parts, axis=0).T.astype(bf16)
    inverse_ref[0] = jnp.concatenate(inverses, axis=0).T


def attend(q, own, other, pk, pv, prefix_count, seg_q, seg_k):
    pairs, count, _ = q.shape
    others = other.shape[0]
    pad = pk.shape[1]
    total = pad + count * (others + 1)
    by_pair = pl.BlockSpec((1, count, PAIR), lambda i: (i, 0, 0))
    by_prefix = pl.BlockSpec((1, pad, PAIR), lambda i: (i, 0, 0))
    return call(
        functools.partial(attend_kernel, prefix_count),
        (pairs,),
        [
            by_pair,
            pl.BlockSpec((2, 1, count, PAIR), lambda i: (0, i, 0, 0)),
            pl.BlockSpec((others, 2, 1, count, PAIR), lambda i: (0, 0, i, 0, 0)),
            by_prefix,
            by_prefix,
            whole((1, count)),
            whole((total - pad, 1)),
        ],
        [
            by_pair,
            pl.BlockSpec((1, 2, total, count), lambda i: (i, 0, 0, 0)),
            by_pair,
        ],
        [
            struct((pairs, count, PAIR), bf16),
            struct((pairs, 2, total, count), bf16),
            struct((pairs, count, PAIR), f32),
        ],
        scratch=[pltpu.VMEM((total, count), f32)],
        flops=8 * total * count * PAIR * pairs,
        moved=4 * pairs * total * count,
        exps=2 * pairs * total * count,
    )(q, own, other, pk, pv, seg_q, seg_k)


def feed_kernel(
    x_ref, mixed_ref, out_w_ref, vec_ref, up_ref, down_ref, ub_ref,
    out_ref, z1_ref, r1_ref, z2_ref, r2_ref, slope_ref, normed_ref, low_ref, acc_ref,
):
    step = pl.program_id(0)
    pairs = mixed_ref.shape[0]

    @pl.when(step == 0)
    def _():
        mixed = jnp.concatenate([mixed_ref[i] for i in range(pairs)], axis=1)
        rows = []
        for i in range(pairs):
            rows += [out_w_ref[0, i], out_w_ref[1, i]]
        attended = dot_nn(mixed, jnp.concatenate(rows, axis=0))
        z, r = unit(x_ref[...].astype(f32) + attended + vec_ref[0:1])
        z1_ref[...] = z
        r1_ref[...] = r
        normed = z * vec_ref[2:3] + vec_ref[4:5]
        normed_ref[...] = normed
        low_ref[...] = normed.astype(bf16)
        acc_ref[...] = jnp.zeros(acc_ref.shape, f32)

    pre = dot_nt(low_ref[...], up_ref[0, 0]) + ub_ref[0]
    spread = 0.5 + 0.5 * lax.erf(pre * math.sqrt(0.5))
    slope = spread + pre * (jnp.exp(-0.5 * pre * pre) * (1.0 / math.sqrt(2.0 * math.pi)))
    slope_ref[0] = slope.astype(bf16)
    acc_ref[...] += dot_nn((pre * spread).astype(bf16), down_ref[0, 0])

    @pl.when(step == pl.num_programs(0) - 1)
    def _():
        z, r = unit(normed_ref[...] + acc_ref[...] + vec_ref[1:2])
        z2_ref[...] = z
        r2_ref[...] = r
        out_ref[...] = (z * vec_ref[3:4] + vec_ref[5:6]).astype(bf16)


def feed(x, mixed, out_table, vectors, up_table, down_table, up_bias):
    count, width = x.shape
    pairs = mixed.shape[0]
    pieces = up_bias.shape[0]
    hidden = up_bias.shape[2]
    square = whole((count, width))
    column = whole((count, 1))
    return call(
        feed_kernel,
        (pieces,),
        [
            square,
            whole(mixed.shape),
            table_all(out_table, width),
            whole(vectors.shape),
            table_piece(up_table, width),
            table_piece(down_table, width),
            pl.BlockSpec((1, 1, hidden), lambda i: (i, 0, 0)),
        ],
        [square, square, column, square, column,
         pl.BlockSpec((1, count, hidden), lambda i: (i, 0, 0))],
        [
            struct((count, width), bf16),
            struct((count, width), f32),
            struct((count, 1), f32),
            struct((count, width), f32),
            struct((count, 1), f32),
            struct((pieces, count, hidden), bf16),
        ],
        scratch=[
            pltpu.VMEM((count, width), f32),
            pltpu.VMEM((count, width), bf16),
            pltpu.VMEM((count, width), f32),
        ],
        flops=2 * count * width * (width + 2 * hidden * pieces),
        moved=2 * (4 * hidden * pieces * width + 10 * count * width),
        exps=2 * count * hidden * pieces,
    )(x, mixed, out_table[0], vectors, up_table[0], down_table[0], up_bias)


def feed_back_kernel(
    grad_ref, z1_ref, r1_ref, z2_ref, r2_ref, slope_ref, out_w_ref, vec_ref, up_ref, down_ref,
    first_ref, mixed_ref, second_ref, low_ref, acc_ref,
):
    step = pl.program_id(0)
    pairs = mixed_ref.shape[0]

    @pl.when(step == 0)
    def _():
        second = unit_back(grad_ref[...].astype(f32), z2_ref[...], r2_ref[...], vec_ref[3:4])
        acc_ref[...] = second
        low_ref[...] = second.astype(bf16)

    d_act = dot_nt(low_ref[...], down_ref[0, 0])
    d_pre = (d_act * slope_ref[0].astype(f32)).astype(bf16)
    acc_ref[...] += dot_nn(d_pre, up_ref[0, 0])

    @pl.when(step == pl.num_programs(0) - 1)
    def _():
        first = unit_back(acc_ref[...], z1_ref[...], r1_ref[...], vec_ref[2:3])
        first_ref[...] = first
        low = first.astype(bf16)
        for i in range(pairs):
            rows = jnp.concatenate([out_w_ref[0, i], out_w_ref[1, i]], axis=0)
            mixed_ref[i] = dot_nt(low, rows).astype(bf16)


def feed_back(grad, kept, slope, out_table, vectors, up_table, down_table):
    count, width = grad.shape
    pieces, _, hidden = slope.shape
    pairs = out_table[0].shape[1]
    square = whole((count, width))
    column = whole((count, 1))
    return call(
        feed_back_kernel,
        (pieces,),
        [
            square, square, column, square, column,
            pl.BlockSpec((1, count, hidden), lambda i: (i, 0, 0)),
            table_all(out_table, width),
            whole(vectors.shape),
            table_piece(up_table, width),
            table_piece(down_table, width),
        ],
        [square, whole((pairs, count, PAIR))],
        [struct((count, width), f32), struct((pairs, count, PAIR), bf16)],
        scratch=[
            pltpu.VMEM((count, width), f32),
            pltpu.VMEM((count, width), bf16),
            pltpu.VMEM((count, width), f32),
        ],
        flops=2 * count * width * (width + 2 * hidden * pieces),
        moved=2 * (4 * hidden * pieces * width + 10 * count * width),
    )(grad, *kept, slope, out_table[0], vectors, up_table[0], down_table[0])


def attend_back_kernel(
    grad_ref, mixed_ref, inverse_ref, raised_ref, q_ref, own_ref, other_ref, pk_ref, pv_ref,
    dq_ref, down_ref, dother_ref, dpk_ref, dpv_ref,
):
    pad = pk_ref.shape[1]
    others = other_ref.shape[0]
    count = q_ref.shape[1]
    keys = jnp.concatenate(
        [pk_ref[0], own_ref[0, 0]] + [other_ref[i, 0, 0] for i in range(others)], axis=0
    )
    values = jnp.concatenate(
        [pv_ref[0], own_ref[1, 0]] + [other_ref[i, 1, 0] for i in range(others)], axis=0
    )
    queries = q_ref[0]
    lane = lax.broadcasted_iota(jnp.int32, queries.shape, 1)
    scaled = grad_ref[0].astype(f32) * inverse_ref[0]
    products = (scaled * mixed_ref[0].astype(f32)).T
    scaled = scaled.astype(bf16)
    d_keys = jnp.zeros(keys.shape, f32)
    d_values = jnp.zeros(keys.shape, f32)
    parts = []
    for head in range(2):
        chosen = (lane // HEAD) == head
        span = slice(head * HEAD, (head + 1) * HEAD)
        delta = jnp.sum(products[span], axis=0, keepdims=True)
        here = jnp.where(chosen, scaled, bf16(0))
        raised = raised_ref[0, head]
        d_score = (raised.astype(f32) * (dot_nt(values, here) - delta)).astype(bf16)
        d_values += dot_nn(raised, here)
        d_keys += dot_nn(d_score, jnp.where(chosen, queries, bf16(0)))
        parts.append(dot_tn(keys, d_score)[span])
    d_query = jnp.concatenate(parts, axis=0).T * (1.0 / math.sqrt(HEAD))
    dq_ref[0] = d_query.astype(bf16)
    dpk_ref[0] = d_keys[:pad]
    dpv_ref[0] = d_values[:pad]
    down_ref[0, 0] = d_keys[pad : pad + count].astype(bf16)
    down_ref[1, 0] = d_values[pad : pad + count].astype(bf16)
    for i in range(others):
        span = slice(pad + (i + 1) * count, pad + (i + 2) * count)
        dother_ref[i, 0, 0] = d_keys[span].astype(bf16)
        dother_ref[i, 1, 0] = d_values[span].astype(bf16)


def attend_back(grad, mixed, inverse, raised, q, own, other, pk, pv):
    pairs, count, _ = q.shape
    others = other.shape[0]
    pad = pk.shape[1]
    total = pad + count * (others + 1)
    by_pair = pl.BlockSpec((1, count, PAIR), lambda i: (i, 0, 0))
    by_prefix = pl.BlockSpec((1, pad, PAIR), lambda i: (i, 0, 0))
    by_own = pl.BlockSpec((2, 1, count, PAIR), lambda i: (0, i, 0, 0))
    by_other = pl.BlockSpec((others, 2, 1, count, PAIR), lambda i: (0, 0, i, 0, 0))
    return call(
        attend_back_kernel,
        (pairs,),
        [
            by_pair, by_pair, by_pair,
            pl.BlockSpec((1, 2, total, count), lambda i: (i, 0, 0, 0)),
            by_pair, by_own, by_other, by_prefix, by_prefix,
        ],
        [by_pair, by_own, by_other, by_prefix, by_prefix],
        [
            struct(q.shape, bf16),
            struct(own.shape, bf16),
            struct(other.shape, bf16),
            struct(pk.shape, f32),
            struct(pk.shape, f32),
        ],
        flops=16 * total * count * PAIR * pairs,
        moved=4 * pairs * total * count,
    )(grad, mixed, inverse, raised, q, own, other, pk, pv)


def project_back_kernel(first_ref, dq_ref, own_ref, got_ref, w_ref, out_ref, acc_ref):
    step = pl.program_id(0)
    others = got_ref.shape[0]

    @pl.when(step == 0)
    def _():
        acc_ref[...] = first_ref[...]

    parts = [dq_ref[0]]
    for part in range(2):
        total = own_ref[part, 0].astype(f32)
        for i in range(others):
            total += got_ref[i, part, 0].astype(f32)
        parts.append(total.astype(bf16))
    acc_ref[...] += dot_nn(jnp.concatenate(parts, axis=1), pair_rows(w_ref))

    @pl.when(step == pl.num_programs(0) - 1)
    def _():
        out_ref[...] = acc_ref[...].astype(bf16)


def project_back(first, dq, own, got, table):
    count, width = first.shape
    pairs = dq.shape[0]
    others = got.shape[0]
    return call(
        project_back_kernel,
        (pairs,),
        [
            whole((count, width)),
            pl.BlockSpec((1, count, PAIR), lambda i: (i, 0, 0)),
            pl.BlockSpec((2, 1, count, PAIR), lambda i: (0, i, 0, 0)),
            pl.BlockSpec((others, 2, 1, count, PAIR), lambda i: (0, 0, i, 0, 0)),
            table_pair(table, width),
        ],
        whole((count, width)),
        struct((count, width), bf16),
        scratch=[pltpu.VMEM((count, width), f32)],
        flops=2 * count * width * 3 * PAIR * pairs,
        moved=2 * (count * width * 7 + 3 * width * PAIR * pairs),
    )(first, dq, own, got, table[0])


def per_device(
    boundary, segment_ids, project_weight, project_bias, output_weight, output_biases,
    norm_gains, norm_shifts, up_weight, up_bias, down_weight, prefix_keys, prefix_values,
):
    section = lax.axis_index("section")
    rank = lax.axis_index("tensor")
    ranks = lax.axis_size("tensor")
    is_first = section == 0
    micro, slots, rows, width = boundary.shape[1:]
    length = slots * ranks
    row_count = micro * rows
    chips = ranks // row_count
    blocks = SECTIONS * chips
    count = length // blocks
    place = rank % chips
    swap = [(0, 1), (1, 0)]
    heads_all = project_weight.shape[3] * ranks
    pairs = heads_all // PAIR
    shards = ranks // pairs
    prefix_count = prefix_keys.shape[1]
    pad = -(-prefix_count // 32) * 32
    low_width = project_weight.shape[3] // 2
    hidden = up_weight.shape[2] // 2

    project_rows = jnp.transpose(project_weight[0], (1, 2, 0)).reshape(3, 2, low_width, width)
    project_rows = jnp.transpose(project_rows, (1, 0, 2, 3)).reshape(2, 3 * low_width, width)
    out_rows = output_weight[0].reshape(2, low_width, width)
    up_rows = jnp.transpose(up_weight[0], (1, 0)).reshape(2, hidden, width)
    down_rows = down_weight[0].reshape(2, hidden, width)
    small = jnp.concatenate(
        [
            jnp.transpose(project_bias[0].reshape(3, 2, low_width), (1, 0, 2)).reshape(2, -1),
            up_bias[0].reshape(2, hidden),
            jnp.transpose(prefix_keys[0].reshape(-1, 2, low_width), (1, 0, 2)).reshape(2, -1),
            jnp.transpose(prefix_values[0].reshape(-1, 2, low_width), (1, 0, 2)).reshape(2, -1),
        ],
        axis=1,
    )
    small_size = small.shape[1]
    small_rows = -(-small_size // (16 * width)) * 16
    small = jnp.pad(small, ((0, 0), (0, small_rows * width - small_size)))
    packed = jnp.concatenate(
        [project_rows, out_rows, up_rows, down_rows, small.reshape(2, small_rows, width)], axis=1
    )
    keep = lax.dynamic_index_in_dim(packed, section, 0, keepdims=False)
    give = lax.dynamic_index_in_dim(packed, 1 - section, 0, keepdims=False)
    got = lax.ppermute(give, "section", swap)
    layer_rows = [jnp.where(is_first, keep, got), jnp.where(is_first, got, keep)]
    sizes = [3 * low_width, low_width, hidden, hidden, small_rows]
    ends = [sum(sizes[: i + 1]) for i in range(len(sizes))]
    p_end, o_end, u_end, d_end, s_end = ends
    early = jnp.concatenate(
        [
            layer_rows[0][:d_end],
            layer_rows[1][:o_end],
            layer_rows[0][d_end:],
            layer_rows[1][d_end:],
        ],
        axis=0,
    )
    late = layer_rows[1][o_end:d_end]
    gather = lambda array: lax.all_gather(array, ("section", "tensor"), axis=0).reshape(
        2, ranks, array.shape[0], width
    )
    early = gather(early)
    late = gather(late)

    def table(array, first, size, groups=1):
        if shards == 1:
            return (array, first, size)
        part = array[:, :, first : first + size].reshape(
            2, pairs, shards, groups, size // groups, width
        )
        part = jnp.transpose(part, (2, 1, 3, 0, 4, 5))
        return (part.reshape(2, pairs, 2 * size, width), 0, 2 * size)

    tables = []
    smalls = []
    for layer in range(2):
        base = layer * d_end
        source, shift = (early, 0) if layer == 0 else (late, -o_end)
        tables.append(
            (
                table(early, base, 3 * low_width, 3),
                table(early, base + p_end, low_width),
                table(source, shift + o_end, hidden),
                table(source, shift + u_end, hidden),
            )
        )
        start = d_end + o_end + layer * small_rows
        flat = early[:, :, start : start + small_rows].reshape(2, ranks, -1)
        cut = 0
        pieces = []
        for groups, size in ((3, low_width), (1, hidden), (prefix_count, low_width), (prefix_count, low_width)):
            part = flat[:, :, cut : cut + groups * size].reshape(2, pairs, shards, groups, size)
            cut += groups * size
            if shards == 1:
                part = part[:, :, 0]
            else:
                part = jnp.transpose(part, (2, 1, 3, 0, 4)).reshape(2, pairs, groups, 2 * size)
            pieces.append(part)
        p_bias = jnp.transpose(pieces[0], (1, 2, 0, 3)).reshape(pairs, 1, 3 * PAIR).astype(f32)
        u_bias = pieces[1].reshape(2 * pairs, 1, -1).astype(f32)
        prefix = [
            jnp.pad(
                jnp.transpose(part, (1, 2, 0, 3)).reshape(pairs, prefix_count, PAIR),
                ((0, 0), (0, pad - prefix_count), (0, 0)),
            )
            for part in pieces[2:]
        ]
        smalls.append((p_bias, u_bias, prefix[0], prefix[1]))

    own_vectors = jnp.concatenate(
        [output_biases[0], norm_gains[0], norm_shifts[0], norm_shifts[0]], axis=0
    )
    got_vectors = lax.ppermute(own_vectors, "section", swap)
    vectors = [
        jnp.where(is_first, own_vectors, got_vectors).astype(f32),
        jnp.where(is_first, got_vectors, own_vectors).astype(f32),
    ]

    by_row = jnp.transpose(boundary[0], (0, 2, 1, 3)).reshape(row_count, slots, width)
    if chips > 1:
        by_row = jnp.repeat(by_row, chips, axis=0)
    row = lax.all_to_all(by_row, "tensor", 0, 0, tiled=True).reshape(length, width)
    block = section * chips + place
    other_block = (1 - section) * chips + place
    mine = lax.dynamic_slice_in_dim(row, block * count, count, 0)
    theirs = lax.dynamic_slice_in_dim(row, other_block * count, count, 0)
    got = lax.ppermute(theirs, "section", swap)
    tokens = jnp.where(is_first, mine, got)
    cotangent = jnp.where(is_first, got, mine)

    def flips():
        routes = []
        for distance in range(1, blocks):
            route = []
            for s in range(SECTIONS):
                for t in range(ranks):
                    index = (s * chips + t % chips) ^ distance
                    route.append(
                        (s * ranks + t, (index // chips) * ranks + t // chips * chips + index % chips)
                    )
            routes.append(route)
        return routes

    routes = flips()

    def exchange(parts):
        return jnp.stack(
            [
                lax.ppermute(part, ("section", "tensor"), route) if chips > 1
                else lax.ppermute(part, "section", swap)
                for part, route in zip(parts, routes)
            ]
        )

    segments = lax.dynamic_index_in_dim(
        segment_ids.reshape(row_count, length), rank // chips, 0, keepdims=False
    )
    seg_q = lax.dynamic_slice_in_dim(segments, block * count, count, 0)
    seg_k = jnp.concatenate(
        [
            lax.dynamic_slice_in_dim(segments, (block ^ distance) * count, count, 0)
            for distance in range(blocks)
        ]
    )[:, None]
    seg_q = seg_q[None, :]

    saved = []
    x = tokens
    for layer in range(2):
        p_table, o_table, u_table, d_table = tables[layer]
        p_bias, u_bias, pk, pv = smalls[layer]
        q, own = project(x, p_table, p_bias)
        other = exchange([own] * (blocks - 1))
        mixed, raised, inverse = attend(q, own, other, pk, pv, prefix_count, seg_q, seg_k)
        out, z1, r1, z2, r2, slope = feed(x, mixed, o_table, vectors[layer], u_table, d_table, u_bias)
        saved.append((q, own, other, mixed, raised, inverse, (z1, r1, z2, r2), slope))
        x = out

    grad = cotangent
    prefix_grads = []
    for layer in (1, 0):
        p_table, o_table, u_table, d_table = tables[layer]
        p_bias, u_bias, pk, pv = smalls[layer]
        q, own, other, mixed, raised, inverse, kept, slope = saved[layer]
        first, d_mixed = feed_back(grad, kept, slope, o_table, vectors[layer], u_table, d_table)
        dq, down, dother, dpk, dpv = attend_back(
            d_mixed, mixed, inverse, raised, q, own, other, pk, pv
        )
        got = exchange([dother[i] for i in range(blocks - 1)])
        grad = project_back(first, dq, down, got, p_table)
        flat = jnp.stack([dpk[:, :prefix_count], dpv[:, :prefix_count]])
        prefix_grads.append(lax.psum(flat, ("section", "dp", "tensor")))

    give = jnp.where(is_first, out, grad)
    keep = jnp.where(is_first, grad, out)
    got = lax.ppermute(give, "section", swap)
    lower = jnp.where(is_first, keep, got)
    upper = jnp.where(is_first, got, keep)
    if chips == 1:
        row = jnp.concatenate([lower, upper], axis=0)
    else:
        row = jnp.zeros((length, width), bf16)
        row = lax.dynamic_update_slice_in_dim(row, lower, place * count, 0)
        row = lax.dynamic_update_slice_in_dim(row, upper, (chips + place) * count, 0)
    back = lax.all_to_all(row.reshape(ranks, slots, width), "tensor", 0, 0, tiled=True)
    if chips > 1:
        back = jnp.sum(back.reshape(row_count, chips, slots, width), axis=1)
    result = jnp.transpose(back.reshape(micro, rows, slots, width), (0, 2, 1, 3))[None]

    both = jnp.where(is_first, prefix_grads[1], prefix_grads[0])
    both = jnp.transpose(both, (0, 2, 1, 3)).reshape(2, prefix_count, heads_all)
    share = heads_all // ranks
    both = lax.dynamic_slice_in_dim(both, rank * share, share, 2)
    return (result, both[0][None], both[1][None])


def solution(mesh):
    in_specs = (
        P("section", None, "tensor", "dp", None),
        P(None, "dp", None),
        P("section", None, None, "tensor"),
        P("section", None, "tensor"),
        P("section", "tensor", None),
        P("section", None, None),
        P("section", None, None),
        P("section", None, None),
        P("section", None, "tensor"),
        P("section", "tensor"),
        P("section", "tensor", None),
        P("section", None, "tensor"),
        P("section", None, "tensor"),
    )
    out_specs = (
        P("section", None, "tensor", "dp", None),
        P("section", None, "tensor"),
        P("section", None, "tensor"),
    )
    return jax.shard_map(
        per_device, mesh=mesh, in_specs=in_specs, out_specs=out_specs, check_vma=False
    )
```

```python
import functools
import math

import jax
import jax.numpy as jnp
from jax import lax
from jax.experimental import pallas as pl
from jax.experimental.pallas import tpu as pltpu
from jax.sharding import PartitionSpec as P

HEAD = 64
PAIR = 2 * HEAD
EPSILON = 1e-05
MASKED = -1000000000.0
VMEM = 56 * 1024 * 1024
SECTIONS = 2

bf16 = jnp.bfloat16
f32 = jnp.float32


def dot_nn(left, right):
    return lax.dot_general(left, right, (((1,), (0,)), ((), ())), preferred_element_type=f32)


def dot_nt(left, right):
    return lax.dot_general(left, right, (((1,), (1,)), ((), ())), preferred_element_type=f32)


def dot_tn(left, right):
    return lax.dot_general(left, right, (((0,), (0,)), ((), ())), preferred_element_type=f32)


def unit(hidden):
    average = jnp.mean(hidden, axis=-1, keepdims=True)
    centered = hidden - average
    variance = jnp.mean(centered * centered, axis=-1, keepdims=True)
    inverse = lax.rsqrt(variance + EPSILON)
    return centered * inverse, inverse


def unit_back(grad, normed, inverse, gain):
    scaled = grad * gain
    return inverse * (
        scaled
        - jnp.mean(scaled, axis=-1, keepdims=True)
        - normed * jnp.mean(scaled * normed, axis=-1, keepdims=True)
    )


GROUP = 1024


class Copies:
    def __init__(self, semaphores):
        self.semaphores = semaphores
        self.used = 0

    def start(self, source, target):
        copy = pltpu.make_async_copy(source, target, self.semaphores.at[self.used])
        self.used += 1
        copy.start()
        return copy


def wait(copies):
    for copy in copies:
        copy.wait()


def call(kernel, in_specs, out_specs, out_shape, scratch=(), grid=None, flops=0, moved=0, exps=0):
    more = {} if grid is None else {"grid": grid}
    return pl.pallas_call(
        kernel,
        in_specs=in_specs,
        out_specs=out_specs,
        out_shape=out_shape,
        scratch_shapes=list(scratch),
        compiler_params=pltpu.CompilerParams(vmem_limit_bytes=VMEM),
        cost_estimate=pl.CostEstimate(flops=flops, bytes_accessed=moved, transcendentals=exps),
        **more,
    )


IN_VMEM = pl.BlockSpec(memory_space=pltpu.VMEM)
IN_HBM = pl.BlockSpec(memory_space=pl.ANY)
IN_SMEM = pl.BlockSpec(memory_space=pltpu.SMEM)


def whole(shape):
    return pl.BlockSpec(shape, lambda i: (0,) * len(shape))


def struct(shape, dtype):
    return jax.ShapeDtypeStruct(shape, dtype)


def load_heads(copies, ref, first, parts, pairs, target):
    started = []
    for part in range(parts):
        started.append([])
        for pair in range(pairs):
            for half in range(2):
                place = (part * pairs + pair) * PAIR + half * HEAD
                started[-1].append(
                    copies.start(
                        ref.at[half, pair, pl.ds(first + part * HEAD, HEAD)],
                        target.at[pl.ds(place, HEAD)],
                    )
                )
    return started


class Hidden:
    def __init__(self, copies, refs, pieces, up, down):
        self.copies, self.refs, self.pieces = copies, refs, pieces
        self.targets = (up, down)
        self.groups = up.shape[0] // GROUP
        self.started = 0
        self.loads = ([], [])

    def fetch(self, group):
        end = (group + 1) * GROUP
        place = sum(piece[4] for piece in self.pieces[: self.started])
        while self.started < len(self.pieces) and place < end:
            index, lead, *firsts, rows = self.pieces[self.started]
            for kind in range(2):
                copy = self.copies.start(
                    self.refs[index].at[(*lead, pl.ds(firsts[kind], rows))],
                    self.targets[kind].at[pl.ds(place, rows)],
                )
                self.loads[kind].append((place, copy))
            place += rows
            self.started += 1

    def wait(self, group, kind):
        end = (group + 1) * GROUP
        while self.loads[kind] and self.loads[kind][0][0] < end:
            self.loads[kind].pop(0)[1].wait()


def project_kernel(first, x_ref, w_ref, b_ref, q_ref, kv_ref, weight, stage, semaphores):
    copies = Copies(semaphores)
    pairs = stage.shape[1]
    wide = pairs * PAIR
    loads = load_heads(copies, w_ref, first, 3, pairs, weight)
    stores = []
    for part in (0, 1, 2):
        wait(loads[part])
        out = dot_nt(x_ref[...], weight[part * wide : (part + 1) * wide]) + b_ref[part]
        out = out.astype(bf16)
        if part == 0:
            out = out * bf16(1.0 / math.sqrt(HEAD))
        for pair in range(pairs):
            stage[part, pair] = out[:, pair * PAIR : (pair + 1) * PAIR]
        target = q_ref if part == 0 else kv_ref.at[part - 1]
        stores.append(copies.start(stage.at[part], target))
    wait(stores)


def project(x, table, bias):
    count, width = x.shape
    pairs = table[0].shape[1]
    return call(
        functools.partial(project_kernel, table[1]),
        [IN_VMEM, IN_HBM, IN_VMEM],
        [IN_HBM, IN_HBM],
        [struct((pairs, count, PAIR), bf16), struct((2, pairs, count, PAIR), bf16)],
        scratch=[
            pltpu.VMEM((3 * pairs * PAIR, width), bf16),
            pltpu.VMEM((3, pairs, count, PAIR), bf16),
            pltpu.SemaphoreType.DMA((6 * pairs + 3,)),
        ],
        flops=2 * count * width * 3 * PAIR * pairs,
        moved=2 * (count * width * 4 + 3 * width * PAIR * pairs),
    )(x, table[0], bias)


def feed_forward(copies, places, x_ref, mixed_ref, ow_ref, h_refs, vec_ref, ub_ref,
                 z1_ref, r1_ref, weight_o, weight_u, weight_d, slope, normed, low, acc):
    o_first, pieces = places
    pairs = mixed_ref.shape[0]
    loads_o = load_heads(copies, ow_ref, o_first, 1, pairs, weight_o)[0]
    weights = Hidden(copies, h_refs, pieces, weight_u, weight_d)
    groups = weights.groups
    weights.fetch(0)
    mixed = jnp.concatenate([mixed_ref[i] for i in range(pairs)], axis=1)
    wait(loads_o)
    attended = dot_nn(mixed, weight_o[...])
    z, r = unit(x_ref[...].astype(f32) + attended + vec_ref[0:1])
    z1_ref[...] = z
    r1_ref[...] = r
    out = z * vec_ref[2:3] + vec_ref[4:5]
    normed[...] = out
    low[...] = out.astype(bf16)

    def before(group):
        weights.fetch(min(group + 1, groups - 1))
        weights.wait(group, 0)
        span = slice(group * GROUP, (group + 1) * GROUP)
        return dot_nt(low[...], weight_u[span]) + ub_ref[:, span]

    later = before(0)
    for group in range(groups):
        pre = later
        if group + 1 < groups:
            later = before(group + 1)
        span = slice(group * GROUP, (group + 1) * GROUP)
        spread = 0.5 + 0.5 * lax.erf(pre * math.sqrt(0.5))
        bell = jnp.exp(-0.5 * pre * pre) * (1.0 / math.sqrt(2.0 * math.pi))
        slope[:, span] = (spread + pre * bell).astype(bf16)
        weights.wait(group, 1)
        out = dot_nn((pre * spread).astype(bf16), weight_d[span])
        if group == 0:
            acc[...] = out
        else:
            acc[...] += out
    return unit(normed[...] + acc[...] + vec_ref[1:2])


def feed_kernel(places, sources, blocks, x_ref, mixed_ref, ow_ref, vec_ref, ub_ref, rank_ref, *rest):
    h_refs = rest[:sources]
    out_refs = rest[sources : sources + max(blocks, 1)]
    (z1_ref, r1_ref, z2_ref, r2_ref, slope_ref, weight_o, weight_u, weight_d,
     z1, slope, normed, low, acc, semaphores) = rest[sources + max(blocks, 1) :]
    copies = Copies(semaphores)
    z, r = feed_forward(
        copies, places, x_ref, mixed_ref, ow_ref, h_refs, vec_ref, ub_ref,
        z1, r1_ref, weight_o, weight_u, weight_d, slope, normed, low, acc,
    )
    stores = [copies.start(z1, z1_ref), copies.start(slope, slope_ref)]
    acc[...] = z
    r2_ref[...] = r
    stores.append(copies.start(acc, z2_ref))
    low[...] = (z * vec_ref[3:4] + vec_ref[5:6]).astype(bf16)
    rows = low.shape[0] // max(blocks, 1)
    for j in range(max(blocks, 1)):
        start = pl.multiple_of((rank_ref[0] ^ j) * rows, rows) if blocks else 0
        stores.append(copies.start(low.at[pl.ds(start, rows)], out_refs[j]))
    wait(stores)


def feed_scratch(count, width, wide, hidden, pairs):
    return [
        pltpu.VMEM((wide, width), bf16),
        pltpu.VMEM((hidden, width), bf16),
        pltpu.VMEM((hidden, width), bf16),
        pltpu.VMEM((count, width), f32),
        pltpu.VMEM((count, hidden), bf16),
        pltpu.VMEM((count, width), f32),
        pltpu.VMEM((count, width), bf16),
        pltpu.VMEM((count, width), f32),
        pltpu.SemaphoreType.DMA((16 * pairs + 8,)),
    ]


def feed_sizes(x, mixed, up_bias):
    count, width = x.shape
    pairs = mixed.shape[0]
    return count, width, pairs, pairs * PAIR, up_bias.shape[1]


def feed(x, mixed, tables, vectors, up_bias, rank, blocks):
    o_table, (arrays, pieces) = tables
    count, width, pairs, wide, hidden = feed_sizes(x, mixed, up_bias)
    square = struct((count, width), f32)
    column = struct((count, 1), f32)
    parts = max(blocks, 1)
    out, kept = [], []
    found = call(
        functools.partial(feed_kernel, (o_table[1], pieces), len(arrays), blocks),
        [IN_VMEM, IN_VMEM, IN_HBM, IN_VMEM, IN_VMEM, IN_SMEM] + [IN_HBM] * len(arrays),
        [IN_HBM] * parts + [IN_HBM, IN_VMEM, IN_HBM, IN_VMEM, IN_HBM],
        [struct((count // parts, width), bf16)] * parts
        + [square, column, square, column, struct((count, hidden), bf16)],
        scratch=feed_scratch(count, width, wide, hidden, pairs),
        flops=2 * count * width * (wide + 2 * hidden),
        moved=2 * (2 * hidden * width + 12 * count * width),
        exps=2 * count * hidden,
    )(x, mixed, o_table[0], vectors, up_bias, rank, *arrays)
    return (found[:blocks] if blocks else found[0], *found[parts:])


def feed_back(weight_o, weight_u, weight_d, vec_ref, z1, r1, slope, low, acc,
              first_ref, mixed_ref, before=lambda group: None, ready=lambda: None):
    pairs = mixed_ref.shape[0]
    low[...] = acc[...].astype(bf16)
    for group in range(weight_u.shape[0] // GROUP):
        before(group)
        span = slice(group * GROUP, (group + 1) * GROUP)
        d_act = dot_nt(low[...], weight_d[span])
        d_pre = (d_act * slope[:, span].astype(f32)).astype(bf16)
        acc[...] += dot_nn(d_pre, weight_u[span])
    ready()
    first = unit_back(acc[...], z1[...], r1[...], vec_ref[2:3])
    first_ref[...] = first
    d_mixed = dot_nt(first.astype(bf16), weight_o[...]).astype(bf16)
    for pair in range(pairs):
        mixed_ref[pair] = d_mixed[:, pair * PAIR : (pair + 1) * PAIR]


def scatter_rows(stage, rank_ref, targets):
    rows = targets[0].shape[0]
    for j, target in enumerate(targets):
        start = pl.multiple_of((rank_ref[0] ^ j) * rows, rows)
        target[...] = stage[pl.ds(start, rows)]


def project_back(first_ref, dq_ref, own_ref, got_ref, weight, loads):
    pairs = dq_ref.shape[0]
    wide = pairs * PAIR
    total = first_ref[...]
    for part in range(3):
        columns = []
        for pair in range(pairs):
            if part == 0:
                columns.append(dq_ref[pair])
            else:
                column = own_ref[part - 1, pair].astype(f32)
                for i in range(got_ref.shape[0]):
                    column += got_ref[i, part - 1, pair].astype(f32)
                columns.append(column.astype(bf16))
        wait(loads[part])
        total += dot_nn(jnp.concatenate(columns, axis=1), weight[part * wide : (part + 1) * wide])
    return total


def link_kernel(p_first, places, sources, *rest):
    if p_first is None:
        grad_ref, *rest = rest
    else:
        first1_ref, dq_ref, own_ref, got_ref, pw_ref, *rest = rest
    ow_ref, vec_ref, z1_ref, r1_ref, z2_ref, r2_ref, slope_ref, *rest = rest
    h_refs = rest[:sources]
    (first_ref, d_mixed_ref,
     weight_o, weight_u, weight_d, z1, slope, low, acc, semaphores, *weight_p) = rest[sources:]
    o_first, pieces = places
    copies = Copies(semaphores)
    pairs = d_mixed_ref.shape[0]
    if p_first is not None:
        loads_p = load_heads(copies, pw_ref, p_first, 3, pairs, weight_p[0])
    weights = Hidden(copies, h_refs, pieces, weight_u, weight_d)
    groups = weights.groups
    slopes = []

    def fetch(group):
        weights.fetch(group)
        span = (slice(None), pl.ds(group * GROUP, GROUP))
        slopes.append(copies.start(slope_ref.at[span], slope.at[span]))

    if p_first is None:
        fetch(0)
        grad = grad_ref[...].astype(f32)
    else:
        total = project_back(first1_ref, dq_ref, own_ref, got_ref, weight_p[0], loads_p)
        fetch(0)
        grad = total.astype(bf16).astype(f32)
    acc[...] = unit_back(grad, z2_ref[...], r2_ref[...], vec_ref[3:4])
    last = []

    def before(group):
        if group + 1 < groups:
            fetch(group + 1)
        else:
            last.append(copies.start(z1_ref, z1))
            last.extend(load_heads(copies, ow_ref, o_first, 1, pairs, weight_o)[0])
        slopes[group].wait()
        weights.wait(group, 0)
        weights.wait(group, 1)

    feed_back(
        weight_o, weight_u, weight_d, vec_ref, z1, r1_ref, slope, low, acc, first_ref, d_mixed_ref,
        before, lambda: wait(last),
    )


def link(grads, p_table, tables, vectors, kept):
    o_table, (arrays, pieces) = tables
    count, width = grads[0].shape
    pairs = o_table[0].shape[1]
    wide = pairs * PAIR
    slope = kept[-1]
    hidden = slope.shape[1]
    more = [] if p_table is None else [p_table[0]]
    return call(
        functools.partial(
            link_kernel, p_table and p_table[1], (o_table[1], pieces), len(arrays)
        ),
        [IN_VMEM] * len(grads) + [IN_HBM] * len(more)
        + [IN_HBM, IN_VMEM, IN_HBM, IN_VMEM, IN_VMEM, IN_VMEM, IN_HBM]
        + [IN_HBM] * len(arrays),
        [IN_VMEM] * 2,
        [struct((count, width), f32), struct((pairs, count, PAIR), bf16)],
        scratch=[
            pltpu.VMEM((wide, width), bf16),
            pltpu.VMEM((hidden, width), bf16),
            pltpu.VMEM((hidden, width), bf16),
            pltpu.VMEM((count, width), f32),
            pltpu.VMEM((count, hidden), bf16),
            pltpu.VMEM((count, width), bf16),
            pltpu.VMEM((count, width), f32),
            pltpu.SemaphoreType.DMA((16 * pairs + 16,)),
        ]
        + [pltpu.VMEM((3 * wide, width), bf16)] * len(more),
        flops=2 * count * width * (4 * wide + 2 * hidden),
        moved=2 * (2 * hidden * width + 4 * wide * width + 16 * count * width),
    )(*grads, *more, o_table[0], vectors, *kept, *arrays)


def leave_kernel(p_first, first_ref, dq_ref, own_ref, got_ref, pw_ref, rank_ref, *rest):
    (*out_refs, weight_p, low, semaphores) = rest
    copies = Copies(semaphores)
    loads = load_heads(copies, pw_ref, p_first, 3, dq_ref.shape[0], weight_p)
    low[...] = project_back(first_ref, dq_ref, own_ref, got_ref, weight_p, loads).astype(bf16)
    scatter_rows(low, rank_ref, out_refs)


def leave(first, dq, own, got, p_table, rank, blocks):
    count, width = first.shape
    pairs = dq.shape[0]
    return call(
        functools.partial(leave_kernel, p_table[1]),
        [IN_VMEM] * 4 + [IN_HBM, IN_SMEM],
        [IN_VMEM] * blocks,
        [struct((count // blocks, width), bf16)] * blocks,
        scratch=[
            pltpu.VMEM((3 * pairs * PAIR, width), bf16),
            pltpu.VMEM((count, width), bf16),
            pltpu.SemaphoreType.DMA((6 * pairs,)),
        ],
        flops=2 * count * width * 3 * PAIR * pairs,
        moved=2 * (count * width * 7 + 3 * width * PAIR * pairs),
    )(first, dq, own, got, p_table[0], rank)


def attend_kernel(
    prefix_count, q_ref, own_ref, other_ref, pk_ref, pv_ref, sq_ref, sk_ref,
    mixed_ref, raised_ref, inverse_ref, bias_ref,
):
    pad = pk_ref.shape[1]
    others = other_ref.shape[0]

    @pl.when(pl.program_id(0) == 0)
    def _():
        row = lax.broadcasted_iota(jnp.int32, (pad, bias_ref.shape[1]), 0)
        bias_ref[:pad] = jnp.where(row < prefix_count, 0.0, MASKED)
        keys = sk_ref[...]
        same = (keys == sq_ref[...]) & (keys >= 0)
        bias_ref[pad:] = jnp.where(same, 0.0, MASKED)

    keys = jnp.concatenate(
        [pk_ref[0], own_ref[0, 0]] + [other_ref[i, 0, 0] for i in range(others)], axis=0
    )
    values = jnp.concatenate(
        [pv_ref[0], own_ref[1, 0]] + [other_ref[i, 1, 0] for i in range(others)], axis=0
    )
    queries = q_ref[0]
    lane = lax.broadcasted_iota(jnp.int32, queries.shape, 1)
    parts = []
    inverses = []
    for head in range(2):
        chosen = (lane // HEAD) == head
        scores = dot_nt(keys, jnp.where(chosen, queries, bf16(0))) + bias_ref[...]
        raised = jnp.exp(scores - jnp.max(scores, axis=0, keepdims=True))
        inverse = 1.0 / jnp.sum(raised, axis=0, keepdims=True)
        low = raised.astype(bf16)
        raised_ref[0, head] = low
        out = dot_tn(values, low)[head * HEAD : (head + 1) * HEAD]
        parts.append(out * inverse)
        inverses.append(jnp.broadcast_to(inverse, out.shape))
    mixed_ref[0] = jnp.concatenate(parts, axis=0).T.astype(bf16)
    inverse_ref[0] = jnp.concatenate(inverses, axis=0).T


def attend(q, own, other, pk, pv, prefix_count, seg_q, seg_k):
    pairs, count, _ = q.shape
    others = other.shape[0]
    pad = pk.shape[1]
    total = pad + count * (others + 1)
    by_pair = pl.BlockSpec((1, count, PAIR), lambda i: (i, 0, 0))
    by_prefix = pl.BlockSpec((1, pad, PAIR), lambda i: (i, 0, 0))
    return call(
        functools.partial(attend_kernel, prefix_count),
        [
            by_pair,
            pl.BlockSpec((2, 1, count, PAIR), lambda i: (0, i, 0, 0)),
            pl.BlockSpec((others, 2, 1, count, PAIR), lambda i: (0, 0, i, 0, 0)),
            by_prefix,
            by_prefix,
            whole((1, count)),
            whole((total - pad, 1)),
        ],
        [
            by_pair,
            pl.BlockSpec((1, 2, total, count), lambda i: (i, 0, 0, 0)),
            by_pair,
        ],
        [
            struct((pairs, count, PAIR), bf16),
            struct((pairs, 2, total, count), bf16),
            struct((pairs, count, PAIR), f32),
        ],
        scratch=[pltpu.VMEM((total, count), f32)],
        grid=(pairs,),
        flops=8 * total * count * PAIR * pairs,
        moved=4 * pairs * total * count,
        exps=2 * pairs * total * count,
    )(q, own, other, pk, pv, seg_q, seg_k)


def attend_back_kernel(
    grad_ref, mixed_ref, inverse_ref, raised_ref, q_ref, own_ref, other_ref, pk_ref, pv_ref,
    dq_ref, down_ref, dother_ref, prefix_ref,
):
    pad = pk_ref.shape[1]
    others = other_ref.shape[0]
    count = q_ref.shape[1]
    keys = jnp.concatenate(
        [pk_ref[0], own_ref[0, 0]] + [other_ref[i, 0, 0] for i in range(others)], axis=0
    )
    values = jnp.concatenate(
        [pv_ref[0], own_ref[1, 0]] + [other_ref[i, 1, 0] for i in range(others)], axis=0
    )
    queries = q_ref[0]
    lane = lax.broadcasted_iota(jnp.int32, queries.shape, 1)
    scaled = grad_ref[0].astype(f32) * inverse_ref[0]
    products = (scaled * mixed_ref[0].astype(f32)).T
    scaled = scaled.astype(bf16)
    d_keys = jnp.zeros(keys.shape, f32)
    d_values = jnp.zeros(keys.shape, f32)
    parts = []
    for head in range(2):
        chosen = (lane // HEAD) == head
        span = slice(head * HEAD, (head + 1) * HEAD)
        delta = jnp.sum(products[span], axis=0, keepdims=True)
        here = jnp.where(chosen, scaled, bf16(0))
        raised = raised_ref[0, head]
        d_score = (raised.astype(f32) * (dot_nt(values, here) - delta)).astype(bf16)
        d_values += dot_nn(raised, here)
        d_keys += dot_nn(d_score, jnp.where(chosen, queries, bf16(0)))
        parts.append(dot_tn(keys, d_score)[span])
    d_query = jnp.concatenate(parts, axis=0).T * (1.0 / math.sqrt(HEAD))
    dq_ref[0] = d_query.astype(bf16)
    prefix_ref[0, :pad] = d_keys[:pad]
    prefix_ref[0, pad:] = d_values[:pad]
    down_ref[0, 0] = d_keys[pad : pad + count].astype(bf16)
    down_ref[1, 0] = d_values[pad : pad + count].astype(bf16)
    for i in range(others):
        span = slice(pad + (i + 1) * count, pad + (i + 2) * count)
        dother_ref[i, 0, 0] = d_keys[span].astype(bf16)
        dother_ref[i, 1, 0] = d_values[span].astype(bf16)


def attend_back(grad, mixed, inverse, raised, q, own, other, pk, pv):
    pairs, count, _ = q.shape
    others = other.shape[0]
    pad = pk.shape[1]
    total = pad + count * (others + 1)
    by_pair = pl.BlockSpec((1, count, PAIR), lambda i: (i, 0, 0))
    by_prefix = pl.BlockSpec((1, pad, PAIR), lambda i: (i, 0, 0))
    by_own = pl.BlockSpec((2, 1, count, PAIR), lambda i: (0, i, 0, 0))
    by_other = pl.BlockSpec((others, 2, 1, count, PAIR), lambda i: (0, 0, i, 0, 0))
    return call(
        attend_back_kernel,
        [
            by_pair, by_pair, by_pair,
            pl.BlockSpec((1, 2, total, count), lambda i: (i, 0, 0, 0)),
            by_pair, by_own, by_other, by_prefix, by_prefix,
        ],
        [by_pair, by_own, by_other, pl.BlockSpec((1, 2 * pad, PAIR), lambda i: (i, 0, 0))],
        [
            struct(q.shape, bf16),
            struct(own.shape, bf16),
            struct(other.shape, bf16),
            struct((pairs, 2 * pad, PAIR), f32),
        ],
        grid=(pairs,),
        flops=16 * total * count * PAIR * pairs,
        moved=4 * pairs * total * count,
    )(grad, mixed, inverse, raised, q, own, other, pk, pv)


def per_device(
    boundary, segment_ids, project_weight, project_bias, output_weight, output_biases,
    norm_gains, norm_shifts, up_weight, up_bias, down_weight, prefix_keys, prefix_values,
):
    section = lax.axis_index("section")
    rank = lax.axis_index("tensor")
    ranks = lax.axis_size("tensor")
    is_first = section == 0
    micro, slots, rows, width = boundary.shape[1:]
    length = slots * ranks
    row_count = micro * rows
    chips = ranks // row_count
    blocks = SECTIONS * chips
    count = length // blocks
    place = rank % chips
    swap = [(0, 1), (1, 0)]
    after = lambda value, *first: lax.optimization_barrier((value, *first))[0]
    heads_all = project_weight.shape[3] * ranks
    pairs = heads_all // PAIR
    shards = ranks // pairs
    prefix_count = prefix_keys.shape[1]
    pad = -(-prefix_count // 32) * 32
    low_width = project_weight.shape[3] // 2
    hidden = up_weight.shape[2] // 2

    quick = chips == 1 and ranks == 8 and lax.axis_size("dp") == 2

    half_ranks = ranks // 2
    low_rank = rank % half_ranks
    block = section * chips + place
    by_row = jnp.transpose(boundary[0], (0, 2, 1, 3)).reshape(row_count, slots, width)

    def ordered(parts):
        for bit in (1, 2):
            flip = (low_rank & bit) != 0
            parts = [jnp.where(flip, parts[i ^ bit], part) for i, part in enumerate(parts)]
        return parts

    if quick:
        lower, upper = by_row[:half_ranks], by_row[half_ranks:]
        keep = jnp.where(is_first, lower, upper)
        got = lax.ppermute(jnp.where(is_first, upper, lower), "section", swap)

        def arrive(rows_here):
            parts = []
            for j in range(half_ranks):
                route = [
                    (s * ranks + t, (t // half_ranks) * ranks + half_ranks * s + ((t % half_ranks) ^ j))
                    for s in range(SECTIONS)
                    for t in range(ranks)
                ]
                part = lax.dynamic_index_in_dim(rows_here, low_rank ^ j, 0, keepdims=False)
                parts.append(lax.ppermute(part, ("section", "tensor"), route))
            return jnp.concatenate(ordered(parts), axis=0)

        tokens = arrive(jnp.where(is_first, keep, got))
        cotangent_rows = jnp.where(is_first, got, keep)
    else:
        if chips > 1:
            by_row = jnp.repeat(by_row, chips, axis=0)
        row = lax.all_to_all(by_row, "tensor", 0, 0, tiled=True).reshape(length, width)
        other_block = (1 - section) * chips + place
        mine = lax.dynamic_slice_in_dim(row, block * count, count, 0)
        theirs = lax.dynamic_slice_in_dim(row, other_block * count, count, 0)
        got = lax.ppermute(theirs, "section", swap)
        tokens = jnp.where(is_first, mine, got)
        cotangent = jnp.where(is_first, got, mine)

    project_rows = jnp.transpose(project_weight[0], (1, 2, 0)).reshape(3, 2, low_width, width)
    project_rows = jnp.transpose(project_rows, (1, 0, 2, 3)).reshape(2, 3 * low_width, width)
    out_rows = output_weight[0].reshape(2, low_width, width)
    up_rows = jnp.transpose(up_weight[0], (1, 0)).reshape(2, hidden, width)
    down_rows = down_weight[0].reshape(2, hidden, width)
    small = jnp.concatenate(
        [
            jnp.transpose(project_bias[0].reshape(3, 2, low_width), (1, 0, 2)).reshape(2, -1),
            up_bias[0].reshape(2, hidden),
            jnp.transpose(prefix_keys[0].reshape(-1, 2, low_width), (1, 0, 2)).reshape(2, -1),
            jnp.transpose(prefix_values[0].reshape(-1, 2, low_width), (1, 0, 2)).reshape(2, -1),
        ],
        axis=1,
    )
    small_size = small.shape[1]
    small_rows = -(-small_size // (16 * width)) * 16
    small = jnp.pad(small, ((0, 0), (0, small_rows * width - small_size)))
    packed = jnp.concatenate(
        [project_rows, out_rows, up_rows, down_rows, small.reshape(2, small_rows, width)], axis=1
    )
    keep = lax.dynamic_index_in_dim(packed, section, 0, keepdims=False)
    give = lax.dynamic_index_in_dim(packed, 1 - section, 0, keepdims=False)
    got = lax.ppermute(give, "section", swap)
    layer_rows = [jnp.where(is_first, keep, got), jnp.where(is_first, got, keep)]
    sizes = [3 * low_width, low_width, hidden, hidden, small_rows]
    p_end, o_end, u_end, d_end, s_end = [sum(sizes[: i + 1]) for i in range(len(sizes))]
    plane = lax.axis_index("dp")
    gather = lambda parts: lax.all_gather(
        jnp.concatenate(parts, axis=0), ("section", "tensor"), axis=0
    ).reshape(2, ranks, -1, width)

    def unpack(flat):
        cut = 0
        found = []
        for groups, size in ((3, low_width), (1, hidden), (prefix_count, low_width), (prefix_count, low_width)):
            part = flat[:, :, cut : cut + groups * size].reshape(2, pairs, shards, groups, size)
            cut += groups * size
            if shards == 1:
                part = part[:, :, 0]
            else:
                part = jnp.transpose(part, (2, 1, 3, 0, 4)).reshape(2, pairs, groups, 2 * size)
            found.append(part)
        p_bias = jnp.transpose(found[0], (2, 1, 0, 3)).reshape(3, 1, heads_all).astype(f32)
        prefix = [
            jnp.pad(
                jnp.transpose(part, (1, 2, 0, 3)).reshape(pairs, prefix_count, PAIR),
                ((0, 0), (0, pad - prefix_count), (0, 0)),
            )
            for part in found[2:]
        ]
        return p_bias, found[1][:, :, 0], prefix[0], prefix[1]

    tables = []
    smalls = []
    early_rows = [
        layer_rows[0][:d_end], layer_rows[1][:p_end], layer_rows[0][d_end:], layer_rows[1][d_end:],
    ]
    late_rows = layer_rows[1][p_end:d_end]
    early = gather(early_rows)
    late = gather([after(late_rows, early, tokens)])
    def table(array, first, size, groups=1):
        if shards == 1:
            return (array, first, size)
        part = array[:, :, first : first + size].reshape(
            2, pairs, shards, groups, size // groups, width
        )
        part = jnp.transpose(part, (2, 1, 3, 0, 4, 5))
        return (part.reshape(2, pairs, 2 * size, width), 0, 2 * size)

    for layer in range(2):
        source, shift = (late, -p_end) if layer else (early, 0)
        up, u_first, rows_here = table(source, shift + o_end, 2 * hidden, 2)
        rows_here //= 2
        pieces = tuple(
            (0, (s, t), u_first, u_first + rows_here, rows_here)
            for s in range(2)
            for t in range(pairs)
        )
        tables.append(
            (
                table(early, layer * d_end, 3 * low_width, 3),
                table(source, shift + p_end, low_width),
                ((up,), pieces),
            )
        )
        start = d_end + p_end + layer * small_rows
        p_bias, u_bias, pk, pv = unpack(
            early[:, :, start : start + small_rows].reshape(2, ranks, -1)
        )
        smalls.append((p_bias, u_bias.reshape(1, -1).astype(f32), pk, pv))

    own_vectors = jnp.concatenate(
        [output_biases[0], norm_gains[0], norm_shifts[0], norm_shifts[0]], axis=0
    )
    got_vectors = lax.ppermute(own_vectors, "section", swap)
    vectors = [
        jnp.where(is_first, own_vectors, got_vectors).astype(f32),
        jnp.where(is_first, got_vectors, own_vectors).astype(f32),
    ]

    def flips():
        routes = []
        for distance in range(1, blocks):
            route = []
            for s in range(SECTIONS):
                for t in range(ranks):
                    index = (s * chips + t % chips) ^ distance
                    route.append(
                        (s * ranks + t, (index // chips) * ranks + t // chips * chips + index % chips)
                    )
            routes.append(route)
        return routes

    routes = flips()

    def exchange(parts):
        return jnp.stack(
            [
                lax.ppermute(part, ("section", "tensor"), route) if chips > 1
                else lax.ppermute(part, "section", swap)
                for part, route in zip(parts, routes)
            ]
        )

    segments = lax.dynamic_index_in_dim(
        segment_ids.reshape(row_count, length), rank // chips, 0, keepdims=False
    )
    seg_q = lax.dynamic_slice_in_dim(segments, block * count, count, 0)
    seg_k = jnp.concatenate(
        [
            lax.dynamic_slice_in_dim(segments, (block ^ distance) * count, count, 0)
            for distance in range(blocks)
        ]
    )[:, None]
    seg_q = seg_q[None, :]

    out_blocks = half_ranks if quick else 1
    order = (low_rank if quick else 0 * rank).astype(jnp.int32).reshape(1)
    saved = []
    x = tokens
    for layer in range(2):
        p_table, *others = tables[layer]
        p_bias, u_bias, pk, pv = smalls[layer]
        q, own = project(x, p_table, p_bias)
        other = exchange([own] * (blocks - 1))
        mixed, raised, inverse = attend(q, own, other, pk, pv, prefix_count, seg_q, seg_k)
        saved.append((mixed, inverse, raised, q, own, other, pk, pv))
        if layer == 1 and quick:
            cotangent = arrive(after(cotangent_rows, late))
        x, *kept = feed(
            x, mixed, others, vectors[layer], u_bias, order, out_blocks if layer else 0
        )
        saved[-1] += (kept,)
    outs = x
    kept_0, kept_1 = (entry[-1] for entry in saved)
    saved = [entry[:-1] for entry in saved]
    first, d_mixed = link((cotangent,), None, tables[1][1:], vectors[1], kept_1)

    def send_blocks(parts):
        got = []
        for j, part in enumerate(parts):
            route = [
                (s * ranks + t, (t // half_ranks) * ranks + half_ranks * s + ((t % half_ranks) ^ j))
                for s in range(SECTIONS)
                for t in range(ranks)
            ]
            got.append(lax.ppermute(part, ("section", "tensor"), route))
        return got

    dq, down, dother, prefix_1 = attend_back(d_mixed, *saved[1])
    if quick:
        outs = send_blocks(outs)
        dother, *outs = lax.optimization_barrier((dother, *outs))
    got = exchange([dother[i] for i in range(blocks - 1)])
    first, d_mixed = link(
        (first, dq, down, got), tables[1][0], tables[0][1:], vectors[0], kept_0
    )
    dq, down, dother, prefix_0 = attend_back(d_mixed, *saved[0])
    got = exchange([dother[i] for i in range(blocks - 1)])
    if quick:
        prefix = jnp.stack([prefix_0, prefix_1], axis=1)
        lower, upper = prefix[: pairs // 2], prefix[pairs // 2 :]
        other = lax.ppermute(jnp.where(is_first, upper, lower), "section", swap)
        prefix = jnp.where(is_first, lower, upper) + other
        got, prefix = lax.optimization_barrier((got, prefix))
    grads = leave(first, dq, down, got, tables[0][0], order, out_blocks)

    if quick:
        grads = send_blocks(grads)
        prefix = sum(
            send_blocks(
                [
                    lax.dynamic_index_in_dim(prefix, low_rank ^ j, 0, keepdims=False)
                    for j in range(half_ranks)
                ]
            )
        )
        outs = jnp.stack(ordered(outs))
        prefix += lax.ppermute(prefix, "dp", swap)
        prefix = jnp.where(is_first, prefix[0], prefix[1]) + lax.ppermute(
            jnp.where(is_first, prefix[1], prefix[0]), "section", swap
        )
        grads = jnp.stack(ordered(grads))
        keep = jnp.where(is_first, grads, outs)
        got = lax.ppermute(jnp.where(is_first, outs, grads), "section", swap)
        back = jnp.concatenate(
            [jnp.where(is_first, keep, got), jnp.where(is_first, got, keep)], axis=0
        )
    else:
        keep = jnp.where(is_first, grads[0], outs[0])
        got = lax.ppermute(jnp.where(is_first, outs[0], grads[0]), "section", swap)
        row = jnp.zeros((length, width), bf16)
        row = lax.dynamic_update_slice_in_dim(
            row, jnp.where(is_first, keep, got), place * count, 0
        )
        row = lax.dynamic_update_slice_in_dim(
            row, jnp.where(is_first, got, keep), (chips + place) * count, 0
        )
        back = lax.all_to_all(row.reshape(ranks, slots, width), "tensor", 0, 0, tiled=True)
        back = jnp.sum(back.reshape(row_count, chips, slots, width), axis=1)
    result = jnp.transpose(back.reshape(micro, rows, slots, width), (0, 2, 1, 3))[None]

    if quick:
        both = prefix.reshape(2, pad, PAIR)[:, :prefix_count]
    else:
        both = jnp.where(
            is_first,
            lax.psum(prefix_0, ("section", "dp", "tensor")),
            lax.psum(prefix_1, ("section", "dp", "tensor")),
        )
        both = both.reshape(pairs, 2, pad, PAIR)[:, :, :prefix_count]
        both = jnp.transpose(both, (1, 2, 0, 3)).reshape(2, prefix_count, heads_all)
        share = heads_all // ranks
        both = lax.dynamic_slice_in_dim(both, rank * share, share, 2)
    return (result, both[0][None], both[1][None])


def solution(mesh):
    in_specs = (
        P("section", None, "tensor", "dp", None),
        P(None, "dp", None),
        P("section", None, None, "tensor"),
        P("section", None, "tensor"),
        P("section", "tensor", None),
        P("section", None, None),
        P("section", None, None),
        P("section", None, None),
        P("section", None, "tensor"),
        P("section", "tensor"),
        P("section", "tensor", None),
        P("section", None, "tensor"),
        P("section", None, "tensor"),
    )
    out_specs = (
        P("section", None, "tensor", "dp", None),
        P("section", None, "tensor"),
        P("section", None, "tensor"),
    )
    return jax.shard_map(
        per_device, mesh=mesh, in_specs=in_specs, out_specs=out_specs, check_vma=False
    )
```

```python
import functools
import math

import jax
import jax.numpy as jnp
from jax import lax
from jax.experimental import pallas as pl
from jax.experimental.pallas import tpu as pltpu
from jax.sharding import PartitionSpec as P

HEAD = 64
PAIR = 2 * HEAD
EPSILON = 1e-05
MASKED = -1000000000.0
VMEM = 60 * 1024 * 1024
SECTIONS = 2

bf16 = jnp.bfloat16
f32 = jnp.float32


def dot_nn(left, right):
    return lax.dot_general(left, right, (((1,), (0,)), ((), ())), preferred_element_type=f32)


def dot_nt(left, right):
    return lax.dot_general(left, right, (((1,), (1,)), ((), ())), preferred_element_type=f32)


def dot_tn(left, right):
    return lax.dot_general(left, right, (((0,), (0,)), ((), ())), preferred_element_type=f32)


def unit(hidden):
    average = jnp.mean(hidden, axis=-1, keepdims=True)
    centered = hidden - average
    variance = jnp.mean(centered * centered, axis=-1, keepdims=True)
    inverse = lax.rsqrt(variance + EPSILON)
    return centered * inverse, inverse


def unit_back(grad, normed, inverse, gain):
    scaled = grad * gain
    return inverse * (
        scaled
        - jnp.mean(scaled, axis=-1, keepdims=True)
        - normed * jnp.mean(scaled * normed, axis=-1, keepdims=True)
    )


GROUP = 1024


class Copies:
    def __init__(self, semaphores):
        self.semaphores = semaphores
        self.used = 0

    def start(self, source, target):
        copy = pltpu.make_async_copy(source, target, self.semaphores.at[self.used])
        self.used += 1
        copy.start()
        return copy


def wait(copies):
    for copy in copies:
        copy.wait()


def call(kernel, in_specs, out_specs, out_shape, scratch=(), grid=None, flops=0, moved=0, exps=0):
    more = {} if grid is None else {"grid": grid}
    return pl.pallas_call(
        kernel,
        in_specs=in_specs,
        out_specs=out_specs,
        out_shape=out_shape,
        scratch_shapes=list(scratch),
        compiler_params=pltpu.CompilerParams(vmem_limit_bytes=VMEM),
        cost_estimate=pl.CostEstimate(flops=flops, bytes_accessed=moved, transcendentals=exps),
        **more,
    )


IN_VMEM = pl.BlockSpec(memory_space=pltpu.VMEM)
IN_HBM = pl.BlockSpec(memory_space=pl.ANY)
IN_SMEM = pl.BlockSpec(memory_space=pltpu.SMEM)


def whole(shape):
    return pl.BlockSpec(shape, lambda i: (0,) * len(shape))


def struct(shape, dtype):
    return jax.ShapeDtypeStruct(shape, dtype)


def pack_kernel(p_ref, o_ref, u_ref, d_ref, s_ref, section_ref, keep_ref, give_ref, stage, semaphores):
    copies = Copies(semaphores)
    place = 0
    sources = [(p_ref[part].T, HEAD) for part in range(3)]
    sources += [(o_ref[...], HEAD), (u_ref[...].T, u_ref.shape[1] // 2), (d_ref[...], d_ref.shape[0] // 2)]
    for value, rows in sources:
        for half in range(2):
            stage[half, place : place + rows] = value[half * rows : (half + 1) * rows]
        place += rows
    for half in range(2):
        stage[half, place:] = s_ref[half]
    section = section_ref[0]
    wait([copies.start(stage.at[1 - section], give_ref), copies.start(stage.at[section], keep_ref)])


def pack(project_w, out_w, up_w, down_w, small, section):
    width = down_w.shape[1]
    rows = (project_w.shape[2] * 3 + out_w.shape[0] + up_w.shape[1] + down_w.shape[0]) // 2
    rows += small.shape[1]
    return call(
        pack_kernel,
        [IN_VMEM] * 5 + [IN_SMEM],
        [IN_HBM] * 2,
        [struct((rows, width), bf16)] * 2,
        scratch=[pltpu.VMEM((2, rows, width), bf16), pltpu.SemaphoreType.DMA((2,))],
        moved=8 * rows * width,
    )(project_w, out_w, up_w, down_w, small, section)


def load_heads(copies, ref, first, parts, pairs, target):
    started = []
    for part in range(parts):
        started.append([])
        for pair in range(pairs):
            for half in range(2):
                place = (part * pairs + pair) * PAIR + half * HEAD
                started[-1].append(
                    copies.start(
                        ref.at[half, pair, pl.ds(first + part * HEAD, HEAD)],
                        target.at[pl.ds(place, HEAD)],
                    )
                )
    return started


def load_projection(copies, refs, first, pairs, target, place_ref):
    if len(refs) == 1:
        return load_heads(copies, refs[0], first, 3, pairs, target)
    started = []
    unit_rows = HEAD // 2
    for index, ref in enumerate(refs):
        plane = place_ref[0] if index == 0 else 1 - place_ref[0]
        for half in range(2 if index == 0 else 1):
            here = (half, place_ref[1], 1 - place_ref[1])[index]
            for pair in range(pairs):
                for unit_index in range(3):
                    place = 3 * plane + unit_index
                    row = (place // 2) * pairs * PAIR + (place % 2) * unit_rows
                    row = pl.multiple_of(row + pair * PAIR + here * HEAD, unit_rows)
                    cut = pl.ds((first if index == 0 else 0) + unit_index * unit_rows, unit_rows)
                    started.append(
                        copies.start(
                            ref.at[half, pair, cut] if index == 0 else ref.at[pair, cut],
                            target.at[pl.ds(row, unit_rows)],
                        )
                    )
    return [started, [], []]


class Hidden:
    def __init__(self, copies, refs, pieces, up, down):
        self.copies, self.refs, self.pieces = copies, refs, pieces
        self.targets = (up, down)
        self.groups = up.shape[0] // GROUP
        self.started = 0
        self.loads = ([], [])

    def fetch(self, group):
        end = (group + 1) * GROUP
        place = sum(piece[4] for piece in self.pieces[: self.started])
        while self.started < len(self.pieces) and place < end:
            index, lead, *firsts, rows = self.pieces[self.started]
            for kind in range(2):
                copy = self.copies.start(
                    self.refs[index].at[(*lead, pl.ds(firsts[kind], rows))],
                    self.targets[kind].at[pl.ds(place, rows)],
                )
                self.loads[kind].append((place, copy))
            place += rows
            self.started += 1

    def wait(self, group, kind):
        end = (group + 1) * GROUP
        while self.loads[kind] and self.loads[kind][0][0] < end:
            self.loads[kind].pop(0)[1].wait()


def project_kernel(first, x_ref, b_ref, place_ref, *rest):
    (*w_refs, q_ref, kv_ref, weight, stage, semaphores) = rest
    copies = Copies(semaphores)
    pairs = stage.shape[1]
    wide = pairs * PAIR
    loads = load_projection(copies, w_refs, first, pairs, weight, place_ref)
    stores = []
    for part in (0, 1, 2):
        wait(loads[part])
        out = dot_nt(x_ref[...], weight[part * wide : (part + 1) * wide]) + b_ref[part]
        out = out.astype(bf16)
        if part == 0:
            out = out * bf16(1.0 / math.sqrt(HEAD))
        for pair in range(pairs):
            stage[part, pair] = out[:, pair * PAIR : (pair + 1) * PAIR]
        target = q_ref if part == 0 else kv_ref.at[part - 1]
        stores.append(copies.start(stage.at[part], target))
    wait(stores)


def project(x, table, bias, place):
    count, width = x.shape
    arrays, first = table
    pairs = arrays[0].shape[1]
    return call(
        functools.partial(project_kernel, first),
        [IN_VMEM, IN_VMEM, IN_SMEM] + [IN_HBM] * len(arrays),
        [IN_HBM, IN_HBM],
        [struct((pairs, count, PAIR), bf16), struct((2, pairs, count, PAIR), bf16)],
        scratch=[
            pltpu.VMEM((3 * pairs * PAIR, width), bf16),
            pltpu.VMEM((3, pairs, count, PAIR), bf16),
            pltpu.SemaphoreType.DMA((12 * pairs + 3,)),
        ],
        flops=2 * count * width * 3 * PAIR * pairs,
        moved=2 * (count * width * 4 + 3 * width * PAIR * pairs),
    )(x, bias, place, *arrays)


def feed_forward(copies, places, x_ref, mixed_ref, ow_ref, h_refs, vec_ref, ub_ref,
                 z1_ref, r1_ref, weight_o, weight_u, weight_d, slope, normed, low, acc):
    o_first, pieces = places
    pairs = mixed_ref.shape[0]
    loads_o = load_heads(copies, ow_ref, o_first, 1, pairs, weight_o)[0]
    weights = Hidden(copies, h_refs, pieces, weight_u, weight_d)
    groups = weights.groups
    weights.fetch(groups - 1)
    mixed = jnp.concatenate([mixed_ref[i] for i in range(pairs)], axis=1)
    wait(loads_o)
    attended = dot_nn(mixed, weight_o[...])
    z, r = unit(x_ref[...].astype(f32) + attended + vec_ref[0:1])
    z1_ref[...] = z.astype(bf16)
    r1_ref[...] = r
    out = z * vec_ref[2:3] + vec_ref[4:5]
    normed[...] = out
    low[...] = out.astype(bf16)

    halves = 2
    rows = low.shape[0] // halves

    def before(chunk):
        group, half = divmod(chunk, halves)
        if half == 0:
            weights.fetch(min(group + 1, groups - 1))
            weights.wait(group, 0)
        span = slice(group * GROUP, (group + 1) * GROUP)
        return dot_nt(low[half * rows : (half + 1) * rows], weight_u[span]) + ub_ref[:, span]

    later = before(0)
    for chunk in range(groups * halves):
        group, half = divmod(chunk, halves)
        pre = later
        if chunk + 1 < groups * halves:
            later = before(chunk + 1)
        span = slice(group * GROUP, (group + 1) * GROUP)
        here = slice(half * rows, (half + 1) * rows)
        spread = 0.5 + 0.5 * lax.erf(pre * math.sqrt(0.5))
        bell = jnp.exp(-0.5 * pre * pre) * (1.0 / math.sqrt(2.0 * math.pi))
        slope[here, span] = (spread + pre * bell).astype(bf16)
        if half == 0:
            weights.wait(group, 1)
        out = dot_nn((pre * spread).astype(bf16), weight_d[span])
        if group == 0:
            acc[here] = out
        else:
            acc[here] += out
    return unit(normed[...] + acc[...] + vec_ref[1:2])


def feed_kernel(places, sources, blocks, x_ref, mixed_ref, ow_ref, vec_ref, ub_ref, rank_ref, *rest):
    h_refs = rest[:sources]
    out_refs = rest[sources : sources + max(blocks, 1)]
    (z1_ref, r1_ref, z2_ref, r2_ref, slope_ref, weight_o, weight_u, weight_d,
     z1, z2, slope, normed, low, acc, semaphores) = rest[sources + max(blocks, 1) :]
    copies = Copies(semaphores)
    z, r = feed_forward(
        copies, places, x_ref, mixed_ref, ow_ref, h_refs, vec_ref, ub_ref,
        z1, r1_ref, weight_o, weight_u, weight_d, slope, normed, low, acc,
    )
    stores = [copies.start(z1, z1_ref), copies.start(slope, slope_ref)]
    z2[...] = z.astype(bf16)
    r2_ref[...] = r
    stores.append(copies.start(z2, z2_ref))
    low[...] = (z * vec_ref[3:4] + vec_ref[5:6]).astype(bf16)
    rows = low.shape[0] // max(blocks, 1)
    for j in range(max(blocks, 1)):
        start = pl.multiple_of((rank_ref[0] ^ j) * rows, rows) if blocks else 0
        stores.append(copies.start(low.at[pl.ds(start, rows)], out_refs[j]))
    wait(stores)


def feed_scratch(count, width, wide, hidden, pairs):
    return [
        pltpu.VMEM((wide, width), bf16),
        pltpu.VMEM((hidden, width), bf16),
        pltpu.VMEM((hidden, width), bf16),
        pltpu.VMEM((count, width), bf16),
        pltpu.VMEM((count, width), bf16),
        pltpu.VMEM((count, hidden), bf16),
        pltpu.VMEM((count, width), f32),
        pltpu.VMEM((count, width), bf16),
        pltpu.VMEM((count, width), f32),
        pltpu.SemaphoreType.DMA((16 * pairs + 8,)),
    ]


def feed_sizes(x, mixed, up_bias):
    count, width = x.shape
    pairs = mixed.shape[0]
    return count, width, pairs, pairs * PAIR, up_bias.shape[1]


def feed(x, mixed, tables, vectors, up_bias, rank, blocks):
    o_table, (arrays, pieces) = tables
    count, width, pairs, wide, hidden = feed_sizes(x, mixed, up_bias)
    square = struct((count, width), bf16)
    column = struct((count, 1), f32)
    parts = max(blocks, 1)
    out, kept = [], []
    found = call(
        functools.partial(feed_kernel, (o_table[1], pieces), len(arrays), blocks),
        [IN_VMEM, IN_VMEM, IN_HBM, IN_VMEM, IN_VMEM, IN_SMEM] + [IN_HBM] * len(arrays),
        [IN_HBM] * parts + [IN_HBM, IN_VMEM, IN_HBM, IN_VMEM, IN_HBM],
        [struct((count // parts, width), bf16)] * parts
        + [square, column, square, column, struct((count, hidden), bf16)],
        scratch=feed_scratch(count, width, wide, hidden, pairs),
        flops=2 * count * width * (wide + 2 * hidden),
        moved=2 * (2 * hidden * width + 12 * count * width),
        exps=2 * count * hidden,
    )(x, mixed, o_table[0], vectors, up_bias, rank, *arrays)
    return (found[:blocks] if blocks else found[0], *found[parts:])


def summed(own, got, part):
    columns = []
    for pair in range(own.shape[1]):
        column = own[part, pair].astype(f32)
        for i in range(got.shape[0]):
            column += got[i, part, pair].astype(f32)
        columns.append(column.astype(bf16))
    return jnp.concatenate(columns, axis=1)


def project_back(first_ref, dq_ref, own_ref, got_ref, weight, loads):
    pairs = dq_ref.shape[0]
    wide = pairs * PAIR
    total = first_ref[...].astype(f32)
    for part in range(3):
        if part == 0:
            left = jnp.concatenate([dq_ref[pair] for pair in range(pairs)], axis=1)
        else:
            left = summed(own_ref, got_ref, part - 1)
        wait(loads[part])
        total += dot_nn(left, weight[part * wide : (part + 1) * wide])
    return total


def leave_kernel(p_first, extra, first_ref, dq_ref, own_ref, got_ref, pw_ref, rank_ref, *rest):
    if extra:
        prefix_ref, *rest = rest
    (*out_refs, weight_p, low, semaphores) = rest
    copies = Copies(semaphores)
    loads = load_heads(copies, pw_ref, p_first, 3, dq_ref.shape[0], weight_p)
    low[...] = project_back(first_ref, dq_ref, own_ref, got_ref, weight_p, loads).astype(bf16)
    rows = low.shape[0] // len(out_refs)
    for j, target in enumerate(out_refs):
        start = pl.multiple_of((rank_ref[0] ^ j) * rows, rows)
        target[:rows] = low[pl.ds(start, rows)]
        if extra:
            value = prefix_ref[rank_ref[0] ^ j].astype(bf16)
            for column in range(value.shape[0] // 16):
                span = slice(column * PAIR, (column + 1) * PAIR)
                target[rows:, span] = value[column * 16 : (column + 1) * 16]


def leave(first, dq, own, got, p_table, rank, blocks, prefix=None):
    count, width = first.shape
    pairs = dq.shape[0]
    more = [] if prefix is None else [prefix]
    return call(
        functools.partial(leave_kernel, p_table[1], len(more)),
        [IN_VMEM] * 4 + [IN_HBM, IN_SMEM] + [IN_VMEM] * len(more),
        [IN_VMEM] * blocks,
        [struct((count // blocks + 16 * len(more), width), bf16)] * blocks,
        scratch=[
            pltpu.VMEM((3 * pairs * PAIR, width), bf16),
            pltpu.VMEM((count, width), bf16),
            pltpu.SemaphoreType.DMA((6 * pairs,)),
        ],
        flops=2 * count * width * 3 * PAIR * pairs,
        moved=2 * (count * width * 7 + 3 * width * PAIR * pairs),
    )(first, dq, own, got, p_table[0][0], rank, *more)


def attend_kernel(
    prefix_count, q_ref, own_ref, other_ref, pk_ref, pv_ref, sq_ref, sk_ref,
    mixed_ref, raised_ref, inverse_ref, bias_ref,
):
    pad = pk_ref.shape[1]
    others = other_ref.shape[0]

    @pl.when(pl.program_id(0) == 0)
    def _():
        row = lax.broadcasted_iota(jnp.int32, (pad, bias_ref.shape[1]), 0)
        bias_ref[:pad] = jnp.where(row < prefix_count, 0.0, MASKED)
        keys = jnp.broadcast_to(sk_ref[...], (8, sk_ref.shape[1])).T[:, :1]
        same = (keys == sq_ref[...]) & (keys >= 0)
        bias_ref[pad:] = jnp.where(same, 0.0, MASKED)

    keys = jnp.concatenate(
        [pk_ref[0], own_ref[0, 0]] + [other_ref[i, 0, 0] for i in range(others)], axis=0
    )
    values = jnp.concatenate(
        [pv_ref[0], own_ref[1, 0]] + [other_ref[i, 1, 0] for i in range(others)], axis=0
    )
    queries = q_ref[0]
    lane = lax.broadcasted_iota(jnp.int32, queries.shape, 1)
    value_lane = lax.broadcasted_iota(jnp.int32, values.shape, 1)
    parts = []
    inverses = []
    count = queries.shape[0]
    score = lambda head: dot_nt(
        keys, jnp.where((lane // HEAD) == head, queries, bf16(0))
    ) + bias_ref[...]
    ahead = score(0)
    for head in range(2):
        scores = ahead
        if head == 0:
            ahead = score(1)
        raised = jnp.exp(scores - jnp.max(scores, axis=0, keepdims=True))
        low = raised.astype(bf16)
        raised_ref[0, head] = low
        ones = jnp.where((value_lane // HEAD) == head, values, bf16(1))
        out = dot_tn(ones, low)
        inverse = 1.0 / out[(1 - head) * HEAD : (1 - head) * HEAD + 1]
        out = out[head * HEAD : (head + 1) * HEAD]
        parts.append(out * inverse)
        inverses.append(jnp.broadcast_to(inverse, out.shape))
    mixed_ref[0] = jnp.concatenate(parts, axis=0).T.astype(bf16)
    inverse_ref[0] = jnp.concatenate(inverses, axis=0).T.astype(bf16)


def attend(q, own, other, pk, pv, prefix_count, seg_q, seg_k):
    pairs, count, _ = q.shape
    others = other.shape[0]
    pad = pk.shape[1]
    total = pad + count * (others + 1)
    by_pair = pl.BlockSpec((1, count, PAIR), lambda i: (i, 0, 0))
    by_prefix = pl.BlockSpec((1, pad, PAIR), lambda i: (i, 0, 0))
    return call(
        functools.partial(attend_kernel, prefix_count),
        [
            by_pair,
            pl.BlockSpec((2, 1, count, PAIR), lambda i: (0, i, 0, 0)),
            pl.BlockSpec((others, 2, 1, count, PAIR), lambda i: (0, 0, i, 0, 0)),
            by_prefix,
            by_prefix,
            whole((1, count)),
            whole((1, total - pad)),
        ],
        [
            by_pair,
            pl.BlockSpec((1, 2, total, count), lambda i: (i, 0, 0, 0)),
            by_pair,
        ],
        [
            struct((pairs, count, PAIR), bf16),
            struct((pairs, 2, total, count), bf16),
            struct((pairs, count, PAIR), bf16),
        ],
        scratch=[pltpu.VMEM((total, count), f32)],
        grid=(pairs,),
        flops=8 * total * count * PAIR * pairs,
        moved=4 * pairs * total * count,
        exps=2 * pairs * total * count,
    )(q, own, other, pk, pv, seg_q, seg_k)


def attention_back(d_out, mixed, inverse, raised, queries, keys, values):
    lane = lax.broadcasted_iota(jnp.int32, queries.shape, 1)
    scaled = d_out.astype(f32) * inverse.astype(f32)
    products = (scaled * mixed.astype(f32)).T
    scaled = scaled.astype(bf16)
    d_keys = jnp.zeros(keys.shape, f32)
    d_values = jnp.zeros(keys.shape, f32)
    parts = []
    for head in range(2):
        chosen = (lane // HEAD) == head
        span = slice(head * HEAD, (head + 1) * HEAD)
        delta = jnp.sum(products[span], axis=0, keepdims=True)
        here = jnp.where(chosen, scaled, bf16(0))
        low = raised(head)
        d_score = (low.astype(f32) * (dot_nt(values, here) - delta)).astype(bf16)
        d_values += dot_nn(low, here)
        d_keys += dot_nn(d_score, jnp.where(chosen, queries, bf16(0)))
        parts.append(dot_tn(keys, d_score)[span])
    return jnp.concatenate(parts, axis=0).T * (1.0 / math.sqrt(HEAD)), d_keys, d_values


def back_kernel(p_first, p_sources, o_first, pieces, sources, place_ref, *rest):
    if p_first is None:
        grad_ref, *rest = rest
    else:
        first1_ref, dq_in, own_in, got_in, *rest = rest
        pw_refs, rest = rest[:p_sources], rest[p_sources:]
    (ow_ref, vec_ref, z1_ref, r1_ref, z2_ref, r2_ref, slope_ref,
     mixed_ref, inverse_ref, raised_ref, q_ref, own_ref, other_ref, pk_ref, pv_ref, *rest) = rest
    h_refs, rest = rest[:sources], rest[sources:]
    outs, rest = rest[:5], rest[5:]
    (weight_o, weight_u, weight_d, unit_in, slope, low, acc, first, dq, down, dother, prefix,
     mixed, inverse, raised, queries, own, other, semaphores, turns, stores, *weight_p) = rest
    copies = Copies(semaphores)
    pairs, count, _ = dq.shape
    others = dother.shape[0]
    pad = pk_ref.shape[1]
    weights = Hidden(copies, h_refs, pieces, weight_u, weight_d)
    groups = weights.groups
    slopes = []

    def fetch(group):
        weights.fetch(group)
        span = (slice(None), pl.ds(group * GROUP, GROUP))
        slopes.append(copies.start(slope_ref.at[span], slope.at[span]))

    if p_first is None:
        load = copies.start(grad_ref, low)
        load_z2 = copies.start(z2_ref, unit_in)
        fetch(0)
        load.wait()
        grad = low[...].astype(f32)
    else:
        load_q = copies.start(dq_in, dq)
        loads_p = load_projection(copies, pw_refs, p_first, pairs, weight_p[0], place_ref)
        loads = [copies.start(own_in, down), copies.start(got_in, dother)]
        load_first = copies.start(first1_ref, first)
        load_z2 = copies.start(z2_ref, unit_in)
        fetch(0)
        wide = pairs * PAIR
        load_q.wait()
        wait(loads_p[0])
        left = jnp.concatenate([dq[pair] for pair in range(pairs)], axis=1)
        total = dot_nn(left, weight_p[0][:wide])
        wait(loads)
        for part in (1, 2):
            wait(loads_p[part])
            total += dot_nn(
                summed(down, dother, part - 1), weight_p[0][part * wide : (part + 1) * wide]
            )
        load_first.wait()
        grad = (total + first[...].astype(f32)).astype(bf16).astype(f32)
    load_z2.wait()
    acc[...] = unit_back(grad, unit_in[...].astype(f32), r2_ref[...], vec_ref[3:4])
    low[...] = acc[...].astype(bf16)
    load_z1 = copies.start(z1_ref, unit_in)
    loads_o = load_heads(copies, ow_ref, o_first, 1, pairs, weight_o)[0]

    def turn(pair, slot):
        moves = (
            (raised_ref.at[pair], raised.at[slot]),
            (q_ref.at[pair], queries.at[slot]),
            (mixed_ref.at[pair], mixed.at[slot]),
            (inverse_ref.at[pair], inverse.at[slot]),
            (own_ref.at[:, pair], own.at[slot]),
            (other_ref.at[:, :, pair], other.at[slot]),
        )
        return [
            pltpu.make_async_copy(source, target, turns.at[slot, i])
            for i, (source, target) in enumerate(moves)
        ]

    for group in range(groups):
        if group + 1 < groups:
            fetch(group + 1)
        if group == groups - 1:
            for pair in range(2):
                for copy in turn(pair, pair):
                    copy.start()
        slopes[group].wait()
        weights.wait(group, 0)
        weights.wait(group, 1)
        span = slice(group * GROUP, (group + 1) * GROUP)
        d_act = dot_nt(low[...], weight_d[span])
        d_pre = (d_act * slope[:, span].astype(f32)).astype(bf16)
        acc[...] += dot_nn(d_pre, weight_u[span])
    load_z1.wait()
    d_first = unit_back(acc[...], unit_in[...].astype(f32), r1_ref[...], vec_ref[2:3])
    first[...] = d_first.astype(bf16)
    store_first = copies.start(first, outs[0])
    wait(loads_o)
    low[...] = dot_nt(d_first.astype(bf16), weight_o[...]).astype(bf16)

    def save(pair):
        moves = (
            (dq.at[pair], outs[1].at[pair]),
            (down.at[:, pair], outs[2].at[:, pair]),
            (dother.at[:, :, pair], outs[3].at[:, :, pair]),
            (prefix.at[pair], outs[4].at[pair]),
        )
        return [
            pltpu.make_async_copy(source, target, stores.at[pair, i])
            for i, (source, target) in enumerate(moves)
        ]

    def step(pair, carry):
        slot = lax.rem(pair, 2)
        for copy in turn(pair, slot):
            copy.wait()
        keys = jnp.concatenate(
            [pk_ref[pair], own[slot, 0]] + [other[slot, i, 0] for i in range(others)], axis=0
        )
        values = jnp.concatenate(
            [pv_ref[pair], own[slot, 1]] + [other[slot, i, 1] for i in range(others)], axis=0
        )
        d_query, d_keys, d_values = attention_back(
            low[:, pl.ds(pl.multiple_of(pair * PAIR, PAIR), PAIR)],
            mixed[slot],
            inverse[slot],
            lambda head: raised[slot, head],
            queries[slot],
            keys,
            values,
        )
        dq[pair] = d_query.astype(bf16)
        prefix[pair, :pad] = d_keys[:pad]
        prefix[pair, pad:] = d_values[:pad]
        for part, d_part in enumerate((d_keys, d_values)):
            down[part, pair] = d_part[pad : pad + count].astype(bf16)
            for i in range(others):
                start = pad + (i + 1) * count
                dother[i, part, pair] = d_part[start : start + count].astype(bf16)
        for copy in save(pair):
            copy.start()

        @pl.when(pair + 2 < pairs)
        def _():
            for copy in turn(pair + 2, slot):
                copy.start()

        return carry

    lax.fori_loop(0, pairs, step, 0)
    store_first.wait()
    for pair in range(pairs):
        for copy in save(pair):
            copy.wait()


def backward(grads, p_table, tables, vectors, kept, attention, place):
    o_table, (arrays, pieces) = tables
    mixed, inverse, raised, q, own, other, pk, pv = attention
    pairs, count, _ = q.shape
    width = o_table[0].shape[-1]
    wide = pairs * PAIR
    total = raised.shape[2]
    pad = pk.shape[1]
    slope = kept[-1]
    hidden = slope.shape[1]
    more, p_first = ([], None) if p_table is None else p_table
    vm = pltpu.VMEM
    return call(
        functools.partial(
            back_kernel, p_first, len(more), o_table[1], pieces, len(arrays)
        ),
        [IN_SMEM] + [IN_HBM] * (len(grads) + len(more))
        + [IN_HBM, IN_VMEM, IN_HBM, IN_VMEM, IN_HBM, IN_VMEM, IN_HBM]
        + [IN_HBM] * 6 + [IN_VMEM] * 2
        + [IN_HBM] * len(arrays),
        [IN_HBM] * 5,
        [
            struct((count, width), bf16),
            struct(q.shape, bf16),
            struct(own.shape, bf16),
            struct(other.shape, bf16),
            struct((pairs, 2 * pad, PAIR), f32),
        ],
        scratch=[
            vm((wide, width), bf16),
            vm((hidden, width), bf16),
            vm((hidden, width), bf16),
            vm((count, width), bf16),
            vm((count, hidden), bf16),
            vm((count, width), bf16),
            vm((count, width), f32),
            vm((count, width), bf16),
            vm(q.shape, bf16),
            vm(own.shape, bf16),
            vm(other.shape, bf16),
            vm((pairs, 2 * pad, PAIR), f32),
            vm((2, count, PAIR), bf16),
            vm((2, count, PAIR), bf16),
            vm((2, 2, total, count), bf16),
            vm((2, count, PAIR), bf16),
            vm((2, 2, count, PAIR), bf16),
            vm((2, other.shape[0], 2, count, PAIR), bf16),
            pltpu.SemaphoreType.DMA((22 * pairs + 16,)),
            pltpu.SemaphoreType.DMA((2, 6)),
            pltpu.SemaphoreType.DMA((pairs, 4)),
        ]
        + [vm((3 * wide, width), bf16)] * (p_table is not None),
        flops=2 * count * width * (4 * wide + 2 * hidden) + 16 * total * count * PAIR * pairs,
        moved=2 * (2 * hidden * width + 4 * wide * width + 16 * count * width) + 4 * pairs * total * count,
    )(place, *grads, *more, o_table[0], vectors, *kept, *attention, *arrays)


def per_device(
    boundary, segment_ids, project_weight, project_bias, output_weight, output_biases,
    norm_gains, norm_shifts, up_weight, up_bias, down_weight, prefix_keys, prefix_values,
):
    section = lax.axis_index("section")
    rank = lax.axis_index("tensor")
    ranks = lax.axis_size("tensor")
    is_first = section == 0
    micro, slots, rows, width = boundary.shape[1:]
    length = slots * ranks
    row_count = micro * rows
    chips = ranks // row_count
    blocks = SECTIONS * chips
    count = length // blocks
    place = rank % chips
    swap = [(0, 1), (1, 0)]
    after = lambda value, *first: lax.optimization_barrier((value, *first))[0]
    heads_all = project_weight.shape[3] * ranks
    pairs = heads_all // PAIR
    shards = ranks // pairs
    prefix_count = prefix_keys.shape[1]
    pad = -(-prefix_count // 32) * 32
    low_width = project_weight.shape[3] // 2
    hidden = up_weight.shape[2] // 2

    quick = chips == 1 and ranks == 8 and lax.axis_size("dp") == 2

    half_ranks = ranks // 2
    low_rank = rank % half_ranks
    block = section * chips + place
    by_row = jnp.transpose(boundary[0], (0, 2, 1, 3)).reshape(row_count, slots, width)

    def ordered(parts):
        bit = 1
        while bit < len(parts):
            flip = (rank & bit) != 0
            parts = [jnp.where(flip, parts[i ^ bit], part) for i, part in enumerate(parts)]
            bit *= 2
        return parts

    if quick:
        lower, upper = by_row[:half_ranks], by_row[half_ranks:]
        keep = jnp.where(is_first, lower, upper)
        got = lax.ppermute(jnp.where(is_first, upper, lower), "section", swap)

        def arrive(rows_here):
            parts = []
            for j in range(half_ranks):
                route = [
                    (s * ranks + t, (t // half_ranks) * ranks + half_ranks * s + ((t % half_ranks) ^ j))
                    for s in range(SECTIONS)
                    for t in range(ranks)
                ]
                part = lax.dynamic_index_in_dim(rows_here, low_rank ^ j, 0, keepdims=False)
                parts.append(lax.ppermute(part, ("section", "tensor"), route))
            return jnp.concatenate(ordered(parts), axis=0)

        tokens = arrive(jnp.where(is_first, keep, got))
        cotangent_rows = jnp.where(is_first, got, keep)
    else:
        if chips > 1:
            by_row = jnp.repeat(by_row, chips, axis=0)
        row = lax.all_to_all(by_row, "tensor", 0, 0, tiled=True).reshape(length, width)
        other_block = (1 - section) * chips + place
        mine = lax.dynamic_slice_in_dim(row, block * count, count, 0)
        theirs = lax.dynamic_slice_in_dim(row, other_block * count, count, 0)
        got = lax.ppermute(theirs, "section", swap)
        tokens = jnp.where(is_first, mine, got)
        cotangent = jnp.where(is_first, got, mine)

    own_vectors = jnp.concatenate(
        [output_biases[0], norm_gains[0], norm_shifts[0], norm_shifts[0]], axis=0
    )
    got_vectors = lax.ppermute(own_vectors, "section", swap)
    vectors = [
        jnp.where(is_first, own_vectors, got_vectors).astype(f32),
        jnp.where(is_first, got_vectors, own_vectors).astype(f32),
    ]

    segments = lax.dynamic_index_in_dim(
        segment_ids.reshape(row_count, length), rank // chips, 0, keepdims=False
    )
    seg_q = lax.dynamic_slice_in_dim(segments, block * count, count, 0)
    seg_k = jnp.concatenate(
        [
            lax.dynamic_slice_in_dim(segments, (block ^ distance) * count, count, 0)
            for distance in range(blocks)
        ]
    )[None, :]
    seg_q = seg_q[None, :]

    project_rows = jnp.transpose(project_weight[0], (1, 2, 0)).reshape(3, 2, low_width, width)
    project_rows = jnp.transpose(project_rows, (1, 0, 2, 3)).reshape(2, 3 * low_width, width)
    out_rows = output_weight[0].reshape(2, low_width, width)
    up_rows = jnp.transpose(up_weight[0], (1, 0)).reshape(2, hidden, width)
    down_rows = down_weight[0].reshape(2, hidden, width)
    small = jnp.concatenate(
        [
            jnp.transpose(project_bias[0].reshape(3, 2, low_width), (1, 0, 2)).reshape(2, -1),
            up_bias[0].reshape(2, hidden),
            jnp.transpose(prefix_keys[0].reshape(-1, 2, low_width), (1, 0, 2)).reshape(2, -1),
            jnp.transpose(prefix_values[0].reshape(-1, 2, low_width), (1, 0, 2)).reshape(2, -1),
        ],
        axis=1,
    )
    small_size = small.shape[1]
    small_rows = -(-small_size // (16 * width)) * 16
    small = jnp.pad(small, ((0, 0), (0, small_rows * width - small_size)))
    small = small.reshape(2, small_rows, width)
    if quick:
        keep, give = pack(
            jnp.transpose(project_weight[0], (1, 0, 2)), output_weight[0], up_weight[0],
            down_weight[0], small, section.astype(jnp.int32).reshape(1),
        )
    else:
        packed = jnp.concatenate([project_rows, out_rows, up_rows, down_rows, small], axis=1)
        keep = lax.dynamic_index_in_dim(packed, section, 0, keepdims=False)
        give = lax.dynamic_index_in_dim(packed, 1 - section, 0, keepdims=False)
    got = lax.ppermute(give, "section", swap)
    layer_rows = [jnp.where(is_first, keep, got), jnp.where(is_first, got, keep)]
    sizes = [3 * low_width, low_width, hidden, hidden, small_rows]
    p_end, o_end, u_end, d_end, s_end = [sum(sizes[: i + 1]) for i in range(len(sizes))]
    plane = lax.axis_index("dp")
    gather = lambda parts: lax.all_gather(
        jnp.concatenate(parts, axis=0), ("section", "tensor"), axis=0
    ).reshape(2, ranks, -1, width)

    def unpack(flat):
        cut = 0
        found = []
        for groups, size in ((3, low_width), (1, hidden), (prefix_count, low_width), (prefix_count, low_width)):
            part = flat[:, :, cut : cut + groups * size].reshape(2, pairs, shards, groups, size)
            cut += groups * size
            if shards == 1:
                part = part[:, :, 0]
            else:
                part = jnp.transpose(part, (2, 1, 3, 0, 4)).reshape(2, pairs, groups, 2 * size)
            found.append(part)
        p_bias = jnp.transpose(found[0], (2, 1, 0, 3)).reshape(3, 1, heads_all).astype(f32)
        prefix = [
            jnp.pad(
                jnp.transpose(part, (1, 2, 0, 3)).reshape(pairs, prefix_count, PAIR),
                ((0, 0), (0, pad - prefix_count), (0, 0)),
            )
            for part in found[2:]
        ]
        return p_bias, found[1][:, :, 0], prefix[0], prefix[1]

    tables = []
    smalls = []
    plane = lax.axis_index("dp")
    share = 3 * low_width // 2
    if quick:
        projection = lax.dynamic_slice_in_dim(layer_rows[1][:p_end], plane * share, share, 0)
    else:
        projection = layer_rows[1][:p_end]
    early_rows = [layer_rows[0][:d_end], projection, layer_rows[0][d_end:], layer_rows[1][d_end:]]
    projection_rows = projection.shape[0]
    late_rows = layer_rows[1][p_end:d_end]
    early = gather(early_rows)
    early, vectors[0], vectors[1], seg_q, seg_k, tokens = lax.optimization_barrier(
        (early, vectors[0], vectors[1], seg_q, seg_k, tokens)
    )
    late = gather([after(late_rows, early)])
    def table(array, first, size, groups=1):
        if shards == 1:
            return (array, first, size)
        part = array[:, :, first : first + size].reshape(
            2, pairs, shards, groups, size // groups, width
        )
        part = jnp.transpose(part, (2, 1, 3, 0, 4, 5))
        return (part.reshape(2, pairs, 2 * size, width), 0, 2 * size)

    def projection_table(layer):
        if quick and layer:
            return None
        array, first, _ = table(early, layer * d_end, 3 * low_width, 3)
        return (array,), first

    for layer in range(2):
        source, shift = (late, -p_end) if layer else (early, 0)
        up, u_first, rows_here = table(source, shift + o_end, 2 * hidden, 2)
        rows_here //= 2
        pieces = tuple(
            (0, (s, t), u_first, u_first + rows_here, rows_here)
            for s in range(2)
            for t in range(pairs)
        )
        tables.append(
            (
                projection_table(layer),
                table(source, shift + p_end, low_width),
                ((up,), pieces),
            )
        )
        start = d_end + projection_rows + layer * small_rows
        p_bias, u_bias, pk, pv = unpack(
            early[:, :, start : start + small_rows].reshape(2, ranks, -1)
        )
        smalls.append((p_bias, u_bias.reshape(1, -1).astype(f32), pk, pv))

    def flips():
        routes = []
        for distance in range(1, blocks):
            route = []
            for s in range(SECTIONS):
                for t in range(ranks):
                    index = (s * chips + t % chips) ^ distance
                    route.append(
                        (s * ranks + t, (index // chips) * ranks + t // chips * chips + index % chips)
                    )
            routes.append(route)
        return routes

    routes = flips()

    def exchange(parts):
        return jnp.stack(
            [
                lax.ppermute(part, ("section", "tensor"), route) if chips > 1
                else lax.ppermute(part, "section", swap)
                for part, route in zip(parts, routes)
            ]
        )

    out_blocks = half_ranks if quick else 1
    order = (low_rank if quick else 0 * rank).astype(jnp.int32).reshape(1)
    place_here = jnp.stack([plane, section]).astype(jnp.int32)
    p_tables = []
    saved = []
    x = tokens
    for layer in range(2):
        p_table, *others = tables[layer]
        p_bias, u_bias, pk, pv = smalls[layer]
        if quick and layer == 0:
            cross = lax.dynamic_index_in_dim(
                early[:, :, d_end : d_end + share], section, 0, keepdims=False
            )
            theirs = lax.ppermute(cross, "dp", swap)
        if quick and layer == 1:
            p_table = ((early, theirs, theirs_too), d_end)
        p_tables.append(p_table)
        q, own = project(x, p_table, p_bias, place_here)
        other = exchange([own] * (blocks - 1))
        mixed, raised, inverse = attend(q, own, other, pk, pv, prefix_count, seg_q, seg_k)
        saved.append((mixed, inverse, raised, q, own, other, pk, pv))
        if layer == 1 and quick:
            cotangent = arrive(after(cotangent_rows, late))
        x, *kept = feed(
            x, mixed, others, vectors[layer], u_bias, order, out_blocks if layer else 0
        )
        saved[-1] += (kept,)
        if layer == 0 and quick:
            theirs, x = lax.optimization_barrier((theirs, x))
            theirs_too = lax.ppermute(theirs, "section", swap)
    outs = x
    kept_0, kept_1 = (entry[-1] for entry in saved)
    saved = [entry[:-1] for entry in saved]
    first, dq, down, dother, prefix_1 = backward(
        (cotangent,), None, tables[1][1:], vectors[1], kept_1, saved[1], place_here
    )

    def send_blocks(parts):
        got = []
        for j, part in enumerate(parts):
            route = [
                (s * ranks + t, (t // half_ranks) * ranks + half_ranks * s + ((t % half_ranks) ^ j))
                for s in range(SECTIONS)
                for t in range(ranks)
            ]
            got.append(lax.ppermute(part, ("section", "tensor"), route))
        return got

    if quick:
        dother, *outs = lax.optimization_barrier((dother, *outs))
        outs = send_blocks(outs)
    got = exchange([dother[i] for i in range(blocks - 1)])
    first, dq, down, dother, prefix_0 = backward(
        (first, dq, down, got), p_tables[1], tables[0][1:], vectors[0], kept_0, saved[0], place_here
    )
    if quick:
        dother, *outs = lax.optimization_barrier((dother, *outs))
    got = exchange([dother[i] for i in range(blocks - 1)])
    if quick:
        prefix = jnp.stack([prefix_0, prefix_1], axis=1)
        lower, upper = prefix[: pairs // 2], prefix[pairs // 2 :]
        other = lax.ppermute(jnp.where(is_first, upper, lower), "section", swap)
        prefix = jnp.where(is_first, lower, upper) + other
        prefix = prefix.reshape(half_ranks, 4 * pad, PAIR)
    else:
        prefix = None
    grads = leave(first, dq, down, got, tables[0][0], order, out_blocks, prefix)

    if quick:
        grads = send_blocks(grads)
        partial = sum(part[slots:].astype(f32) for part in grads)
        grads = jnp.stack(ordered([part[:slots] for part in grads]))
        outs = jnp.stack(ordered(outs))
        keep = jnp.where(is_first, grads, outs)
        got = lax.ppermute(jnp.where(is_first, outs, grads), "section", swap)
        partial += lax.ppermute(partial, "dp", swap)
        partial = jnp.transpose(partial.reshape(16, -1, PAIR), (1, 0, 2)).reshape(2, 2 * pad, PAIR)
        prefix = jnp.where(is_first, partial[0], partial[1]) + lax.ppermute(
            jnp.where(is_first, partial[1], partial[0]), "section", swap
        )
        back = jnp.concatenate(
            [jnp.where(is_first, keep, got), jnp.where(is_first, got, keep)], axis=0
        )
    else:
        keep = jnp.where(is_first, grads[0], outs[0])
        got = lax.ppermute(jnp.where(is_first, outs[0], grads[0]), "section", swap)
        row = jnp.zeros((length, width), bf16)
        row = lax.dynamic_update_slice_in_dim(
            row, jnp.where(is_first, keep, got), place * count, 0
        )
        row = lax.dynamic_update_slice_in_dim(
            row, jnp.where(is_first, got, keep), (chips + place) * count, 0
        )
        back = lax.all_to_all(row.reshape(ranks, slots, width), "tensor", 0, 0, tiled=True)
        back = jnp.sum(back.reshape(row_count, chips, slots, width), axis=1)
    result = jnp.transpose(back.reshape(micro, rows, slots, width), (0, 2, 1, 3))[None]

    if quick:
        both = prefix.reshape(2, pad, PAIR)[:, :prefix_count]
    else:
        both = jnp.where(
            is_first,
            lax.psum(prefix_0, ("section", "dp", "tensor")),
            lax.psum(prefix_1, ("section", "dp", "tensor")),
        )
        both = both.reshape(pairs, 2, pad, PAIR)[:, :, :prefix_count]
        both = jnp.transpose(both, (1, 2, 0, 3)).reshape(2, prefix_count, heads_all)
        share = heads_all // ranks
        both = lax.dynamic_slice_in_dim(both, rank * share, share, 2)
    return (result, both[0][None], both[1][None])


def solution(mesh):
    in_specs = (
        P("section", None, "tensor", "dp", None),
        P(None, "dp", None),
        P("section", None, None, "tensor"),
        P("section", None, "tensor"),
        P("section", "tensor", None),
        P("section", None, None),
        P("section", None, None),
        P("section", None, None),
        P("section", None, "tensor"),
        P("section", "tensor"),
        P("section", "tensor", None),
        P("section", None, "tensor"),
        P("section", None, "tensor"),
    )
    out_specs = (
        P("section", None, "tensor", "dp", None),
        P("section", None, "tensor"),
        P("section", None, "tensor"),
    )
    return jax.shard_map(
        per_device, mesh=mesh, in_specs=in_specs, out_specs=out_specs, check_vma=False
    )
```

```python
import functools
import math

import jax
import jax.numpy as jnp
from jax import lax
from jax.experimental import pallas as pl
from jax.experimental.pallas import tpu as pltpu
from jax.sharding import PartitionSpec as P

HEAD = 64
PAIR = 2 * HEAD
EPSILON = 1e-05
MASKED = -1000000000.0
VMEM = 60 * 1024 * 1024
SECTIONS = 2

bf16 = jnp.bfloat16
f32 = jnp.float32


def dot_nn(left, right):
    return lax.dot_general(left, right, (((1,), (0,)), ((), ())), preferred_element_type=f32)


def dot_nt(left, right):
    return lax.dot_general(left, right, (((1,), (1,)), ((), ())), preferred_element_type=f32)


def dot_tn(left, right):
    return lax.dot_general(left, right, (((0,), (0,)), ((), ())), preferred_element_type=f32)


def unit(hidden):
    average = jnp.mean(hidden, axis=-1, keepdims=True)
    centered = hidden - average
    variance = jnp.mean(centered * centered, axis=-1, keepdims=True)
    inverse = lax.rsqrt(variance + EPSILON)
    return centered * inverse, inverse


def unit_back(grad, normed, inverse, gain):
    scaled = grad * gain
    return inverse * (
        scaled
        - jnp.mean(scaled, axis=-1, keepdims=True)
        - normed * jnp.mean(scaled * normed, axis=-1, keepdims=True)
    )


GROUP = 1024


class Copies:
    def __init__(self, semaphores):
        self.semaphores = semaphores
        self.used = 0

    def start(self, source, target):
        copy = pltpu.make_async_copy(source, target, self.semaphores.at[self.used])
        self.used += 1
        copy.start()
        return copy


def wait(copies):
    for copy in copies:
        copy.wait()


def call(kernel, in_specs, out_specs, out_shape, scratch=(), grid=None, flops=0, moved=0, exps=0, vmem=VMEM):
    more = {} if grid is None else {"grid": grid}
    return pl.pallas_call(
        kernel,
        in_specs=in_specs,
        out_specs=out_specs,
        out_shape=out_shape,
        scratch_shapes=list(scratch),
        compiler_params=pltpu.CompilerParams(vmem_limit_bytes=vmem),
        cost_estimate=pl.CostEstimate(flops=flops, bytes_accessed=moved, transcendentals=exps),
        **more,
    )


IN_VMEM = pl.BlockSpec(memory_space=pltpu.VMEM)
IN_HBM = pl.BlockSpec(memory_space=pltpu.HBM)
IN_ANY = pl.BlockSpec(memory_space=pl.ANY)
IN_SMEM = pl.BlockSpec(memory_space=pltpu.SMEM)


def whole(shape):
    return pl.BlockSpec(shape, lambda i: (0,) * len(shape))


def struct(shape, dtype):
    return jax.ShapeDtypeStruct(shape, dtype)


def pack_kernel(p_ref, o_ref, u_ref, d_ref, section_ref, keep_ref, give_ref, stage, semaphores):
    copies = Copies(semaphores)
    place = 0
    sources = [(p_ref[part].T, HEAD) for part in range(3)]
    sources += [(o_ref[...], HEAD), (u_ref[...].T, u_ref.shape[1] // 2), (d_ref[...], d_ref.shape[0] // 2)]
    for value, rows in sources:
        for half in range(2):
            stage[half, place : place + rows] = value[half * rows : (half + 1) * rows]
        place += rows
    section = section_ref[0]
    wait([copies.start(stage.at[1 - section], give_ref), copies.start(stage.at[section], keep_ref)])


def pack(project_w, out_w, up_w, down_w, section):
    width = down_w.shape[1]
    rows = (project_w.shape[2] * 3 + out_w.shape[0] + up_w.shape[1] + down_w.shape[0]) // 2
    return call(
        pack_kernel,
        [IN_VMEM] * 4 + [IN_SMEM],
        [IN_HBM] * 2,
        [struct((rows, width), bf16)] * 2,
        scratch=[pltpu.VMEM((2, rows, width), bf16), pltpu.SemaphoreType.DMA((2,))],
        moved=8 * rows * width,
    )(project_w, out_w, up_w, down_w, section)


def load_heads(copies, ref, first, parts, pairs, target):
    started = []
    for part in range(parts):
        started.append([])
        for pair in range(pairs):
            for half in range(2):
                place = (part * pairs + pair) * PAIR + half * HEAD
                started[-1].append(
                    copies.start(
                        ref.at[half, pair, pl.ds(first + part * HEAD, HEAD)],
                        target.at[pl.ds(place, HEAD)],
                    )
                )
    return started


def load_projection(copies, refs, first, pairs, target, place_ref):
    if len(refs) == 1:
        return load_heads(copies, refs[0], first, 3, pairs, target)
    started = []
    unit_rows = HEAD // 2
    for index, ref in enumerate(refs):
        plane = place_ref[0] if index == 0 else 1 - place_ref[0]
        for half in range(2 if index == 0 else 1):
            here = (half, place_ref[1], 1 - place_ref[1])[index]
            for pair in range(pairs):
                for unit_index in range(3):
                    place = 3 * plane + unit_index
                    row = (place // 2) * pairs * PAIR + (place % 2) * unit_rows
                    row = pl.multiple_of(row + pair * PAIR + here * HEAD, unit_rows)
                    cut = pl.ds((first if index == 0 else 0) + unit_index * unit_rows, unit_rows)
                    started.append(
                        copies.start(
                            ref.at[half, pair, cut] if index == 0 else ref.at[pair, cut],
                            target.at[pl.ds(row, unit_rows)],
                        )
                    )
    return [started, [], []]


class Hidden:
    def __init__(self, copies, refs, pieces, up, down):
        self.copies, self.refs, self.pieces = copies, refs, pieces
        self.targets = (up, down)
        self.groups = up.shape[0] // GROUP
        self.started = 0
        self.loads = ([], [])

    def fetch(self, group):
        end = (group + 1) * GROUP
        place = sum(piece[4] for piece in self.pieces[: self.started])
        while self.started < len(self.pieces) and place < end:
            index, lead, *firsts, rows = self.pieces[self.started]
            for kind in range(2):
                copy = self.copies.start(
                    self.refs[index].at[(*lead, pl.ds(firsts[kind], rows))],
                    self.targets[kind].at[pl.ds(place, rows)],
                )
                self.loads[kind].append((place, copy))
            place += rows
            self.started += 1

    def wait(self, group, kind):
        end = (group + 1) * GROUP
        while self.loads[kind] and self.loads[kind][0][0] < end:
            self.loads[kind].pop(0)[1].wait()


def project_kernel(first, x_ref, b_ref, place_ref, *rest):
    (*w_refs, q_ref, kv_ref, weight, stage, semaphores) = rest
    copies = Copies(semaphores)
    pairs = stage.shape[1]
    wide = pairs * PAIR
    loads = load_projection(copies, w_refs, first, pairs, weight, place_ref)
    stores = []
    for part in (0, 1, 2):
        wait(loads[part])
        out = dot_nt(x_ref[...], weight[part * wide : (part + 1) * wide]) + b_ref[part]
        out = out.astype(bf16)
        if part == 0:
            out = out * bf16(1.0 / math.sqrt(HEAD))
        for pair in range(pairs):
            stage[part, pair] = out[:, pair * PAIR : (pair + 1) * PAIR]
        target = q_ref if part == 0 else kv_ref.at[part - 1]
        stores.append(copies.start(stage.at[part], target))
    wait(stores)


def project(x, table, bias, place):
    count, width = x.shape
    arrays, first = table
    pairs = arrays[0].shape[1]
    return call(
        functools.partial(project_kernel, first),
        [IN_VMEM, IN_VMEM, IN_SMEM] + [IN_HBM] * len(arrays),
        [IN_HBM, IN_HBM],
        [struct((pairs, count, PAIR), bf16), struct((2, pairs, count, PAIR), bf16)],
        scratch=[
            pltpu.VMEM((3 * pairs * PAIR, width), bf16),
            pltpu.VMEM((3, pairs, count, PAIR), bf16),
            pltpu.SemaphoreType.DMA((12 * pairs + 3,)),
        ],
        flops=2 * count * width * 3 * PAIR * pairs,
        moved=2 * (count * width * 4 + 3 * width * PAIR * pairs),
    )(x, bias, place, *arrays)


def feed_forward(copies, places, x_ref, mixed_ref, ow_ref, h_refs, vec_ref, ub_ref,
                 z1_ref, r1_ref, weight_o, weight_u, weight_d, slope, normed, low, acc):
    o_first, pieces = places
    pairs = mixed_ref.shape[0]
    loads_o = load_heads(copies, ow_ref, o_first, 1, pairs, weight_o)[0]
    weights = Hidden(copies, h_refs, pieces, weight_u, weight_d)
    groups = weights.groups
    weights.fetch(groups - 1)
    mixed = jnp.concatenate([mixed_ref[i] for i in range(pairs)], axis=1)
    wait(loads_o)
    attended = dot_nn(mixed, weight_o[...])
    z, r = unit(x_ref[...].astype(f32) + attended + vec_ref[0:1])
    z1_ref[...] = z.astype(bf16)
    r1_ref[...] = r
    out = z * vec_ref[2:3] + vec_ref[4:5]
    normed[...] = out
    low[...] = out.astype(bf16)

    halves = 2
    rows = low.shape[0] // halves

    def before(chunk):
        group, half = divmod(chunk, halves)
        if half == 0:
            weights.fetch(min(group + 1, groups - 1))
            weights.wait(group, 0)
        span = slice(group * GROUP, (group + 1) * GROUP)
        return dot_nt(low[half * rows : (half + 1) * rows], weight_u[span]) + ub_ref[:, span]

    later = before(0)
    for chunk in range(groups * halves):
        group, half = divmod(chunk, halves)
        pre = later
        if chunk + 1 < groups * halves:
            later = before(chunk + 1)
        span = slice(group * GROUP, (group + 1) * GROUP)
        here = slice(half * rows, (half + 1) * rows)
        spread = 0.5 + 0.5 * lax.erf(pre * math.sqrt(0.5))
        bell = jnp.exp(-0.5 * pre * pre) * (1.0 / math.sqrt(2.0 * math.pi))
        slope[here, span] = (spread + pre * bell).astype(bf16)
        if half == 0:
            weights.wait(group, 1)
        out = dot_nn((pre * spread).astype(bf16), weight_d[span])
        if group == 0:
            acc[here] = out
        else:
            acc[here] += out
    return unit(normed[...] + acc[...] + vec_ref[1:2])


def feed_kernel(places, sources, blocks, x_ref, mixed_ref, ow_ref, vec_ref, ub_ref, rank_ref, *rest):
    h_refs = rest[:sources]
    out_refs = rest[sources : sources + max(blocks, 1)]
    (z1_ref, r1_ref, z2_ref, r2_ref, slope_ref, weight_o, weight_u, weight_d,
     z1, z2, slope, normed, low, acc, semaphores) = rest[sources + max(blocks, 1) :]
    copies = Copies(semaphores)
    z, r = feed_forward(
        copies, places, x_ref, mixed_ref, ow_ref, h_refs, vec_ref, ub_ref,
        z1, r1_ref, weight_o, weight_u, weight_d, slope, normed, low, acc,
    )
    stores = [copies.start(z1, z1_ref), copies.start(slope, slope_ref)]
    z2[...] = z.astype(bf16)
    r2_ref[...] = r
    stores.append(copies.start(z2, z2_ref))
    low[...] = (z * vec_ref[3:4] + vec_ref[5:6]).astype(bf16)
    rows = low.shape[0] // max(blocks, 1)
    for j in range(max(blocks, 1)):
        start = pl.multiple_of((rank_ref[0] ^ j) * rows, rows) if blocks else 0
        stores.append(copies.start(low.at[pl.ds(start, rows)], out_refs[j]))
    wait(stores)


def feed_scratch(count, width, wide, hidden, pairs):
    return [
        pltpu.VMEM((wide, width), bf16),
        pltpu.VMEM((hidden, width), bf16),
        pltpu.VMEM((hidden, width), bf16),
        pltpu.VMEM((count, width), bf16),
        pltpu.VMEM((count, width), bf16),
        pltpu.VMEM((count, hidden), bf16),
        pltpu.VMEM((count, width), f32),
        pltpu.VMEM((count, width), bf16),
        pltpu.VMEM((count, width), f32),
        pltpu.SemaphoreType.DMA((16 * pairs + 8,)),
    ]


def feed_sizes(x, mixed, up_bias):
    count, width = x.shape
    pairs = mixed.shape[0]
    return count, width, pairs, pairs * PAIR, up_bias.shape[1]


def feed(x, mixed, tables, vectors, up_bias, rank, blocks):
    o_table, (arrays, pieces) = tables
    count, width, pairs, wide, hidden = feed_sizes(x, mixed, up_bias)
    square = struct((count, width), bf16)
    column = struct((count, 1), f32)
    parts = max(blocks, 1)
    out, kept = [], []
    found = call(
        functools.partial(feed_kernel, (o_table[1], pieces), len(arrays), blocks),
        [IN_VMEM, IN_VMEM, IN_HBM, IN_VMEM, IN_VMEM, IN_SMEM] + [IN_HBM] * len(arrays),
        [IN_HBM] * parts + [IN_HBM, IN_VMEM, IN_HBM, IN_VMEM, IN_HBM],
        [struct((count // parts, width), bf16)] * parts
        + [square, column, square, column, struct((count, hidden), bf16)],
        scratch=feed_scratch(count, width, wide, hidden, pairs),
        flops=2 * count * width * (wide + 2 * hidden),
        moved=2 * (2 * hidden * width + 12 * count * width),
        exps=2 * count * hidden,
    )(x, mixed, o_table[0], vectors, up_bias, rank, *arrays)
    return (found[:blocks] if blocks else found[0], *found[parts:])


def summed(own, got, part):
    columns = []
    for pair in range(own.shape[1]):
        column = own[part, pair].astype(f32)
        for i in range(got.shape[0]):
            column += got[i, part, pair].astype(f32)
        columns.append(column.astype(bf16))
    return jnp.concatenate(columns, axis=1)


def leave_kernel(p_first, extra, first_ref, dq_ref, own_ref, got_ref, pw_ref, rank_ref, *rest):
    if extra:
        prefix_ref, *rest = rest
    (*out_refs, weight_p, low, first, dq, own, got, semaphores) = rest
    copies = Copies(semaphores)
    pairs = dq.shape[0]
    wide = pairs * PAIR
    load_q = copies.start(dq_ref, dq)
    loads = load_heads(copies, pw_ref, p_first, 3, pairs, weight_p)
    others = [copies.start(own_ref, own), copies.start(got_ref, got)]
    load_first = copies.start(first_ref, first)
    load_q.wait()
    wait(loads[0])
    total = dot_nn(jnp.concatenate([dq[pair] for pair in range(pairs)], axis=1), weight_p[:wide])
    wait(others)
    for part in (1, 2):
        wait(loads[part])
        total += dot_nn(summed(own, got, part - 1), weight_p[part * wide : (part + 1) * wide])
    load_first.wait()
    low[...] = (total + first[...].astype(f32)).astype(bf16)
    rows = low.shape[0] // len(out_refs)
    for j, target in enumerate(out_refs):
        start = pl.multiple_of((rank_ref[0] ^ j) * rows, rows)
        target[:rows] = low[pl.ds(start, rows)]
        if extra:
            value = prefix_ref[rank_ref[0] ^ j].astype(bf16)
            for column in range(value.shape[0] // 16):
                span = slice(column * PAIR, (column + 1) * PAIR)
                target[rows:, span] = value[column * 16 : (column + 1) * 16]


def leave(first, dq, own, got, p_table, rank, blocks, prefix=None):
    count, width = first.shape
    pairs = dq.shape[0]
    more = [] if prefix is None else [prefix]
    return call(
        functools.partial(leave_kernel, p_table[1], len(more)),
        [IN_ANY] * 4 + [IN_HBM, IN_SMEM] + [IN_VMEM] * len(more),
        [IN_VMEM] * blocks,
        [struct((count // blocks + 16 * len(more), width), bf16)] * blocks,
        scratch=[
            pltpu.VMEM((3 * pairs * PAIR, width), bf16),
            pltpu.VMEM((count, width), bf16),
            pltpu.VMEM((count, width), bf16),
            pltpu.VMEM(dq.shape, bf16),
            pltpu.VMEM(own.shape, bf16),
            pltpu.VMEM(got.shape, bf16),
            pltpu.SemaphoreType.DMA((6 * pairs + 4,)),
        ],
        flops=2 * count * width * 3 * PAIR * pairs,
        moved=2 * (count * width * 7 + 3 * width * PAIR * pairs),
        vmem=28 * 1024 * 1024,
    )(first, dq, own, got, p_table[0][0], rank, *more)


def attend_kernel(
    prefix_count, q_ref, own_ref, other_ref, pk_ref, pv_ref, sq_ref, sk_ref,
    mixed_ref, raised_ref, inverse_ref, bias_ref,
):
    pad = pk_ref.shape[1]
    others = other_ref.shape[0]

    @pl.when(pl.program_id(0) == 0)
    def _():
        row = lax.broadcasted_iota(jnp.int32, (pad, bias_ref.shape[1]), 0)
        bias_ref[:pad] = jnp.where(row < prefix_count, 0.0, MASKED)
        keys = jnp.broadcast_to(sk_ref[...], (8, sk_ref.shape[1])).T[:, :1]
        same = (keys == sq_ref[...]) & (keys >= 0)
        bias_ref[pad:] = jnp.where(same, 0.0, MASKED)

    keys = jnp.concatenate(
        [pk_ref[0], own_ref[0, 0]] + [other_ref[i, 0, 0] for i in range(others)], axis=0
    )
    values = jnp.concatenate(
        [pv_ref[0], own_ref[1, 0]] + [other_ref[i, 1, 0] for i in range(others)], axis=0
    )
    queries = q_ref[0]
    lane = lax.broadcasted_iota(jnp.int32, queries.shape, 1)
    value_lane = lax.broadcasted_iota(jnp.int32, values.shape, 1)
    parts = []
    inverses = []
    count = queries.shape[0]
    score = lambda head: dot_nt(
        keys, jnp.where((lane // HEAD) == head, queries, bf16(0))
    ) + bias_ref[...]
    ahead = score(0)
    for head in range(2):
        scores = ahead
        if head == 0:
            ahead = score(1)
        raised = jnp.exp(scores - jnp.max(scores, axis=0, keepdims=True))
        low = raised.astype(bf16)
        raised_ref[0, head] = low
        ones = jnp.where((value_lane // HEAD) == head, values, bf16(1))
        out = dot_tn(ones, low)
        inverse = 1.0 / out[(1 - head) * HEAD : (1 - head) * HEAD + 1]
        out = out[head * HEAD : (head + 1) * HEAD]
        parts.append(out * inverse)
        inverses.append(jnp.broadcast_to(inverse, out.shape))
    mixed_ref[0] = jnp.concatenate(parts, axis=0).T.astype(bf16)
    inverse_ref[0] = jnp.concatenate(inverses, axis=0).T.astype(bf16)


def attend(q, own, other, pk, pv, prefix_count, seg_q, seg_k):
    pairs, count, _ = q.shape
    others = other.shape[0]
    pad = pk.shape[1]
    total = pad + count * (others + 1)
    by_pair = pl.BlockSpec((1, count, PAIR), lambda i: (i, 0, 0))
    by_prefix = pl.BlockSpec((1, pad, PAIR), lambda i: (i, 0, 0))
    return call(
        functools.partial(attend_kernel, prefix_count),
        [
            by_pair,
            pl.BlockSpec((2, 1, count, PAIR), lambda i: (0, i, 0, 0)),
            pl.BlockSpec((others, 2, 1, count, PAIR), lambda i: (0, 0, i, 0, 0)),
            by_prefix,
            by_prefix,
            whole((1, count)),
            whole((1, total - pad)),
        ],
        [
            by_pair,
            pl.BlockSpec((1, 2, total, count), lambda i: (i, 0, 0, 0)),
            by_pair,
        ],
        [
            struct((pairs, count, PAIR), bf16),
            struct((pairs, 2, total, count), bf16),
            struct((pairs, count, PAIR), bf16),
        ],
        scratch=[pltpu.VMEM((total, count), f32)],
        grid=(pairs,),
        flops=8 * total * count * PAIR * pairs,
        moved=4 * pairs * total * count,
        exps=2 * pairs * total * count,
    )(q, own, other, pk, pv, seg_q, seg_k)


def attention_back(d_out, mixed, inverse, raised, queries, keys, values):
    lane = lax.broadcasted_iota(jnp.int32, queries.shape, 1)
    scaled = d_out.astype(f32) * inverse.astype(f32)
    products = (scaled * mixed.astype(f32)).T
    scaled = scaled.astype(bf16)
    d_keys = jnp.zeros(keys.shape, f32)
    d_values = jnp.zeros(keys.shape, f32)
    parts = []
    for head in range(2):
        chosen = (lane // HEAD) == head
        span = slice(head * HEAD, (head + 1) * HEAD)
        delta = jnp.sum(products[span], axis=0, keepdims=True)
        here = jnp.where(chosen, scaled, bf16(0))
        low = raised(head)
        d_score = (low.astype(f32) * (dot_nt(values, here) - delta)).astype(bf16)
        d_values += dot_nn(low, here)
        d_keys += dot_nn(d_score, jnp.where(chosen, queries, bf16(0)))
        parts.append(dot_tn(keys, d_score)[span])
    return jnp.concatenate(parts, axis=0).T * (1.0 / math.sqrt(HEAD)), d_keys, d_values


def back_kernel(p_first, p_sources, o_first, pieces, sources, place_ref, *rest):
    if p_first is None:
        grad_ref, *rest = rest
    else:
        first1_ref, dq_in, own_in, got_in, *rest = rest
        pw_refs, rest = rest[:p_sources], rest[p_sources:]
    (ow_ref, vec_ref, z1_ref, r1_ref, z2_ref, r2_ref, slope_ref,
     mixed_ref, inverse_ref, raised_ref, q_ref, own_ref, other_ref, pk_ref, pv_ref, *rest) = rest
    h_refs, rest = rest[:sources], rest[sources:]
    outs, rest = rest[:5], rest[5:]
    (weight_o, weight_u, weight_d, unit_in, slope, low, acc, first, dq, down, dother, prefix,
     mixed, inverse, raised, queries, own, other, semaphores, turns, stores, *weight_p) = rest
    copies = Copies(semaphores)
    pairs, count, _ = dq.shape
    others = dother.shape[0]
    pad = pk_ref.shape[1]
    weights = Hidden(copies, h_refs, pieces, weight_u, weight_d)
    groups = weights.groups
    slopes = []

    def fetch(group):
        weights.fetch(group)
        span = (slice(None), pl.ds(group * GROUP, GROUP))
        slopes.append(copies.start(slope_ref.at[span], slope.at[span]))

    if p_first is None:
        load = copies.start(grad_ref, low)
        load_z2 = copies.start(z2_ref, unit_in)
        fetch(0)
        load.wait()
        grad = low[...].astype(f32)
    else:
        load_q = copies.start(dq_in, dq)
        loads_p = load_projection(copies, pw_refs, p_first, pairs, weight_p[0], place_ref)
        loads = [copies.start(own_in, down), copies.start(got_in, dother)]
        load_first = copies.start(first1_ref, first)
        load_z2 = copies.start(z2_ref, unit_in)
        fetch(0)
        wide = pairs * PAIR
        load_q.wait()
        wait(loads_p[0])
        left = jnp.concatenate([dq[pair] for pair in range(pairs)], axis=1)
        total = dot_nn(left, weight_p[0][:wide])
        wait(loads)
        for part in (1, 2):
            wait(loads_p[part])
            total += dot_nn(
                summed(down, dother, part - 1), weight_p[0][part * wide : (part + 1) * wide]
            )
        load_first.wait()
        grad = (total + first[...].astype(f32)).astype(bf16).astype(f32)
    load_z2.wait()
    acc[...] = unit_back(grad, unit_in[...].astype(f32), r2_ref[...], vec_ref[3:4])
    low[...] = acc[...].astype(bf16)
    load_z1 = copies.start(z1_ref, unit_in)
    loads_o = load_heads(copies, ow_ref, o_first, 1, pairs, weight_o)[0]

    def turn(pair, slot):
        moves = (
            (raised_ref.at[pair], raised.at[slot]),
            (q_ref.at[pair], queries.at[slot]),
            (mixed_ref.at[pair], mixed.at[slot]),
            (inverse_ref.at[pair], inverse.at[slot]),
            (own_ref.at[:, pair], own.at[slot]),
            (other_ref.at[:, :, pair], other.at[slot]),
        )
        return [
            pltpu.make_async_copy(source, target, turns.at[slot, i])
            for i, (source, target) in enumerate(moves)
        ]

    for group in range(groups):
        if group + 1 < groups:
            fetch(group + 1)
        if group == groups - 1:
            for pair in range(2):
                for copy in turn(pair, pair):
                    copy.start()
        slopes[group].wait()
        weights.wait(group, 0)
        weights.wait(group, 1)
        span = slice(group * GROUP, (group + 1) * GROUP)
        d_act = dot_nt(low[...], weight_d[span])
        d_pre = (d_act * slope[:, span].astype(f32)).astype(bf16)
        acc[...] += dot_nn(d_pre, weight_u[span])
    load_z1.wait()
    d_first = unit_back(acc[...], unit_in[...].astype(f32), r1_ref[...], vec_ref[2:3])
    first[...] = d_first.astype(bf16)
    store_first = copies.start(first, outs[0])
    wait(loads_o)
    low[...] = dot_nt(d_first.astype(bf16), weight_o[...]).astype(bf16)

    def save(pair):
        moves = (
            (dq.at[pair], outs[1].at[pair]),
            (down.at[:, pair], outs[2].at[:, pair]),
            (dother.at[:, :, pair], outs[3].at[:, :, pair]),
            (prefix.at[pair], outs[4].at[pair]),
        )
        return [
            pltpu.make_async_copy(source, target, stores.at[pair, i])
            for i, (source, target) in enumerate(moves)
        ]

    def step(pair, carry):
        slot = lax.rem(pair, 2)
        for copy in turn(pair, slot):
            copy.wait()
        keys = jnp.concatenate(
            [pk_ref[pair], own[slot, 0]] + [other[slot, i, 0] for i in range(others)], axis=0
        )
        values = jnp.concatenate(
            [pv_ref[pair], own[slot, 1]] + [other[slot, i, 1] for i in range(others)], axis=0
        )
        d_query, d_keys, d_values = attention_back(
            low[:, pl.ds(pl.multiple_of(pair * PAIR, PAIR), PAIR)],
            mixed[slot],
            inverse[slot],
            lambda head: raised[slot, head],
            queries[slot],
            keys,
            values,
        )
        dq[pair] = d_query.astype(bf16)
        prefix[pair, :pad] = d_keys[:pad]
        prefix[pair, pad:] = d_values[:pad]
        for part, d_part in enumerate((d_keys, d_values)):
            down[part, pair] = d_part[pad : pad + count].astype(bf16)
            for i in range(others):
                start = pad + (i + 1) * count
                dother[i, part, pair] = d_part[start : start + count].astype(bf16)
        for copy in save(pair):
            copy.start()

        @pl.when(pair + 2 < pairs)
        def _():
            for copy in turn(pair + 2, slot):
                copy.start()

        return carry

    lax.fori_loop(0, pairs, step, 0)
    store_first.wait()
    for pair in range(pairs):
        for copy in save(pair):
            copy.wait()


def backward(grads, p_table, tables, vectors, kept, attention, place):
    o_table, (arrays, pieces) = tables
    mixed, inverse, raised, q, own, other, pk, pv = attention
    pairs, count, _ = q.shape
    width = o_table[0].shape[-1]
    wide = pairs * PAIR
    total = raised.shape[2]
    pad = pk.shape[1]
    slope = kept[-1]
    hidden = slope.shape[1]
    more, p_first = ([], None) if p_table is None else p_table
    vm = pltpu.VMEM
    return call(
        functools.partial(
            back_kernel, p_first, len(more), o_table[1], pieces, len(arrays)
        ),
        [IN_SMEM] + [IN_HBM] * (len(grads) + len(more))
        + [IN_HBM, IN_VMEM, IN_HBM, IN_VMEM, IN_HBM, IN_VMEM, IN_HBM]
        + [IN_HBM] * 6 + [IN_VMEM] * 2
        + [IN_HBM] * len(arrays),
        [IN_HBM] * 5,
        [
            struct((count, width), bf16),
            struct(q.shape, bf16),
            struct(own.shape, bf16),
            struct(other.shape, bf16),
            struct((pairs, 2 * pad, PAIR), f32),
        ],
        scratch=[
            vm((wide, width), bf16),
            vm((hidden, width), bf16),
            vm((hidden, width), bf16),
            vm((count, width), bf16),
            vm((count, hidden), bf16),
            vm((count, width), bf16),
            vm((count, width), f32),
            vm((count, width), bf16),
            vm(q.shape, bf16),
            vm(own.shape, bf16),
            vm(other.shape, bf16),
            vm((pairs, 2 * pad, PAIR), f32),
            vm((2, count, PAIR), bf16),
            vm((2, count, PAIR), bf16),
            vm((2, 2, total, count), bf16),
            vm((2, count, PAIR), bf16),
            vm((2, 2, count, PAIR), bf16),
            vm((2, other.shape[0], 2, count, PAIR), bf16),
            pltpu.SemaphoreType.DMA((22 * pairs + 16,)),
            pltpu.SemaphoreType.DMA((2, 6)),
            pltpu.SemaphoreType.DMA((pairs, 4)),
        ]
        + [vm((3 * wide, width), bf16)] * (p_table is not None),
        flops=2 * count * width * (4 * wide + 2 * hidden) + 16 * total * count * PAIR * pairs,
        moved=2 * (2 * hidden * width + 4 * wide * width + 16 * count * width) + 4 * pairs * total * count,
    )(place, *grads, *more, o_table[0], vectors, *kept, *attention, *arrays)


def per_device(
    boundary, segment_ids, project_weight, project_bias, output_weight, output_biases,
    norm_gains, norm_shifts, up_weight, up_bias, down_weight, prefix_keys, prefix_values,
):
    section = lax.axis_index("section")
    rank = lax.axis_index("tensor")
    ranks = lax.axis_size("tensor")
    is_first = section == 0
    micro, slots, rows, width = boundary.shape[1:]
    length = slots * ranks
    row_count = micro * rows
    chips = ranks // row_count
    blocks = SECTIONS * chips
    count = length // blocks
    place = rank % chips
    swap = [(0, 1), (1, 0)]
    after = lambda value, *first: lax.optimization_barrier((value, *first))[0]
    heads_all = project_weight.shape[3] * ranks
    pairs = heads_all // PAIR
    shards = ranks // pairs
    prefix_count = prefix_keys.shape[1]
    pad = -(-prefix_count // 32) * 32
    low_width = project_weight.shape[3] // 2
    hidden = up_weight.shape[2] // 2

    quick = chips == 1 and ranks == 8 and lax.axis_size("dp") == 2

    half_ranks = ranks // 2
    low_rank = rank % half_ranks
    block = section * chips + place
    by_row = jnp.transpose(boundary[0], (0, 2, 1, 3)).reshape(row_count, slots, width)

    def ordered(parts):
        bit = 1
        while bit < len(parts):
            flip = (rank & bit) != 0
            parts = [jnp.where(flip, parts[i ^ bit], part) for i, part in enumerate(parts)]
            bit *= 2
        return parts

    if quick:
        lower, upper = by_row[:half_ranks], by_row[half_ranks:]
        keep = jnp.where(is_first, lower, upper)
        got = lax.ppermute(jnp.where(is_first, upper, lower), "section", swap)

        def arrive(rows_here):
            parts = []
            for j in range(half_ranks):
                route = [
                    (s * ranks + t, (t // half_ranks) * ranks + half_ranks * s + ((t % half_ranks) ^ j))
                    for s in range(SECTIONS)
                    for t in range(ranks)
                ]
                part = lax.dynamic_index_in_dim(rows_here, low_rank ^ j, 0, keepdims=False)
                parts.append(lax.ppermute(part, ("section", "tensor"), route))
            return jnp.concatenate(ordered(parts), axis=0)

        tokens = arrive(jnp.where(is_first, keep, got))
        cotangent_rows = jnp.where(is_first, got, keep)
    else:
        if chips > 1:
            by_row = jnp.repeat(by_row, chips, axis=0)
        row = lax.all_to_all(by_row, "tensor", 0, 0, tiled=True).reshape(length, width)
        other_block = (1 - section) * chips + place
        mine = lax.dynamic_slice_in_dim(row, block * count, count, 0)
        theirs = lax.dynamic_slice_in_dim(row, other_block * count, count, 0)
        got = lax.ppermute(theirs, "section", swap)
        tokens = jnp.where(is_first, mine, got)
        cotangent = jnp.where(is_first, got, mine)

    own_vectors = jnp.concatenate(
        [output_biases[0], norm_gains[0], norm_shifts[0], norm_shifts[0]], axis=0
    )
    got_vectors = lax.ppermute(own_vectors, "section", swap)
    vectors = [
        jnp.where(is_first, own_vectors, got_vectors).astype(f32),
        jnp.where(is_first, got_vectors, own_vectors).astype(f32),
    ]

    segments = lax.dynamic_index_in_dim(
        segment_ids.reshape(row_count, length), rank // chips, 0, keepdims=False
    )
    seg_q = lax.dynamic_slice_in_dim(segments, block * count, count, 0)
    seg_k = jnp.concatenate(
        [
            lax.dynamic_slice_in_dim(segments, (block ^ distance) * count, count, 0)
            for distance in range(blocks)
        ]
    )[None, :]
    seg_q = seg_q[None, :]

    project_rows = jnp.transpose(project_weight[0], (1, 2, 0)).reshape(3, 2, low_width, width)
    project_rows = jnp.transpose(project_rows, (1, 0, 2, 3)).reshape(2, 3 * low_width, width)
    out_rows = output_weight[0].reshape(2, low_width, width)
    up_rows = jnp.transpose(up_weight[0], (1, 0)).reshape(2, hidden, width)
    down_rows = down_weight[0].reshape(2, hidden, width)
    if quick:
        keep, give = pack(
            jnp.transpose(project_weight[0], (1, 0, 2)), output_weight[0], up_weight[0],
            down_weight[0], section.astype(jnp.int32).reshape(1),
        )
        give, project_bias, up_bias, prefix_keys, prefix_values = lax.optimization_barrier(
            (give, project_bias, up_bias, prefix_keys, prefix_values)
        )
    else:
        packed = jnp.concatenate([project_rows, out_rows, up_rows, down_rows], axis=1)
        keep = lax.dynamic_index_in_dim(packed, section, 0, keepdims=False)
        give = lax.dynamic_index_in_dim(packed, 1 - section, 0, keepdims=False)
    got = lax.ppermute(give, "section", swap)
    small = jnp.concatenate(
        [
            jnp.transpose(project_bias[0].reshape(3, 2, low_width), (1, 0, 2)).reshape(2, -1),
            up_bias[0].reshape(2, hidden),
            jnp.transpose(prefix_keys[0].reshape(-1, 2, low_width), (1, 0, 2)).reshape(2, -1),
            jnp.transpose(prefix_values[0].reshape(-1, 2, low_width), (1, 0, 2)).reshape(2, -1),
        ],
        axis=1,
    )
    small_size = small.shape[1]
    small_rows = -(-small_size // (16 * width)) * 16
    small = jnp.pad(small, ((0, 0), (0, small_rows * width - small_size)))
    small = small.reshape(2, small_rows, width)
    keep_small = jnp.where(is_first, small[0], small[1])
    got_small = lax.ppermute(jnp.where(is_first, small[1], small[0]), "section", swap)
    small_first = jnp.where(is_first, keep_small, got_small)
    small_second = jnp.where(is_first, got_small, keep_small)
    rows_first = lambda cut: jnp.where(is_first, keep[cut], got[cut])
    rows_second = lambda cut: jnp.where(is_first, got[cut], keep[cut])
    sizes = [3 * low_width, low_width, hidden, hidden, small_rows]
    p_end, o_end, u_end, d_end, s_end = [sum(sizes[: i + 1]) for i in range(len(sizes))]
    plane = lax.axis_index("dp")
    gather = lambda parts: lax.all_gather(
        jnp.concatenate(parts, axis=0), ("section", "tensor"), axis=0
    ).reshape(2, ranks, -1, width)

    def unpack(flat):
        cut = 0
        found = []
        for groups, size in ((3, low_width), (1, hidden), (prefix_count, low_width), (prefix_count, low_width)):
            part = flat[:, :, cut : cut + groups * size].reshape(2, pairs, shards, groups, size)
            cut += groups * size
            if shards == 1:
                part = part[:, :, 0]
            else:
                part = jnp.transpose(part, (2, 1, 3, 0, 4)).reshape(2, pairs, groups, 2 * size)
            found.append(part)
        p_bias = jnp.transpose(found[0], (2, 1, 0, 3)).reshape(3, 1, heads_all).astype(f32)
        prefix = [
            jnp.pad(
                jnp.transpose(part, (1, 2, 0, 3)).reshape(pairs, prefix_count, PAIR),
                ((0, 0), (0, pad - prefix_count), (0, 0)),
            )
            for part in found[2:]
        ]
        return p_bias, found[1][:, :, 0], prefix[0], prefix[1]

    tables = []
    smalls = []
    plane = lax.axis_index("dp")
    share = 3 * low_width // 2
    projection = rows_second(slice(0, p_end))
    if quick:
        projection = jnp.where(plane == 0, projection[:share], projection[share:])
    early_rows = [rows_first(slice(0, d_end)), projection, small_first, small_second]
    projection_rows = projection.shape[0]
    late_rows = rows_second(slice(p_end, d_end))
    early = gather(early_rows)
    early, vectors[0], vectors[1], seg_q, seg_k, tokens = lax.optimization_barrier(
        (early, vectors[0], vectors[1], seg_q, seg_k, tokens)
    )
    late = gather([after(late_rows, early)])
    def table(array, first, size, groups=1):
        if shards == 1:
            return (array, first, size)
        part = array[:, :, first : first + size].reshape(
            2, pairs, shards, groups, size // groups, width
        )
        part = jnp.transpose(part, (2, 1, 3, 0, 4, 5))
        return (part.reshape(2, pairs, 2 * size, width), 0, 2 * size)

    def projection_table(layer):
        if quick and layer:
            return None
        array, first, _ = table(early, layer * d_end, 3 * low_width, 3)
        return (array,), first

    for layer in range(2):
        source, shift = (late, -p_end) if layer else (early, 0)
        up, u_first, rows_here = table(source, shift + o_end, 2 * hidden, 2)
        rows_here //= 2
        pieces = tuple(
            (0, (s, t), u_first, u_first + rows_here, rows_here)
            for s in range(2)
            for t in range(pairs)
        )
        tables.append(
            (
                projection_table(layer),
                table(source, shift + p_end, low_width),
                ((up,), pieces),
            )
        )
        start = d_end + projection_rows + layer * small_rows
        p_bias, u_bias, pk, pv = unpack(
            early[:, :, start : start + small_rows].reshape(2, ranks, -1)
        )
        smalls.append((p_bias, u_bias.reshape(1, -1).astype(f32), pk, pv))

    def flips():
        routes = []
        for distance in range(1, blocks):
            route = []
            for s in range(SECTIONS):
                for t in range(ranks):
                    index = (s * chips + t % chips) ^ distance
                    route.append(
                        (s * ranks + t, (index // chips) * ranks + t // chips * chips + index % chips)
                    )
            routes.append(route)
        return routes

    routes = flips()

    def exchange(parts):
        return jnp.stack(
            [
                lax.ppermute(part, ("section", "tensor"), route) if chips > 1
                else lax.ppermute(part, "section", swap)
                for part, route in zip(parts, routes)
            ]
        )

    out_blocks = half_ranks if quick else 1
    order = (low_rank if quick else 0 * rank).astype(jnp.int32).reshape(1)
    place_here = jnp.stack([plane, section]).astype(jnp.int32)
    p_tables = []
    saved = []
    x = tokens
    for layer in range(2):
        p_table, *others = tables[layer]
        p_bias, u_bias, pk, pv = smalls[layer]
        if quick and layer == 0:
            cross = lax.dynamic_slice(
                early, (section, 0, d_end, 0), (1, pairs, share, width)
            ).reshape(pairs, share, width)
            theirs = lax.ppermute(cross, "dp", swap)
        if quick and layer == 1:
            p_table = ((early, theirs, theirs_too), d_end)
        p_tables.append(p_table)
        q, own = project(x, p_table, p_bias, place_here)
        other = exchange([own] * (blocks - 1))
        mixed, raised, inverse = attend(q, own, other, pk, pv, prefix_count, seg_q, seg_k)
        saved.append((mixed, inverse, raised, q, own, other, pk, pv))
        if layer == 1 and quick:
            cotangent = arrive(after(cotangent_rows, late))
        x, *kept = feed(
            x, mixed, others, vectors[layer], u_bias, order, out_blocks if layer else 0
        )
        saved[-1] += (kept,)
        if layer == 0 and quick:
            theirs, x = lax.optimization_barrier((theirs, x))
            theirs_too = lax.ppermute(theirs, "section", swap)
    outs = x
    kept_0, kept_1 = (entry[-1] for entry in saved)
    saved = [entry[:-1] for entry in saved]
    first, dq, down, dother, prefix_1 = backward(
        (cotangent,), None, tables[1][1:], vectors[1], kept_1, saved[1], place_here
    )

    def send_blocks(parts):
        got = []
        for j, part in enumerate(parts):
            route = [
                (s * ranks + t, (t // half_ranks) * ranks + half_ranks * s + ((t % half_ranks) ^ j))
                for s in range(SECTIONS)
                for t in range(ranks)
            ]
            got.append(lax.ppermute(part, ("section", "tensor"), route))
        return got

    if quick:
        dother, *outs = lax.optimization_barrier((dother, *outs))
        outs = send_blocks(outs)
    got = exchange([dother[i] for i in range(blocks - 1)])
    first, dq, down, dother, prefix_0 = backward(
        (first, dq, down, got), p_tables[1], tables[0][1:], vectors[0], kept_0, saved[0], place_here
    )
    if quick:
        dother, *outs = lax.optimization_barrier((dother, *outs))
    got = exchange([dother[i] for i in range(blocks - 1)])
    if quick:
        prefix = jnp.stack([prefix_0, prefix_1], axis=1)
        lower, upper = prefix[: pairs // 2], prefix[pairs // 2 :]
        other = lax.ppermute(jnp.where(is_first, upper, lower), "section", swap)
        prefix = jnp.where(is_first, lower, upper) + other
        prefix = prefix.reshape(half_ranks, 4 * pad, PAIR)
    else:
        prefix = None
    grads = leave(first, dq, down, got, tables[0][0], order, out_blocks, prefix)

    if quick:
        grads = send_blocks(grads)
        partial = sum(part[slots:].astype(f32) for part in grads)
        grads = jnp.stack(ordered([part[:slots] for part in grads]))
        outs = jnp.stack(ordered(outs))
        keep = jnp.where(is_first, grads, outs)
        got = lax.ppermute(jnp.where(is_first, outs, grads), "section", swap)
        partial += lax.ppermute(partial, "dp", swap)
        partial = jnp.transpose(partial.reshape(16, -1, PAIR), (1, 0, 2)).reshape(2, 2 * pad, PAIR)
        prefix = jnp.where(is_first, partial[0], partial[1]) + lax.ppermute(
            jnp.where(is_first, partial[1], partial[0]), "section", swap
        )
        back = jnp.concatenate(
            [jnp.where(is_first, keep, got), jnp.where(is_first, got, keep)], axis=0
        )
    else:
        keep = jnp.where(is_first, grads[0], outs[0])
        got = lax.ppermute(jnp.where(is_first, outs[0], grads[0]), "section", swap)
        row = jnp.zeros((length, width), bf16)
        row = lax.dynamic_update_slice_in_dim(
            row, jnp.where(is_first, keep, got), place * count, 0
        )
        row = lax.dynamic_update_slice_in_dim(
            row, jnp.where(is_first, got, keep), (chips + place) * count, 0
        )
        back = lax.all_to_all(row.reshape(ranks, slots, width), "tensor", 0, 0, tiled=True)
        back = jnp.sum(back.reshape(row_count, chips, slots, width), axis=1)
    result = jnp.transpose(back.reshape(micro, rows, slots, width), (0, 2, 1, 3))[None]

    if quick:
        both = prefix.reshape(2, pad, PAIR)[:, :prefix_count]
    else:
        both = jnp.where(
            is_first,
            lax.psum(prefix_0, ("section", "dp", "tensor")),
            lax.psum(prefix_1, ("section", "dp", "tensor")),
        )
        both = both.reshape(pairs, 2, pad, PAIR)[:, :, :prefix_count]
        both = jnp.transpose(both, (1, 2, 0, 3)).reshape(2, prefix_count, heads_all)
        share = heads_all // ranks
        both = lax.dynamic_slice_in_dim(both, rank * share, share, 2)
    return (result, both[0][None], both[1][None])


def solution(mesh):
    in_specs = (
        P("section", None, "tensor", "dp", None),
        P(None, "dp", None),
        P("section", None, None, "tensor"),
        P("section", None, "tensor"),
        P("section", "tensor", None),
        P("section", None, None),
        P("section", None, None),
        P("section", None, None),
        P("section", None, "tensor"),
        P("section", "tensor"),
        P("section", "tensor", None),
        P("section", None, "tensor"),
        P("section", None, "tensor"),
    )
    out_specs = (
        P("section", None, "tensor", "dp", None),
        P("section", None, "tensor"),
        P("section", None, "tensor"),
    )
    return jax.shard_map(
        per_device, mesh=mesh, in_specs=in_specs, out_specs=out_specs, check_vma=False
    )
```

```python
import functools
import math

import jax
import jax.numpy as jnp
from jax import lax
from jax.experimental import pallas as pl
from jax.experimental.pallas import tpu as pltpu
from jax.sharding import PartitionSpec as P

HEAD = 64
PAIR = 2 * HEAD
EPSILON = 1e-05
MASKED = -1000000000.0
VMEM = 60 * 1024 * 1024
SECTIONS = 2

bf16 = jnp.bfloat16
f32 = jnp.float32


def dot_nn(left, right):
    return lax.dot_general(left, right, (((1,), (0,)), ((), ())), preferred_element_type=f32)


def dot_nt(left, right):
    return lax.dot_general(left, right, (((1,), (1,)), ((), ())), preferred_element_type=f32)


def dot_tn(left, right):
    return lax.dot_general(left, right, (((0,), (0,)), ((), ())), preferred_element_type=f32)


def unit(hidden):
    average = jnp.mean(hidden, axis=-1, keepdims=True)
    centered = hidden - average
    variance = jnp.mean(centered * centered, axis=-1, keepdims=True)
    inverse = lax.rsqrt(variance + EPSILON)
    return centered * inverse, inverse


def unit_back(grad, normed, inverse, gain):
    scaled = grad * gain
    return inverse * (
        scaled
        - jnp.mean(scaled, axis=-1, keepdims=True)
        - normed * jnp.mean(scaled * normed, axis=-1, keepdims=True)
    )


GROUP = 1024


class Copies:
    def __init__(self, semaphores):
        self.semaphores = semaphores
        self.used = 0

    def start(self, source, target):
        copy = pltpu.make_async_copy(source, target, self.semaphores.at[self.used])
        self.used += 1
        copy.start()
        return copy


def wait(copies):
    for copy in copies:
        copy.wait()


def call(kernel, in_specs, out_specs, out_shape, scratch=(), grid=None, flops=0, moved=0, exps=0, vmem=VMEM):
    more = {} if grid is None else {"grid": grid}
    return pl.pallas_call(
        kernel,
        in_specs=in_specs,
        out_specs=out_specs,
        out_shape=out_shape,
        scratch_shapes=list(scratch),
        compiler_params=pltpu.CompilerParams(vmem_limit_bytes=vmem),
        cost_estimate=pl.CostEstimate(flops=flops, bytes_accessed=moved, transcendentals=exps),
        **more,
    )


IN_VMEM = pl.BlockSpec(memory_space=pltpu.VMEM)
IN_HBM = pl.BlockSpec(memory_space=pltpu.HBM)
IN_ANY = pl.BlockSpec(memory_space=pl.ANY)
IN_SMEM = pl.BlockSpec(memory_space=pltpu.SMEM)


def whole(shape):
    return pl.BlockSpec(shape, lambda i: (0,) * len(shape))


def struct(shape, dtype):
    return jax.ShapeDtypeStruct(shape, dtype)


def pack_kernel(p_ref, o_ref, u_ref, d_ref, section_ref, keep_ref, give_ref, stage, semaphores):
    copies = Copies(semaphores)
    place = 0
    sources = [(p_ref[part].T, HEAD) for part in range(3)]
    sources += [(o_ref[...], HEAD), (u_ref[...].T, u_ref.shape[1] // 2), (d_ref[...], d_ref.shape[0] // 2)]
    for value, rows in sources:
        for half in range(2):
            stage[half, place : place + rows] = value[half * rows : (half + 1) * rows]
        place += rows
    section = section_ref[0]
    wait([copies.start(stage.at[1 - section], give_ref), copies.start(stage.at[section], keep_ref)])


def pack(project_w, out_w, up_w, down_w, section):
    width = down_w.shape[1]
    rows = (project_w.shape[2] * 3 + out_w.shape[0] + up_w.shape[1] + down_w.shape[0]) // 2
    return call(
        pack_kernel,
        [IN_VMEM] * 4 + [IN_SMEM],
        [IN_HBM] * 2,
        [struct((rows, width), bf16)] * 2,
        scratch=[pltpu.VMEM((2, rows, width), bf16), pltpu.SemaphoreType.DMA((2,))],
        moved=8 * rows * width,
    )(project_w, out_w, up_w, down_w, section)


def load_heads(copies, ref, first, parts, pairs, target):
    started = []
    for part in range(parts):
        started.append([])
        for pair in range(pairs):
            for half in range(2):
                place = (part * pairs + pair) * PAIR + half * HEAD
                started[-1].append(
                    copies.start(
                        ref.at[half, pair, pl.ds(first + part * HEAD, HEAD)],
                        target.at[pl.ds(place, HEAD)],
                    )
                )
    return started


def load_projection(copies, refs, first, pairs, target, place_ref):
    if len(refs) == 1:
        return load_heads(copies, refs[0], first, 3, pairs, target)
    started = []
    unit_rows = HEAD // 2
    for index, ref in enumerate(refs):
        plane = place_ref[0] if index == 0 else 1 - place_ref[0]
        for half in range(2 if index == 0 else 1):
            here = (half, place_ref[1], 1 - place_ref[1])[index]
            for pair in range(pairs):
                for unit_index in range(3):
                    place = 3 * plane + unit_index
                    row = (place // 2) * pairs * PAIR + (place % 2) * unit_rows
                    row = pl.multiple_of(row + pair * PAIR + here * HEAD, unit_rows)
                    cut = pl.ds((first if index == 0 else 0) + unit_index * unit_rows, unit_rows)
                    started.append(
                        copies.start(
                            ref.at[half, pair, cut] if index == 0 else ref.at[pair, cut],
                            target.at[pl.ds(row, unit_rows)],
                        )
                    )
    return [started, [], []]


class Hidden:
    def __init__(self, copies, refs, pieces, up, down):
        self.copies, self.refs, self.pieces = copies, refs, pieces
        self.targets = (up, down)
        self.groups = up.shape[0] // GROUP
        self.started = 0
        self.loads = ([], [])

    def fetch(self, group):
        end = (group + 1) * GROUP
        place = sum(piece[4] for piece in self.pieces[: self.started])
        while self.started < len(self.pieces) and place < end:
            index, lead, *firsts, rows = self.pieces[self.started]
            for kind in range(2):
                copy = self.copies.start(
                    self.refs[index].at[(*lead, pl.ds(firsts[kind], rows))],
                    self.targets[kind].at[pl.ds(place, rows)],
                )
                self.loads[kind].append((place, copy))
            place += rows
            self.started += 1

    def wait(self, group, kind):
        end = (group + 1) * GROUP
        while self.loads[kind] and self.loads[kind][0][0] < end:
            self.loads[kind].pop(0)[1].wait()


def project_kernel(first, x_ref, b_ref, place_ref, *rest):
    (*w_refs, q_ref, kv_ref, weight, stage, semaphores) = rest
    copies = Copies(semaphores)
    pairs = stage.shape[1]
    wide = pairs * PAIR
    loads = load_projection(copies, w_refs, first, pairs, weight, place_ref)
    stores = []
    for part in (0, 1, 2):
        wait(loads[part])
        out = dot_nt(x_ref[...], weight[part * wide : (part + 1) * wide]) + b_ref[part]
        out = out.astype(bf16)
        if part == 0:
            out = out * bf16(1.0 / math.sqrt(HEAD))
        for pair in range(pairs):
            stage[part, pair] = out[:, pair * PAIR : (pair + 1) * PAIR]
        target = q_ref if part == 0 else kv_ref.at[part - 1]
        stores.append(copies.start(stage.at[part], target))
    wait(stores)


def project(x, table, bias, place):
    count, width = x.shape
    arrays, first = table
    pairs = arrays[0].shape[1]
    return call(
        functools.partial(project_kernel, first),
        [IN_VMEM, IN_VMEM, IN_SMEM] + [IN_HBM] * len(arrays),
        [IN_HBM, IN_HBM],
        [struct((pairs, count, PAIR), bf16), struct((2, pairs, count, PAIR), bf16)],
        scratch=[
            pltpu.VMEM((3 * pairs * PAIR, width), bf16),
            pltpu.VMEM((3, pairs, count, PAIR), bf16),
            pltpu.SemaphoreType.DMA((12 * pairs + 3,)),
        ],
        flops=2 * count * width * 3 * PAIR * pairs,
        moved=2 * (count * width * 4 + 3 * width * PAIR * pairs),
    )(x, bias, place, *arrays)


def feed_forward(copies, places, x_ref, mixed_ref, ow_ref, h_refs, vec_ref, ub_ref,
                 z1_ref, r1_ref, weight_o, weight_u, weight_d, slope, normed, low, acc):
    o_first, pieces = places
    pairs = mixed_ref.shape[0]
    loads_o = load_heads(copies, ow_ref, o_first, 1, pairs, weight_o)[0]
    weights = Hidden(copies, h_refs, pieces, weight_u, weight_d)
    groups = weights.groups
    weights.fetch(groups - 1)
    mixed = jnp.concatenate([mixed_ref[i] for i in range(pairs)], axis=1)
    wait(loads_o)
    attended = dot_nn(mixed, weight_o[...])
    z, r = unit(x_ref[...].astype(f32) + attended + vec_ref[0:1])
    z1_ref[...] = z.astype(bf16)
    r1_ref[...] = r
    out = z * vec_ref[2:3] + vec_ref[4:5]
    normed[...] = out
    low[...] = out.astype(bf16)

    halves = 2
    rows = low.shape[0] // halves

    def before(chunk):
        group, half = divmod(chunk, halves)
        if half == 0:
            weights.fetch(min(group + 1, groups - 1))
            weights.wait(group, 0)
        span = slice(group * GROUP, (group + 1) * GROUP)
        return dot_nt(low[half * rows : (half + 1) * rows], weight_u[span]) + ub_ref[:, span]

    later = before(0)
    for chunk in range(groups * halves):
        group, half = divmod(chunk, halves)
        pre = later
        if chunk + 1 < groups * halves:
            later = before(chunk + 1)
        span = slice(group * GROUP, (group + 1) * GROUP)
        here = slice(half * rows, (half + 1) * rows)
        spread = 0.5 + 0.5 * lax.erf(pre * math.sqrt(0.5))
        bell = jnp.exp(-0.5 * pre * pre) * (1.0 / math.sqrt(2.0 * math.pi))
        slope[here, span] = (spread + pre * bell).astype(bf16)
        if half == 0:
            weights.wait(group, 1)
        out = dot_nn((pre * spread).astype(bf16), weight_d[span])
        if group == 0:
            acc[here] = out
        else:
            acc[here] += out
    return unit(normed[...] + acc[...] + vec_ref[1:2])


def feed_kernel(places, sources, blocks, x_ref, mixed_ref, ow_ref, vec_ref, ub_ref, rank_ref, *rest):
    h_refs = rest[:sources]
    out_refs = rest[sources : sources + max(blocks, 1)]
    (z1_ref, r1_ref, z2_ref, r2_ref, slope_ref, weight_o, weight_u, weight_d,
     z1, z2, slope, normed, low, acc, semaphores) = rest[sources + max(blocks, 1) :]
    copies = Copies(semaphores)
    z, r = feed_forward(
        copies, places, x_ref, mixed_ref, ow_ref, h_refs, vec_ref, ub_ref,
        z1, r1_ref, weight_o, weight_u, weight_d, slope, normed, low, acc,
    )
    stores = [copies.start(z1, z1_ref), copies.start(slope, slope_ref)]
    z2[...] = z.astype(bf16)
    r2_ref[...] = r
    stores.append(copies.start(z2, z2_ref))
    low[...] = (z * vec_ref[3:4] + vec_ref[5:6]).astype(bf16)
    rows = low.shape[0] // max(blocks, 1)
    for j in range(max(blocks, 1)):
        start = pl.multiple_of((rank_ref[0] ^ j) * rows, rows) if blocks else 0
        stores.append(copies.start(low.at[pl.ds(start, rows)], out_refs[j]))
    wait(stores)


def feed_scratch(count, width, wide, hidden, pairs):
    return [
        pltpu.VMEM((wide, width), bf16),
        pltpu.VMEM((hidden, width), bf16),
        pltpu.VMEM((hidden, width), bf16),
        pltpu.VMEM((count, width), bf16),
        pltpu.VMEM((count, width), bf16),
        pltpu.VMEM((count, hidden), bf16),
        pltpu.VMEM((count, width), f32),
        pltpu.VMEM((count, width), bf16),
        pltpu.VMEM((count, width), f32),
        pltpu.SemaphoreType.DMA((16 * pairs + 8,)),
    ]


def feed_sizes(x, mixed, up_bias):
    count, width = x.shape
    pairs = mixed.shape[0]
    return count, width, pairs, pairs * PAIR, up_bias.shape[1]


def feed(x, mixed, tables, vectors, up_bias, rank, blocks):
    o_table, (arrays, pieces) = tables
    count, width, pairs, wide, hidden = feed_sizes(x, mixed, up_bias)
    square = struct((count, width), bf16)
    column = struct((count, 1), f32)
    parts = max(blocks, 1)
    out, kept = [], []
    found = call(
        functools.partial(feed_kernel, (o_table[1], pieces), len(arrays), blocks),
        [IN_VMEM, IN_VMEM, IN_HBM, IN_VMEM, IN_VMEM, IN_SMEM] + [IN_HBM] * len(arrays),
        [IN_HBM] * parts + [IN_HBM, IN_VMEM, IN_HBM, IN_VMEM, IN_HBM],
        [struct((count // parts, width), bf16)] * parts
        + [square, column, square, column, struct((count, hidden), bf16)],
        scratch=feed_scratch(count, width, wide, hidden, pairs),
        flops=2 * count * width * (wide + 2 * hidden),
        moved=2 * (2 * hidden * width + 12 * count * width),
        exps=2 * count * hidden,
    )(x, mixed, o_table[0], vectors, up_bias, rank, *arrays)
    return (found[:blocks] if blocks else found[0], *found[parts:])


def summed(own, got, part):
    columns = []
    for pair in range(own.shape[1]):
        column = own[part, pair].astype(f32)
        for i in range(got.shape[0]):
            column += got[i, part, pair].astype(f32)
        columns.append(column.astype(bf16))
    return jnp.concatenate(columns, axis=1)


def leave_kernel(p_first, extra, first_ref, dq_ref, own_ref, got_ref, pw_ref, rank_ref, *rest):
    if extra:
        prefix_ref, *rest = rest
    (*out_refs, weight_p, low, first, dq, own, got, semaphores) = rest
    copies = Copies(semaphores)
    pairs = dq.shape[0]
    wide = pairs * PAIR
    load_q = copies.start(dq_ref, dq)
    loads = load_heads(copies, pw_ref, p_first, 3, pairs, weight_p)
    others = [copies.start(own_ref, own), copies.start(got_ref, got)]
    load_first = copies.start(first_ref, first)
    load_q.wait()
    wait(loads[0])
    total = dot_nn(jnp.concatenate([dq[pair] for pair in range(pairs)], axis=1), weight_p[:wide])
    wait(others)
    for part in (1, 2):
        wait(loads[part])
        total += dot_nn(summed(own, got, part - 1), weight_p[part * wide : (part + 1) * wide])
    load_first.wait()
    low[...] = (total + first[...].astype(f32)).astype(bf16)
    rows = low.shape[0] // len(out_refs)
    for j, target in enumerate(out_refs):
        start = pl.multiple_of((rank_ref[0] ^ j) * rows, rows)
        target[:rows] = low[pl.ds(start, rows)]
        if extra:
            value = prefix_ref[rank_ref[0] ^ j].astype(bf16)
            for column in range(value.shape[0] // 16):
                span = slice(column * PAIR, (column + 1) * PAIR)
                target[rows:, span] = value[column * 16 : (column + 1) * 16]


def leave(first, dq, own, got, p_table, rank, blocks, prefix=None):
    count, width = first.shape
    pairs = dq.shape[0]
    more = [] if prefix is None else [prefix]
    return call(
        functools.partial(leave_kernel, p_table[1], len(more)),
        [IN_ANY] * 4 + [IN_HBM, IN_SMEM] + [IN_VMEM] * len(more),
        [IN_VMEM] * blocks,
        [struct((count // blocks + 16 * len(more), width), bf16)] * blocks,
        scratch=[
            pltpu.VMEM((3 * pairs * PAIR, width), bf16),
            pltpu.VMEM((count, width), bf16),
            pltpu.VMEM((count, width), bf16),
            pltpu.VMEM(dq.shape, bf16),
            pltpu.VMEM(own.shape, bf16),
            pltpu.VMEM(got.shape, bf16),
            pltpu.SemaphoreType.DMA((6 * pairs + 4,)),
        ],
        flops=2 * count * width * 3 * PAIR * pairs,
        moved=2 * (count * width * 7 + 3 * width * PAIR * pairs),
        vmem=28 * 1024 * 1024,
    )(first, dq, own, got, p_table[0][0], rank, *more)


def attend_kernel(
    prefix_count, q_ref, own_ref, other_ref, pk_ref, pv_ref, sq_ref, sk_ref,
    mixed_ref, raised_ref, inverse_ref, bias_ref,
):
    pad = pk_ref.shape[1]
    others = other_ref.shape[0]

    @pl.when(pl.program_id(0) == 0)
    def _():
        row = lax.broadcasted_iota(jnp.int32, (pad, bias_ref.shape[1]), 0)
        bias_ref[:pad] = jnp.where(row < prefix_count, 0.0, MASKED)
        keys = jnp.broadcast_to(sk_ref[...], (8, sk_ref.shape[1])).T[:, :1]
        same = (keys == sq_ref[...]) & (keys >= 0)
        bias_ref[pad:] = jnp.where(same, 0.0, MASKED)

    keys = jnp.concatenate(
        [pk_ref[0], own_ref[0, 0]] + [other_ref[i, 0, 0] for i in range(others)], axis=0
    )
    values = jnp.concatenate(
        [pv_ref[0], own_ref[1, 0]] + [other_ref[i, 1, 0] for i in range(others)], axis=0
    )
    queries = q_ref[0]
    lane = lax.broadcasted_iota(jnp.int32, queries.shape, 1)
    value_lane = lax.broadcasted_iota(jnp.int32, values.shape, 1)
    parts = []
    inverses = []
    count = queries.shape[0]
    score = lambda head: dot_nt(
        keys, jnp.where((lane // HEAD) == head, queries, bf16(0))
    ) + bias_ref[...]
    ahead = score(0)
    for head in range(2):
        scores = ahead
        if head == 0:
            ahead = score(1)
        raised = jnp.exp(scores - jnp.max(scores, axis=0, keepdims=True))
        low = raised.astype(bf16)
        raised_ref[0, head] = low
        ones = jnp.where((value_lane // HEAD) == head, values, bf16(1))
        out = dot_tn(ones, low)
        inverse = 1.0 / out[(1 - head) * HEAD : (1 - head) * HEAD + 1]
        out = out[head * HEAD : (head + 1) * HEAD]
        parts.append(out * inverse)
        inverses.append(jnp.broadcast_to(inverse, out.shape))
    mixed_ref[0] = jnp.concatenate(parts, axis=0).T.astype(bf16)
    inverse_ref[0] = jnp.concatenate(inverses, axis=0).T.astype(bf16)


def attend(q, own, other, pk, pv, prefix_count, seg_q, seg_k):
    pairs, count, _ = q.shape
    others = other.shape[0]
    pad = pk.shape[1]
    total = pad + count * (others + 1)
    by_pair = pl.BlockSpec((1, count, PAIR), lambda i: (i, 0, 0))
    by_prefix = pl.BlockSpec((1, pad, PAIR), lambda i: (i, 0, 0))
    return call(
        functools.partial(attend_kernel, prefix_count),
        [
            by_pair,
            pl.BlockSpec((2, 1, count, PAIR), lambda i: (0, i, 0, 0)),
            pl.BlockSpec((others, 2, 1, count, PAIR), lambda i: (0, 0, i, 0, 0)),
            by_prefix,
            by_prefix,
            whole((1, count)),
            whole((1, total - pad)),
        ],
        [
            by_pair,
            pl.BlockSpec((1, 2, total, count), lambda i: (i, 0, 0, 0)),
            by_pair,
        ],
        [
            struct((pairs, count, PAIR), bf16),
            struct((pairs, 2, total, count), bf16),
            struct((pairs, count, PAIR), bf16),
        ],
        scratch=[pltpu.VMEM((total, count), f32)],
        grid=(pairs,),
        flops=8 * total * count * PAIR * pairs,
        moved=4 * pairs * total * count,
        exps=2 * pairs * total * count,
    )(q, own, other, pk, pv, seg_q, seg_k)


def attention_back(d_out, mixed, inverse, raised, queries, keys, values):
    lane = lax.broadcasted_iota(jnp.int32, queries.shape, 1)
    scaled = d_out.astype(f32) * inverse.astype(f32)
    products = (scaled * mixed.astype(f32)).T
    scaled = scaled.astype(bf16)
    d_keys = jnp.zeros(keys.shape, f32)
    d_values = jnp.zeros(keys.shape, f32)
    parts = []
    for head in range(2):
        chosen = (lane // HEAD) == head
        span = slice(head * HEAD, (head + 1) * HEAD)
        delta = jnp.sum(products[span], axis=0, keepdims=True)
        here = jnp.where(chosen, scaled, bf16(0))
        low = raised(head)
        d_score = (low.astype(f32) * (dot_nt(values, here) - delta)).astype(bf16)
        d_values += dot_nn(low, here)
        d_keys += dot_nn(d_score, jnp.where(chosen, queries, bf16(0)))
        parts.append(dot_tn(keys, d_score)[span])
    return jnp.concatenate(parts, axis=0).T * (1.0 / math.sqrt(HEAD)), d_keys, d_values


def back_kernel(p_first, p_sources, o_first, pieces, sources, place_ref, *rest):
    if p_first is None:
        grad_ref, *rest = rest
    else:
        first1_ref, dq_in, own_in, got_in, *rest = rest
        pw_refs, rest = rest[:p_sources], rest[p_sources:]
    (ow_ref, vec_ref, z1_ref, r1_ref, z2_ref, r2_ref, slope_ref,
     mixed_ref, inverse_ref, raised_ref, q_ref, own_ref, other_ref, pk_ref, pv_ref, *rest) = rest
    h_refs, rest = rest[:sources], rest[sources:]
    outs, rest = rest[:5], rest[5:]
    (weight_o, weight_u, weight_d, unit_in, slope, low, acc, first, dq, down, dother, prefix,
     mixed, inverse, raised, queries, own, other, semaphores, turns, stores, *weight_p) = rest
    copies = Copies(semaphores)
    pairs, count, _ = dq.shape
    others = dother.shape[0]
    pad = pk_ref.shape[1]
    weights = Hidden(copies, h_refs, pieces, weight_u, weight_d)
    groups = weights.groups
    slopes = []

    def fetch(group):
        weights.fetch(group)
        span = (slice(None), pl.ds(group * GROUP, GROUP))
        slopes.append(copies.start(slope_ref.at[span], slope.at[span]))

    if p_first is None:
        load = copies.start(grad_ref, low)
        load_z2 = copies.start(z2_ref, unit_in)
        fetch(0)
        load.wait()
        grad = low[...].astype(f32)
    else:
        load_q = copies.start(dq_in, dq)
        loads_p = load_projection(copies, pw_refs, p_first, pairs, weight_p[0], place_ref)
        loads = [copies.start(own_in, down), copies.start(got_in, dother)]
        load_first = copies.start(first1_ref, first)
        load_z2 = copies.start(z2_ref, unit_in)
        fetch(0)
        wide = pairs * PAIR
        load_q.wait()
        wait(loads_p[0])
        left = jnp.concatenate([dq[pair] for pair in range(pairs)], axis=1)
        total = dot_nn(left, weight_p[0][:wide])
        wait(loads)
        for part in (1, 2):
            wait(loads_p[part])
            total += dot_nn(
                summed(down, dother, part - 1), weight_p[0][part * wide : (part + 1) * wide]
            )
        load_first.wait()
        grad = (total + first[...].astype(f32)).astype(bf16).astype(f32)
    load_z2.wait()
    acc[...] = unit_back(grad, unit_in[...].astype(f32), r2_ref[...], vec_ref[3:4])
    low[...] = acc[...].astype(bf16)
    load_z1 = copies.start(z1_ref, unit_in)
    loads_o = load_heads(copies, ow_ref, o_first, 1, pairs, weight_o)[0]

    def turn(pair, slot):
        moves = (
            (raised_ref.at[pair], raised.at[slot]),
            (q_ref.at[pair], queries.at[slot]),
            (mixed_ref.at[pair], mixed.at[slot]),
            (inverse_ref.at[pair], inverse.at[slot]),
            (own_ref.at[:, pair], own.at[slot]),
            (other_ref.at[:, :, pair], other.at[slot]),
        )
        return [
            pltpu.make_async_copy(source, target, turns.at[slot, i])
            for i, (source, target) in enumerate(moves)
        ]

    for group in range(groups):
        if group + 1 < groups:
            fetch(group + 1)
        if group == groups - 1:
            for pair in range(2):
                for copy in turn(pair, pair):
                    copy.start()
        slopes[group].wait()
        weights.wait(group, 0)
        weights.wait(group, 1)
        span = slice(group * GROUP, (group + 1) * GROUP)
        d_act = dot_nt(low[...], weight_d[span])
        d_pre = (d_act * slope[:, span].astype(f32)).astype(bf16)
        acc[...] += dot_nn(d_pre, weight_u[span])
    load_z1.wait()
    d_first = unit_back(acc[...], unit_in[...].astype(f32), r1_ref[...], vec_ref[2:3])
    first[...] = d_first.astype(bf16)
    store_first = copies.start(first, outs[0])
    wait(loads_o)
    low[...] = dot_nt(d_first.astype(bf16), weight_o[...]).astype(bf16)

    def save(pair):
        moves = (
            (dq.at[pair], outs[1].at[pair]),
            (down.at[:, pair], outs[2].at[:, pair]),
            (dother.at[:, :, pair], outs[3].at[:, :, pair]),
            (prefix.at[pair], outs[4].at[pair]),
        )
        return [
            pltpu.make_async_copy(source, target, stores.at[pair, i])
            for i, (source, target) in enumerate(moves)
        ]

    def step(pair, carry):
        slot = lax.rem(pair, 2)
        for copy in turn(pair, slot):
            copy.wait()
        keys = jnp.concatenate(
            [pk_ref[pair], own[slot, 0]] + [other[slot, i, 0] for i in range(others)], axis=0
        )
        values = jnp.concatenate(
            [pv_ref[pair], own[slot, 1]] + [other[slot, i, 1] for i in range(others)], axis=0
        )
        d_query, d_keys, d_values = attention_back(
            low[:, pl.ds(pl.multiple_of(pair * PAIR, PAIR), PAIR)],
            mixed[slot],
            inverse[slot],
            lambda head: raised[slot, head],
            queries[slot],
            keys,
            values,
        )
        dq[pair] = d_query.astype(bf16)
        prefix[pair, :pad] = d_keys[:pad]
        prefix[pair, pad:] = d_values[:pad]
        for part, d_part in enumerate((d_keys, d_values)):
            down[part, pair] = d_part[pad : pad + count].astype(bf16)
            for i in range(others):
                start = pad + (i + 1) * count
                dother[i, part, pair] = d_part[start : start + count].astype(bf16)
        for copy in save(pair):
            copy.start()

        @pl.when(pair + 2 < pairs)
        def _():
            for copy in turn(pair + 2, slot):
                copy.start()

        return carry

    lax.fori_loop(0, pairs, step, 0)
    store_first.wait()
    for pair in range(pairs):
        for copy in save(pair):
            copy.wait()


def backward(grads, p_table, tables, vectors, kept, attention, place):
    o_table, (arrays, pieces) = tables
    mixed, inverse, raised, q, own, other, pk, pv = attention
    pairs, count, _ = q.shape
    width = o_table[0].shape[-1]
    wide = pairs * PAIR
    total = raised.shape[2]
    pad = pk.shape[1]
    slope = kept[-1]
    hidden = slope.shape[1]
    more, p_first = ([], None) if p_table is None else p_table
    vm = pltpu.VMEM
    return call(
        functools.partial(
            back_kernel, p_first, len(more), o_table[1], pieces, len(arrays)
        ),
        [IN_SMEM] + [IN_HBM] * (len(grads) + len(more))
        + [IN_HBM, IN_VMEM, IN_HBM, IN_VMEM, IN_HBM, IN_VMEM, IN_HBM]
        + [IN_HBM] * 6 + [IN_VMEM] * 2
        + [IN_HBM] * len(arrays),
        [IN_HBM] * 5,
        [
            struct((count, width), bf16),
            struct(q.shape, bf16),
            struct(own.shape, bf16),
            struct(other.shape, bf16),
            struct((pairs, 2 * pad, PAIR), f32),
        ],
        scratch=[
            vm((wide, width), bf16),
            vm((hidden, width), bf16),
            vm((hidden, width), bf16),
            vm((count, width), bf16),
            vm((count, hidden), bf16),
            vm((count, width), bf16),
            vm((count, width), f32),
            vm((count, width), bf16),
            vm(q.shape, bf16),
            vm(own.shape, bf16),
            vm(other.shape, bf16),
            vm((pairs, 2 * pad, PAIR), f32),
            vm((2, count, PAIR), bf16),
            vm((2, count, PAIR), bf16),
            vm((2, 2, total, count), bf16),
            vm((2, count, PAIR), bf16),
            vm((2, 2, count, PAIR), bf16),
            vm((2, other.shape[0], 2, count, PAIR), bf16),
            pltpu.SemaphoreType.DMA((22 * pairs + 16,)),
            pltpu.SemaphoreType.DMA((2, 6)),
            pltpu.SemaphoreType.DMA((pairs, 4)),
        ]
        + [vm((3 * wide, width), bf16)] * (p_table is not None),
        flops=2 * count * width * (4 * wide + 2 * hidden) + 16 * total * count * PAIR * pairs,
        moved=2 * (2 * hidden * width + 4 * wide * width + 16 * count * width) + 4 * pairs * total * count,
    )(place, *grads, *more, o_table[0], vectors, *kept, *attention, *arrays)


def per_device(
    boundary, segment_ids, project_weight, project_bias, output_weight, output_biases,
    norm_gains, norm_shifts, up_weight, up_bias, down_weight, prefix_keys, prefix_values,
):
    section = lax.axis_index("section")
    rank = lax.axis_index("tensor")
    ranks = lax.axis_size("tensor")
    is_first = section == 0
    micro, slots, rows, width = boundary.shape[1:]
    length = slots * ranks
    row_count = micro * rows
    chips = ranks // row_count
    blocks = SECTIONS * chips
    count = length // blocks
    place = rank % chips
    swap = [(0, 1), (1, 0)]
    after = lambda value, *first: lax.optimization_barrier((value, *first))[0]
    heads_all = project_weight.shape[3] * ranks
    pairs = heads_all // PAIR
    shards = ranks // pairs
    prefix_count = prefix_keys.shape[1]
    pad = -(-prefix_count // 32) * 32
    low_width = project_weight.shape[3] // 2
    hidden = up_weight.shape[2] // 2

    quick = chips == 1 and ranks == 8 and lax.axis_size("dp") == 2

    half_ranks = ranks // 2
    low_rank = rank % half_ranks
    block = section * chips + place
    by_row = jnp.transpose(boundary[0], (0, 2, 1, 3)).reshape(row_count, slots, width)

    def ordered(parts):
        bit = 1
        while bit < len(parts):
            flip = (rank & bit) != 0
            parts = [jnp.where(flip, parts[i ^ bit], part) for i, part in enumerate(parts)]
            bit *= 2
        return parts

    if quick:
        lower, upper = by_row[:half_ranks], by_row[half_ranks:]
        keep = jnp.where(is_first, lower, upper)
        got = lax.ppermute(jnp.where(is_first, upper, lower), "section", swap)

        def arrive(rows_here):
            parts = []
            for j in range(half_ranks):
                route = [
                    (s * ranks + t, (t // half_ranks) * ranks + half_ranks * s + ((t % half_ranks) ^ j))
                    for s in range(SECTIONS)
                    for t in range(ranks)
                ]
                part = lax.dynamic_index_in_dim(rows_here, low_rank ^ j, 0, keepdims=False)
                parts.append(lax.ppermute(part, ("section", "tensor"), route))
            return parts

        tokens = jnp.concatenate(ordered(arrive(jnp.where(is_first, keep, got))), axis=0)
        cotangent_rows = jnp.where(is_first, got, keep)
    else:
        if chips > 1:
            by_row = jnp.repeat(by_row, chips, axis=0)
        row = lax.all_to_all(by_row, "tensor", 0, 0, tiled=True).reshape(length, width)
        other_block = (1 - section) * chips + place
        mine = lax.dynamic_slice_in_dim(row, block * count, count, 0)
        theirs = lax.dynamic_slice_in_dim(row, other_block * count, count, 0)
        got = lax.ppermute(theirs, "section", swap)
        tokens = jnp.where(is_first, mine, got)
        cotangent = jnp.where(is_first, got, mine)

    own_vectors = jnp.concatenate(
        [output_biases[0], norm_gains[0], norm_shifts[0], norm_shifts[0]], axis=0
    )
    got_vectors = lax.ppermute(own_vectors, "section", swap)
    vectors = [
        jnp.where(is_first, own_vectors, got_vectors).astype(f32),
        jnp.where(is_first, got_vectors, own_vectors).astype(f32),
    ]

    segments = lax.dynamic_index_in_dim(
        segment_ids.reshape(row_count, length), rank // chips, 0, keepdims=False
    )
    seg_q = lax.dynamic_slice_in_dim(segments, block * count, count, 0)
    seg_k = jnp.concatenate(
        [
            lax.dynamic_slice_in_dim(segments, (block ^ distance) * count, count, 0)
            for distance in range(blocks)
        ]
    )[None, :]
    seg_q = seg_q[None, :]

    project_rows = jnp.transpose(project_weight[0], (1, 2, 0)).reshape(3, 2, low_width, width)
    project_rows = jnp.transpose(project_rows, (1, 0, 2, 3)).reshape(2, 3 * low_width, width)
    out_rows = output_weight[0].reshape(2, low_width, width)
    up_rows = jnp.transpose(up_weight[0], (1, 0)).reshape(2, hidden, width)
    down_rows = down_weight[0].reshape(2, hidden, width)
    if quick:
        keep, give = pack(
            jnp.transpose(project_weight[0], (1, 0, 2)), output_weight[0], up_weight[0],
            down_weight[0], section.astype(jnp.int32).reshape(1),
        )
        give, project_bias, up_bias, prefix_keys, prefix_values = lax.optimization_barrier(
            (give, project_bias, up_bias, prefix_keys, prefix_values)
        )
    else:
        packed = jnp.concatenate([project_rows, out_rows, up_rows, down_rows], axis=1)
        keep = lax.dynamic_index_in_dim(packed, section, 0, keepdims=False)
        give = lax.dynamic_index_in_dim(packed, 1 - section, 0, keepdims=False)
    got = lax.ppermute(give, "section", swap)
    small = jnp.concatenate(
        [
            jnp.transpose(project_bias[0].reshape(3, 2, low_width), (1, 0, 2)).reshape(2, -1),
            up_bias[0].reshape(2, hidden),
            jnp.transpose(prefix_keys[0].reshape(-1, 2, low_width), (1, 0, 2)).reshape(2, -1),
            jnp.transpose(prefix_values[0].reshape(-1, 2, low_width), (1, 0, 2)).reshape(2, -1),
        ],
        axis=1,
    )
    small_size = small.shape[1]
    small_rows = -(-small_size // (16 * width)) * 16
    small = jnp.pad(small, ((0, 0), (0, small_rows * width - small_size)))
    small = small.reshape(2, small_rows, width)
    keep_small = jnp.where(is_first, small[0], small[1])
    got_small = lax.ppermute(jnp.where(is_first, small[1], small[0]), "section", swap)
    small_first = jnp.where(is_first, keep_small, got_small)
    small_second = jnp.where(is_first, got_small, keep_small)
    rows_first = lambda cut: jnp.where(is_first, keep[cut], got[cut])
    rows_second = lambda cut: jnp.where(is_first, got[cut], keep[cut])
    sizes = [3 * low_width, low_width, hidden, hidden, small_rows]
    p_end, o_end, u_end, d_end, s_end = [sum(sizes[: i + 1]) for i in range(len(sizes))]
    plane = lax.axis_index("dp")
    gather = lambda parts: lax.all_gather(
        jnp.concatenate(parts, axis=0), ("section", "tensor"), axis=0
    ).reshape(2, ranks, -1, width)

    def unpack(flat):
        cut = 0
        found = []
        for groups, size in ((3, low_width), (1, hidden), (prefix_count, low_width), (prefix_count, low_width)):
            part = flat[:, :, cut : cut + groups * size].reshape(2, pairs, shards, groups, size)
            cut += groups * size
            if shards == 1:
                part = part[:, :, 0]
            else:
                part = jnp.transpose(part, (2, 1, 3, 0, 4)).reshape(2, pairs, groups, 2 * size)
            found.append(part)
        p_bias = jnp.transpose(found[0], (2, 1, 0, 3)).reshape(3, 1, heads_all).astype(f32)
        prefix = [
            jnp.pad(
                jnp.transpose(part, (1, 2, 0, 3)).reshape(pairs, prefix_count, PAIR),
                ((0, 0), (0, pad - prefix_count), (0, 0)),
            )
            for part in found[2:]
        ]
        return p_bias, found[1][:, :, 0], prefix[0], prefix[1]

    tables = []
    smalls = []
    plane = lax.axis_index("dp")
    share = 3 * low_width // 2
    projection = rows_second(slice(0, p_end))
    if quick:
        projection = jnp.where(plane == 0, projection[:share], projection[share:])
    early_rows = [rows_first(slice(0, d_end)), projection, small_first, small_second]
    projection_rows = projection.shape[0]
    late_rows = rows_second(slice(p_end, d_end))
    early = gather(early_rows)
    early, vectors[0], vectors[1], seg_q, seg_k, tokens = lax.optimization_barrier(
        (early, vectors[0], vectors[1], seg_q, seg_k, tokens)
    )
    late = gather([after(late_rows, early)])
    def table(array, first, size, groups=1):
        if shards == 1:
            return (array, first, size)
        part = array[:, :, first : first + size].reshape(
            2, pairs, shards, groups, size // groups, width
        )
        part = jnp.transpose(part, (2, 1, 3, 0, 4, 5))
        return (part.reshape(2, pairs, 2 * size, width), 0, 2 * size)

    def projection_table(layer):
        if quick and layer:
            return None
        array, first, _ = table(early, layer * d_end, 3 * low_width, 3)
        return (array,), first

    for layer in range(2):
        source, shift = (late, -p_end) if layer else (early, 0)
        up, u_first, rows_here = table(source, shift + o_end, 2 * hidden, 2)
        rows_here //= 2
        pieces = tuple(
            (0, (s, t), u_first, u_first + rows_here, rows_here)
            for s in range(2)
            for t in range(pairs)
        )
        tables.append(
            (
                projection_table(layer),
                table(source, shift + p_end, low_width),
                ((up,), pieces),
            )
        )
        start = d_end + projection_rows + layer * small_rows
        p_bias, u_bias, pk, pv = unpack(
            early[:, :, start : start + small_rows].reshape(2, ranks, -1)
        )
        smalls.append((p_bias, u_bias.reshape(1, -1).astype(f32), pk, pv))

    def flips():
        routes = []
        for distance in range(1, blocks):
            route = []
            for s in range(SECTIONS):
                for t in range(ranks):
                    index = (s * chips + t % chips) ^ distance
                    route.append(
                        (s * ranks + t, (index // chips) * ranks + t // chips * chips + index % chips)
                    )
            routes.append(route)
        return routes

    routes = flips()

    def exchange(parts):
        return jnp.stack(
            [
                lax.ppermute(part, ("section", "tensor"), route) if chips > 1
                else lax.ppermute(part, "section", swap)
                for part, route in zip(parts, routes)
            ]
        )

    out_blocks = half_ranks if quick else 1
    order = (low_rank if quick else 0 * rank).astype(jnp.int32).reshape(1)
    place_here = jnp.stack([plane, section]).astype(jnp.int32)
    p_tables = []
    saved = []
    x = tokens
    for layer in range(2):
        p_table, *others = tables[layer]
        p_bias, u_bias, pk, pv = smalls[layer]
        if quick and layer == 0:
            cross = lax.dynamic_slice(
                early, (section, 0, d_end, 0), (1, pairs, share, width)
            ).reshape(pairs, share, width)
            theirs = lax.ppermute(cross, "dp", swap)
        if quick and layer == 1:
            p_table = ((early, theirs, theirs_too), d_end)
        p_tables.append(p_table)
        q, own = project(x, p_table, p_bias, place_here)
        other = exchange([own] * (blocks - 1))
        mixed, raised, inverse = attend(q, own, other, pk, pv, prefix_count, seg_q, seg_k)
        saved.append((mixed, inverse, raised, q, own, other, pk, pv))
        if layer == 1 and quick:
            cotangent = arrive(after(cotangent_rows, mixed))
        x, *kept = feed(
            x, mixed, others, vectors[layer], u_bias, order, out_blocks if layer else 0
        )
        saved[-1] += (kept,)
        if layer == 0 and quick:
            theirs, x = lax.optimization_barrier((theirs, x))
            theirs_too = lax.ppermute(theirs, "section", swap)
    outs = x
    if quick:
        cotangent, outs = lax.optimization_barrier((cotangent, outs))
        cotangent = jnp.concatenate(ordered(cotangent), axis=0)
    kept_0, kept_1 = (entry[-1] for entry in saved)
    saved = [entry[:-1] for entry in saved]
    first, dq, down, dother, prefix_1 = backward(
        (cotangent,), None, tables[1][1:], vectors[1], kept_1, saved[1], place_here
    )

    def send_blocks(parts):
        got = []
        for j, part in enumerate(parts):
            route = [
                (s * ranks + t, (t // half_ranks) * ranks + half_ranks * s + ((t % half_ranks) ^ j))
                for s in range(SECTIONS)
                for t in range(ranks)
            ]
            got.append(lax.ppermute(part, ("section", "tensor"), route))
        return got

    if quick:
        dother, *outs = lax.optimization_barrier((dother, *outs))
        outs = send_blocks(outs)
    got = exchange([dother[i] for i in range(blocks - 1)])
    first, dq, down, dother, prefix_0 = backward(
        (first, dq, down, got), p_tables[1], tables[0][1:], vectors[0], kept_0, saved[0], place_here
    )
    if quick:
        dother, *outs = lax.optimization_barrier((dother, *outs))
    got = exchange([dother[i] for i in range(blocks - 1)])
    if quick:
        prefix = jnp.stack([prefix_0, prefix_1], axis=1)
        lower, upper = prefix[: pairs // 2], prefix[pairs // 2 :]
        other = lax.ppermute(jnp.where(is_first, upper, lower), "section", swap)
        prefix = jnp.where(is_first, lower, upper) + other
        prefix = prefix.reshape(half_ranks, 4 * pad, PAIR)
    else:
        prefix = None
    grads = leave(first, dq, down, got, tables[0][0], order, out_blocks, prefix)

    if quick:
        grads = send_blocks(grads)
        partial = sum(part[slots:].astype(f32) for part in grads)
        grads = jnp.stack(ordered([part[:slots] for part in grads]))
        outs = jnp.stack(ordered(outs))
        keep = jnp.where(is_first, grads, outs)
        got = lax.ppermute(jnp.where(is_first, outs, grads), "section", swap)
        partial += lax.ppermute(partial, "dp", swap)
        partial = jnp.transpose(partial.reshape(16, -1, PAIR), (1, 0, 2)).reshape(2, 2 * pad, PAIR)
        prefix = jnp.where(is_first, partial[0], partial[1]) + lax.ppermute(
            jnp.where(is_first, partial[1], partial[0]), "section", swap
        )
        back = jnp.concatenate(
            [jnp.where(is_first, keep, got), jnp.where(is_first, got, keep)], axis=0
        )
    else:
        keep = jnp.where(is_first, grads[0], outs[0])
        got = lax.ppermute(jnp.where(is_first, outs[0], grads[0]), "section", swap)
        row = jnp.zeros((length, width), bf16)
        row = lax.dynamic_update_slice_in_dim(
            row, jnp.where(is_first, keep, got), place * count, 0
        )
        row = lax.dynamic_update_slice_in_dim(
            row, jnp.where(is_first, got, keep), (chips + place) * count, 0
        )
        back = lax.all_to_all(row.reshape(ranks, slots, width), "tensor", 0, 0, tiled=True)
        back = jnp.sum(back.reshape(row_count, chips, slots, width), axis=1)
    result = jnp.transpose(back.reshape(micro, rows, slots, width), (0, 2, 1, 3))[None]

    if quick:
        both = prefix.reshape(2, pad, PAIR)[:, :prefix_count]
    else:
        both = jnp.where(
            is_first,
            lax.psum(prefix_0, ("section", "dp", "tensor")),
            lax.psum(prefix_1, ("section", "dp", "tensor")),
        )
        both = both.reshape(pairs, 2, pad, PAIR)[:, :, :prefix_count]
        both = jnp.transpose(both, (1, 2, 0, 3)).reshape(2, prefix_count, heads_all)
        share = heads_all // ranks
        both = lax.dynamic_slice_in_dim(both, rank * share, share, 2)
    return (result, both[0][None], both[1][None])


def solution(mesh):
    in_specs = (
        P("section", None, "tensor", "dp", None),
        P(None, "dp", None),
        P("section", None, None, "tensor"),
        P("section", None, "tensor"),
        P("section", "tensor", None),
        P("section", None, None),
        P("section", None, None),
        P("section", None, None),
        P("section", None, "tensor"),
        P("section", "tensor"),
        P("section", "tensor", None),
        P("section", None, "tensor"),
        P("section", None, "tensor"),
    )
    out_specs = (
        P("section", None, "tensor", "dp", None),
        P("section", None, "tensor"),
        P("section", None, "tensor"),
    )
    return jax.shard_map(
        per_device, mesh=mesh, in_specs=in_specs, out_specs=out_specs, check_vma=False
    )
```
